32 devices in a mesh: dp: 8 (over z, x), mp: 4 (over y, core).
Axes of the slice: x: 2, y: 2, z: 4, core: 2. Of those that a mesh axis runs over, the one named last changes fastest.
Arguments:
- tokens: bfloat16 [16384, 768], P('dp'), may hold values from -6 to 6
- cotangent: bfloat16 [16384, 768], P('dp'), may hold values from -6 to 6
- lengths: int32 [16], P('dp'), may hold values from 128 to 1024, as said below
- tile_order: int32 [192], replicated, may hold values from 0 to 191, as said below
- master: float32 [4, 192, 96, 96], P('mp', 'dp')
- first_moment: float32 [4, 192, 96, 96], P('mp', 'dp')
- second_moment: float32 [4, 192, 96, 96], P('mp', 'dp')
- basis_left: float32 [4, 192, 96, 96], P('mp', 'dp'), may hold values from -0.625 to 0.625
- basis_right: float32 [4, 192, 96, 96], P('mp', 'dp'), may hold values from -0.625 to 0.625
- local_vec: float32 [4, 1152], P('mp'), may hold values from -1.2 to 1.2
- local_first: float32 [4, 1152], P('mp')
- local_second: float32 [4, 1152], P('mp')
- shared_vec: float32 [6, 768], replicated
- shared_first: float32 [6, 768], replicated
- shared_second: float32 [6, 768], replicated
Outputs:
- output: bfloat16 [16384, 768], P(('dp', 'mp'))
- input_grad: float32 [16384, 768], P(('dp', 'mp'))
- tile_grad: float32 [4, 192, 96, 96], P('mp', 'dp')
- tile_first: float32 [4, 192, 96, 96], P('mp', 'dp')
- tile_second: float32 [4, 192, 96, 96], P('mp', 'dp')
- tile_weight: float32 [4, 192, 96, 96], P('mp', 'dp')
- local_grad: float32 [4, 1152], P('mp')
- local_first_new: float32 [4, 1152], P('mp')
- local_second_new: float32 [4, 1152], P('mp')
- local_new: float32 [4, 1152], P('mp')
- shared_grad: float32 [6, 768], replicated
- shared_first_new: float32 [6, 768], replicated
- shared_second_new: float32 [6, 768], replicated
- shared_new: float32 [6, 768], replicated
The draws below stay inside these ranges and needn't reach their ends.
Inputs may be any that keep to these rules, and one draw needn't show every extreme that they name: `lengths`: the first len slots of each sequence hold its tokens, the rest padding; some sequence has 1024 tokens and some has 128. `tile_order`: a permutation of the 192 tiles; owner i along dp holds slots i * 24 to (i + 1) * 24 - 1.
All inputs are finite; a program needn't handle non-finite values.
Results may differ from the reference program's by a relative error of at most 0.019.
Values may be sent and summed in bfloat16 or wider, within the bound.
A program may use at most 192 MiB of HBM per device.

```python
import math
import jax
import jax.numpy as jnp
from jax import lax

D = 768
HD = 64
FF = 3072
L = 1024
GRAIN = 64
B = 96
STEP = 5
SEQ_DEV = 2
DM = 192
HM = 3
FM = 768
LV = 1152
NT = 192
SEQS = 16
TOKENS = 16384
N_DP = 8
N_MP = 4


def slot_order(key):
    return jax.random.permutation(jax.random.fold_in(key, 97), NT).astype(jnp.int32)


def tile_scales(order, factors):
    cut_one = D // B * (3 * DM // B)
    cut_two = cut_one + DM // B * (D // B)
    cut_three = cut_two + D // B * (FM // B)
    return jnp.where(order < cut_one, factors[0], jnp.where(order < cut_two, factors[1], jnp.where(order < cut_three, factors[2], factors[3])))


def grad_root():
    return math.sqrt(SEQ_DEV * N_DP * (L + 2 * GRAIN) / 2.0)


def second_draw(key, shape, scale):
    keys = jax.random.split(key, 2)
    factor = jax.random.uniform(keys[0], shape, jnp.float32, 1.0, 4.0)
    spread = jnp.exp(jax.random.uniform(keys[1], shape, jnp.float32, math.log(0.5), math.log(2.0)))
    return scale * scale * factor * spread


def draw_lengths(key, part):
    key = jax.random.fold_in(key, 1)
    keys = jax.random.split(key, 3)
    values = jax.random.randint(keys[0], (SEQS,), 2 * GRAIN, L + 1, jnp.int32)
    top_at = jax.random.randint(keys[1], (), 0, SEQS, jnp.int32)
    least_at = (top_at + 1 + jax.random.randint(keys[2], (), 0, SEQS - 1, jnp.int32)) % SEQS
    return values.at[top_at].set(L).at[least_at].set(2 * GRAIN)


def draw_tile_order(key, part):
    return slot_order(key)


def draw_master(key, part):
    order = slot_order(key)
    key = jax.random.fold_in(key, 2)
    scale = tile_scales(order, [D ** (-0.5), (D // 32) ** (-0.5), D ** (-0.5), FF ** (-0.5)])
    return jax.random.normal(key, (N_MP, NT, B, B), jnp.float32) * scale[None, :, None, None]


def draw_first_moment(key, part):
    order = slot_order(key)
    key = jax.random.fold_in(key, 3)
    scale = grad_root() * tile_scales(order, [1.0, 0.2, 0.6, 0.6])
    return jax.random.normal(key, (N_MP, NT, B, B), jnp.float32) * scale[None, :, None, None]


def draw_second_moment(key, part):
    order = slot_order(key)
    key = jax.random.fold_in(key, 4)
    scale = grad_root() * tile_scales(order, [1.0, 0.2, 0.6, 0.6])
    return second_draw(key, (N_MP, NT, B, B), scale[None, :, None, None])


def draw_shared_vec(key, part):
    key = jax.random.fold_in(key, 5)
    base = 0.2 * jax.random.normal(key, (6, D), jnp.float32)
    return base + jnp.array([0.0, 0.0, 1.0, 0.0, 1.0, 0.0], jnp.float32)[:, None]


def draw_local_first(key, part):
    key = jax.random.fold_in(key, 6)
    return grad_root() * jax.random.normal(key, (N_MP, LV), jnp.float32)


def draw_local_second(key, part):
    key = jax.random.fold_in(key, 7)
    return second_draw(key, (N_MP, LV), grad_root())


def draw_shared_first(key, part):
    key = jax.random.fold_in(key, 8)
    return grad_root() * jax.random.normal(key, (6, D), jnp.float32)


def draw_shared_second(key, part):
    key = jax.random.fold_in(key, 9)
    return second_draw(key, (6, D), grad_root())


def shard_levels(key, shape, cuts, low, largest):
    loudness, own = 1.0, jax.random.fold_in(key, 6)
    for dim, parts in cuts:
        steps = jnp.exp(jax.random.uniform(jax.random.fold_in(own, dim), (parts,), jnp.float32, low / len(cuts), largest / len(cuts)))
        loudness = loudness * jnp.repeat(steps, shape[dim] // parts).reshape([-1 if axis == dim else 1 for axis in range(len(shape))])
    return loudness


def noise(stream_key, extent, scale, bound, pieces=(), held_as=jnp.bfloat16):
    level = shard_levels(stream_key, extent, pieces, -0.22, 0.18) if pieces else 1.0
    drawn = jax.random.normal(stream_key, extent, jnp.float32) * scale * level
    return jnp.minimum(jnp.maximum(drawn, -bound), bound).astype(held_as)


def setup_inputs(seed: int = 0) -> dict:
    key_of = jax.random.split(jax.random.key(seed), 16)
    return {
        "tokens": noise(key_of[0], (TOKENS, D), 1.0, 6.0, ((0, 8),)),
        "cotangent": noise(key_of[1], (TOKENS, D), 1.0, 6.0, ((0, 8),)),
        "lengths": draw_lengths(jax.random.fold_in(key_of[15], 71), 0),
        "tile_order": draw_tile_order(jax.random.fold_in(key_of[15], 71), 0),
        "master": draw_master(jax.random.fold_in(key_of[15], 71), 0),
        "first_moment": draw_first_moment(jax.random.fold_in(key_of[15], 71), 0),
        "second_moment": draw_second_moment(jax.random.fold_in(key_of[15], 71), 0),
        "basis_left": noise(key_of[7], (N_MP, NT, B, B), B ** -0.5, 0.625, ((0, 4), (1, 8)), jnp.float32),
        "basis_right": noise(key_of[8], (N_MP, NT, B, B), B ** -0.5, 0.625, ((0, 4), (1, 8)), jnp.float32),
        "local_vec": noise(key_of[9], (N_MP, LV), 0.2, 1.2, ((0, 4),), jnp.float32),
        "local_first": draw_local_first(jax.random.fold_in(key_of[15], 71), 0),
        "local_second": draw_local_second(jax.random.fold_in(key_of[15], 71), 0),
        "shared_vec": draw_shared_vec(jax.random.fold_in(key_of[15], 71), 0),
        "shared_first": draw_shared_first(jax.random.fold_in(key_of[15], 71), 0),
        "shared_second": draw_shared_second(jax.random.fold_in(key_of[15], 71), 0),
    }


@jax.custom_vjp
def low(v):
    return lax.optimization_barrier(v.astype(jnp.bfloat16)).astype(jnp.float32)

@jax.custom_vjp
def low_back(v):
    return v

def low_keep(v):
    return (low(v), None)

def low_pass(kept, grad):
    return (grad,)

def back_keep(v):
    return (v, None)

def back_low(kept, grad):
    return (low(grad),)
low.defvjp(low_keep, low_pass)
low_back.defvjp(back_keep, back_low)
NORM_EPS = 1e-05
BETA_ONE = 0.5
BETA_TWO = 0.5
ADAM_EPS = 1e-08
RATE_TILES = 0.04
RATE_VECTORS = 0.2
DECAY = 0.01
NEG_BIG = -1e+30
HIGH = lax.Precision.HIGHEST
ROOT_HALF = 0.7071067811865476

def gelu(values):
    return 0.5 * values * (1.0 + lax.erf(values * ROOT_HALF))

def normalize(values, gain, shift):
    centre = values - lax.optimization_barrier(jnp.mean(values, -1, keepdims=True))
    inv_scale = lax.rsqrt(lax.optimization_barrier(jnp.mean(centre * centre, -1, keepdims=True)) + NORM_EPS)
    return centre * inv_scale * gain + shift

def permitted(length, head_kind, seq_len):
    positions = jnp.arange(seq_len, dtype=jnp.int32)
    boundary = GRAIN * ((length + 2 * GRAIN - 1) // (2 * GRAIN))
    upper_half = positions >= boundary
    same_block = upper_half[:, None] == upper_half[None, :]
    within = (head_kind == 0)[:, None, None]
    return (positions < length)[None, None, :] & (same_block[None] == within)

def to_tiles(matrix, tile_edge):
    row_count, col_count = matrix.shape
    return matrix.reshape(row_count // tile_edge, tile_edge, col_count // tile_edge, tile_edge).transpose(0, 2, 1, 3).reshape(-1, tile_edge, tile_edge)

def from_tiles(tile_set, row_count, col_count):
    tile_edge = tile_set.shape[-1]
    return tile_set.reshape(row_count // tile_edge, col_count // tile_edge, tile_edge, tile_edge).transpose(0, 2, 1, 3).reshape(row_count, col_count)

def adam(grad, first, second):
    first_new = BETA_ONE * first + (1.0 - BETA_ONE) * grad
    second_new = BETA_TWO * second + (1.0 - BETA_TWO) * grad * grad
    step_dir = first_new / (1.0 - BETA_ONE ** STEP) / (jnp.sqrt(second_new / (1.0 - BETA_TWO ** STEP)) + ADAM_EPS)
    return (first_new, second_new, step_dir)

def layer(layer_params, inputs, length):
    w_qkv, w_out, w_up, w_down, local_vec, shared_vec = layer_params
    scale_qk = HD ** (-0.5)
    positions = jnp.arange(L, dtype=jnp.int32)
    valid = (positions < length).astype(jnp.float32)
    attn_total = jnp.zeros((L, D), jnp.float32)
    for group_id in range(N_MP):
        rounded_in = low_back(inputs)
        vector = local_vec[group_id]
        bias_qkv = jnp.concatenate([vector[:DM], jnp.zeros((DM,), jnp.float32), vector[DM:2 * DM]])
        qkv_all = jnp.dot(rounded_in, w_qkv[group_id], precision=HIGH) + bias_qkv
        qkv_all = low(low_back(qkv_all)).reshape(L, 3, HM, HD)
        head_kind = (group_id * HM + jnp.arange(HM, dtype=jnp.int32)) % 2
        allowed = permitted(length, head_kind, L)
        scores = jnp.einsum('qhd,khd->hqk', qkv_all[:, 0], qkv_all[:, 1], precision=HIGH) * scale_qk
        scores = jnp.where(allowed, low_back(scores), NEG_BIG)
        row_top = lax.optimization_barrier(jnp.max(scores, -1, keepdims=True))
        exponent = jnp.exp(scores - row_top)
        attn_probs = low(exponent / lax.optimization_barrier(jnp.sum(exponent, -1, keepdims=True)))
        mixed_heads = jnp.einsum('hqk,khd->qhd', attn_probs, qkv_all[:, 2], precision=HIGH).reshape(L, DM)
        mixed_heads = low(low_back(mixed_heads))
        attn_total = attn_total + low(jnp.dot(mixed_heads, w_out[group_id], precision=HIGH))
    z_one = inputs + low_back(attn_total) + shared_vec[0]
    hidden = normalize(z_one, shared_vec[2], shared_vec[3])
    hidden_low = low(hidden)
    ffn_total = jnp.zeros((L, D), jnp.float32)
    for group_id in range(N_MP):
        hidden_in = low_back(hidden_low)
        pre_act = jnp.dot(hidden_in, w_up[group_id], precision=HIGH) + local_vec[group_id][2 * DM:]
        activation = low(gelu(low_back(pre_act)))
        ffn_total = ffn_total + low(jnp.dot(activation, w_down[group_id], precision=HIGH))
    z_two = hidden + low_back(ffn_total) + shared_vec[1]
    return normalize(z_two, shared_vec[4], shared_vec[5]) * valid[:, None]

def reference(tokens, cotangent, lengths, tile_order, master, first_moment, second_moment, basis_left, basis_right, local_vec, local_first, local_second, shared_vec, shared_first, shared_second):
    weights = low(master)
    inverse = jnp.zeros((NT,), jnp.int32).at[tile_order].set(jnp.arange(NT, dtype=jnp.int32))
    natural = weights[:, inverse]
    cut_one = D // B * (3 * DM // B)
    cut_two = cut_one + DM // B * (D // B)
    cut_three = cut_two + D // B * (FM // B)
    w_qkv = jax.vmap(lambda tile_set: from_tiles(tile_set, D, 3 * DM))(natural[:, :cut_one])
    w_out = jax.vmap(lambda tile_set: from_tiles(tile_set, DM, D))(natural[:, cut_one:cut_two])
    w_up = jax.vmap(lambda tile_set: from_tiles(tile_set, D, FM))(natural[:, cut_two:cut_three])
    w_down = jax.vmap(lambda tile_set: from_tiles(tile_set, FM, D))(natural[:, cut_three:])
    layer_params = (w_qkv, w_out, w_up, w_down, local_vec, shared_vec)
    inputs = tokens.astype(jnp.float32).reshape(SEQS, L, D)
    cot_seq = cotangent.astype(jnp.float32).reshape(SEQS, L, D)

    def one_sequence(totals, seq_item):
        seq_in, seq_cot, length = seq_item
        result, pullback = jax.vjp(lambda params_now, input_now: layer(params_now, input_now, length), layer_params, seq_in)
        grad_sums, grad_in = pullback(seq_cot)
        return (jax.tree.map(jnp.add, totals, grad_sums), (result.astype(jnp.bfloat16), grad_in))
    totals, (outputs, input_grads) = lax.scan(one_sequence, jax.tree.map(jnp.zeros_like, layer_params), (inputs, cot_seq, lengths))
    tiler = jax.vmap(lambda matrix: to_tiles(matrix, B))
    natural_grads = jnp.concatenate([tiler(totals[0]), tiler(totals[1]), tiler(totals[2]), tiler(totals[3])], axis=1)
    tile_grads = natural_grads[:, tile_order]
    rotated = jnp.einsum('nski,nskl->nsil', basis_left, tile_grads, precision=HIGH)
    rotated = jnp.einsum('nsil,nslj->nsij', rotated, basis_right, precision=HIGH)
    tile_first, tile_second, direction = adam(rotated, first_moment, second_moment)
    turned = jnp.einsum('nsik,nskl->nsil', basis_left, direction, precision=HIGH)
    turned = jnp.einsum('nsil,nsjl->nsij', turned, basis_right, precision=HIGH)
    tile_weight = master - RATE_TILES * (turned + DECAY * master)
    local_grad = totals[4]
    local_first_new, local_second_new, local_dir = adam(local_grad, local_first, local_second)
    shared_grad = totals[5]
    shared_first_new, shared_second_new, shared_dir = adam(shared_grad, shared_first, shared_second)
    return (outputs.reshape(TOKENS, D), input_grads.reshape(TOKENS, D), tile_grads, tile_first, tile_second, tile_weight, local_grad, local_first_new, local_second_new, local_vec - RATE_VECTORS * local_dir, shared_grad, shared_first_new, shared_second_new, shared_vec - RATE_VECTORS * shared_dir)
```

```python
import functools
import jax
import jax.numpy as jnp
from jax import lax
from jax.experimental import pallas as pl
from jax.experimental.pallas import tpu as pltpu
from jax.sharding import PartitionSpec as P

MESH = pl.DeviceIdType.MESH
f32 = jnp.float32
bf16 = jnp.bfloat16


def lanes_of(shape):
    return lax.broadcasted_iota(jnp.int32, shape, len(shape) - 1)


def turn(v, amount):
    return pltpu.roll(v, amount, v.ndim - 1)


def pack_four(tiles):
    lane = lanes_of(tiles[0].shape)
    return [
        jnp.where(lane < 96, tiles[k], turn(tiles[3], 96 - 32 * k)) for k in range(3)
    ]


def fourth_of(blocks):
    lane = lanes_of(blocks[0].shape)
    first, second, third = (turn(blocks[k], 32 + 32 * k) for k in range(3))
    return jnp.where(lane < 32, first, jnp.where(lane < 64, second, third))


def join_four(tiles):
    lane = lanes_of(tiles[0].shape)
    b, c, d = turn(tiles[1], 96), turn(tiles[2], 64), turn(tiles[3], 32)
    return [
        jnp.where(lane < 96, tiles[0], b),
        jnp.where(lane < 64, b, c),
        jnp.where(lane < 32, c, d),
    ]


def split_four(pieces):
    lane = lanes_of(pieces[0].shape)
    return [
        pieces[0],
        jnp.where(lane < 32, turn(pieces[0], 32), turn(pieces[1], 32)),
        jnp.where(lane < 64, turn(pieces[1], 64), turn(pieces[2], 64)),
        turn(pieces[2], 96),
    ]


def place():
    d, m = lax.axis_index("dp"), lax.axis_index("mp")
    return d // 2, d % 2, m // 2, m % 2


class Net:
    def __init__(self, nz):
        self.nz = nz
        self.z, self.x, self.y, self.c = place()
        self.d = self.z * 2 + self.x
        self.m = self.y * 2 + self.c
        self.xn = (self.z * 2 + 1 - self.x, self.m)
        self.yn = (self.d, (1 - self.y) * 2 + self.c)
        self.cn = (self.d, self.y * 2 + 1 - self.c)
        self.up = (self.d + 2, self.m)
        self.dn = (self.d - 2, self.m)
        self.has_up = self.z < nz - 1
        self.has_dn = self.z > 0

    def enter(self):
        bar = pltpu.get_barrier_semaphore()
        others = [(lax.rem(self.z + k, self.nz) * 2 + self.x, self.m) for k in range(1, self.nz)]
        peers = [self.xn, self.yn, self.cn] + others
        for peer in peers:
            pl.semaphore_signal(bar, inc=1, device_id=peer, device_id_type=MESH)
        pl.semaphore_wait(bar, len(peers))


def send(src, dst, ss, rs, peer):
    return pltpu.make_async_remote_copy(
        src_ref=src, dst_ref=dst, send_sem=ss, recv_sem=rs, device_id=peer, device_id_type=MESH
    )


def tile_qkv(r, j):
    return (j % 8) // 2, r * 6 + (j // 8) * 2 + j % 2


def tile_out(r, j):
    return r // 2, 48 + (r % 2) * 8 + j


def tile_up(r, j):
    return j // 8, 64 + r * 8 + j % 8


def tile_down(r, j):
    return r // 8, 128 + (r % 8) * 8 + j


GRIDS = ((8, 24, tile_qkv), (8, 8, tile_out), (8, 32, tile_up), (32, 8, tile_down))


def gather_kernel(
    nz, src_ref, master_ref, local_ref, o_qkv, o_out, o_up, o_down, o_local,
    G, LV, d_qkv, d_out, d_up, d_down,
    zs, zr, xs, xr, ys, yr, xds, xdr, yds, ydr, cs, cr, outs, lvs, lvr,
):
    net = Net(nz)
    z, x, y, c, m = net.z, net.x, net.y, net.c, net.m
    my = (1 - y) * 2 + c
    net.enter()
    full = 18
    half = 9
    LV[m] = local_ref[...]
    lv_y = send(LV.at[m], LV.at[m], lvs.at[0], lvr.at[0], net.yn)
    lv_c = send(LV.at[m], LV.at[m], lvs.at[1], lvr.at[1], net.cn)
    lv_d = send(LV.at[my], LV.at[my], lvs.at[2], lvr.at[2], net.cn)
    lv_y.start()
    lv_c.start()

    def slot(mo, zo, xo, lo=0, n=full):
        return G.at[mo, pl.ds((zo * 2 + xo) * 24 + lo, n)]

    for q in range(6):
        tiles = [
            jnp.concatenate([master_ref[4 * q + k], jnp.zeros((96, 32), f32)], axis=-1)
            for k in range(4)
        ]
        for k, block in enumerate(pack_four(tiles)):
            G[m, net.d * 24 + 3 * q + k] = block.astype(bf16)

    def z_copy(zo, direction):
        s = slot(m, zo, x)
        peer = net.up if direction == 0 else net.dn
        return send(s, s, zs.at[zo, direction], zr.at[zo], peer)

    def c_copy(zo, kind):
        mo = (m, m, my, my)[kind]
        xo = (x, 1 - x, x, 1 - x)[kind]
        s = slot(mo, zo, xo)
        return send(s, s, cs.at[zo, kind], cr.at[zo, kind], net.cn)

    def c_arrival(zo, kind):
        mo = (m, m, my, my)[kind] + 1 - 2 * c
        xo = (x, 1 - x, x, 1 - x)[kind]
        s = slot(mo, zo, xo)
        return send(s, s, cs.at[zo, kind], cr.at[zo, kind], net.cn)

    def x_copy(zo, xo):
        s = slot(m, zo, xo)
        return send(s, s, xs.at[zo], xr.at[zo], net.xn)

    def y_copy(zo, mo):
        s = slot(mo, zo, x)
        return send(s, s, ys.at[zo], yr.at[zo], net.yn)

    def xd_copy(zo, xo):
        s = slot(my, zo, xo, 0, half)
        return send(s, s, xds.at[zo], xdr.at[zo], net.xn)

    def yd_copy(zo, mo):
        s = slot(mo, zo, 1 - x, half, half)
        return send(s, s, yds.at[zo], ydr.at[zo], net.yn)

    def fan(zo):
        x_copy(zo, x).start()
        y_copy(zo, m).start()
        c_copy(zo, 0).start()

    def diag(zo):
        x_copy(zo, 1 - x).wait_recv()
        yd_copy(zo, m).start()
        c_copy(zo, 1).start()
        y_copy(zo, my).wait_recv()
        xd_copy(zo, x).start()
        c_copy(zo, 2).start()

    def fin(zo):
        xd_copy(zo, 1 - x).wait_recv()
        yd_copy(zo, my).wait_recv()
        c_copy(zo, 3).start()

    def each(step, fn):
        if step == 0:
            fn(z, 0)
            return

        @pl.when(z >= step)
        def _():
            fn(z - step, 1)

        @pl.when(z + step < nz)
        def _():
            fn(z + step, -1)

    def arrive(zo, side):
        if isinstance(side, int) and side == 0:
            @pl.when(net.has_up)
            def _():
                z_copy(zo, 0).start()

            @pl.when(net.has_dn)
            def _():
                z_copy(zo, 1).start()
        elif side == 1:
            z_copy(zo, 0).wait_recv()

            @pl.when(net.has_up)
            def _():
                z_copy(zo, 0).start()
        else:
            z_copy(zo, 1).wait_recv()

            @pl.when(net.has_dn)
            def _():
                z_copy(zo, 1).start()
        fan(zo)

    for step in range(nz + 2):
        if step < nz:
            each(step, arrive)
        if 0 <= step - 1 < nz:
            each(step - 1, lambda zo, side: diag(zo))
        if 0 <= step - 2:
            each(step - 2, lambda zo, side: fin(zo))
    send(LV.at[my], LV.at[my], lvs.at[0], lvr.at[0], net.yn).wait_recv()
    lv_d.start()
    mc = m + 1 - 2 * c
    send(LV.at[mc], LV.at[mc], lvs.at[1], lvr.at[1], net.cn).wait_recv()
    mc = my + 1 - 2 * c
    send(LV.at[mc], LV.at[mc], lvs.at[2], lvr.at[2], net.cn).wait_recv()
    o_local[...] = LV[...]
    lv_y.wait_send()
    lv_c.wait_send()
    lv_d.wait_send()
    for zo in range(nz):
        for kind in range(4):
            c_arrival(zo, kind).wait_recv()

    def sent(zo, side):
        x_copy(zo, x).wait_send()
        y_copy(zo, m).wait_send()
        yd_copy(zo, m).wait_send()
        xd_copy(zo, x).wait_send()
        for kind in range(4):
            c_copy(zo, kind).wait_send()
        if side == 0 or side == 1:
            @pl.when(net.has_up)
            def _():
                z_copy(zo, 0).wait_send()
        if side == 0 or side == -1:
            @pl.when(net.has_dn)
            def _():
                z_copy(zo, 1).wait_send()

    for step in range(nz):
        each(step, sent)

    def fourth(i, _):
        mo, rest = i // (2 * nz), i % (2 * nz)
        for q in range(6):
            tile = fourth_of([G[mo, rest * 24 + 3 * q + k].astype(f32) for k in range(3)])
            G[mo, rest * 24 + 18 + q] = tile.astype(bf16)
        return 0

    lax.fori_loop(0, 4 * 2 * nz, fourth, 0)

    copies = []
    for i, ((rows, cols, where), dense, out) in enumerate(
        zip(GRIDS, (d_qkv, d_out, d_up, d_down), (o_qkv, o_out, o_up, o_down))
    ):
        def fill(r, _):
            for g in range(cols // 4):
                tiles = []
                for t in range(4):
                    p, n = where(r, 4 * g + t)
                    tiles.append(G[p, src_ref[n]].astype(f32))
                for k, piece in enumerate(join_four(tiles)):
                    dense[pl.ds(pl.multiple_of(r * 96, 96), 96), pl.ds(384 * g + 128 * k, 128)] = (
                        piece.astype(bf16)
                    )
            return 0

        lax.fori_loop(0, rows, fill, 0)
        copy = pltpu.make_async_copy(dense, out, outs.at[i])
        copy.start()
        copies.append(copy)
    for copy in copies:
        copy.wait()


def gather_weights(nz, src, master, local):
    dma = pltpu.SemaphoreType.DMA
    shapes = [(r * 96, c * 96) for r, c, _ in GRIDS]
    return pl.pallas_call(
        functools.partial(gather_kernel, nz),
        out_shape=[jax.ShapeDtypeStruct(s, bf16) for s in shapes]
        + [jax.ShapeDtypeStruct((4, *local.shape), f32)],
        in_specs=[pl.BlockSpec(memory_space=pltpu.SMEM)]
        + [pl.BlockSpec(memory_space=pltpu.VMEM)] * 2,
        out_specs=[pl.BlockSpec(memory_space=pl.ANY)] * 4 + [pl.BlockSpec(memory_space=pltpu.VMEM)],
        scratch_shapes=[pltpu.VMEM((4, 2 * nz * 24, 96, 128), bf16), pltpu.VMEM((4, *local.shape), f32)]
        + [pltpu.VMEM(s, bf16) for s in shapes]
        + [dma((nz, 2)), dma((nz,))]
        + [dma((nz,))] * 8
        + [dma((nz, 4)), dma((nz, 4)), dma((4,)), dma((3,)), dma((3,))],
        compiler_params=pltpu.CompilerParams(
            collective_id=0, has_side_effects=True, vmem_limit_bytes=56 << 20
        ),
        name="gather_weights",
    )(src, master, local)


def slot_sources(tile_order, per_owner):
    count = tile_order.shape[0]
    hit = tile_order[None, :] == jnp.arange(count, dtype=jnp.int32)[:, None]
    at = jnp.sum(jnp.where(hit, jnp.arange(count, dtype=jnp.int32)[None, :], 0), 1)
    owner, pos = at // per_owner, at % per_owner
    quad, k = pos // 4, pos % 4
    return owner * 24 + jnp.where(k < 3, 3 * quad + k, 18 + quad)
NEG_BIG = -1e30
NORM_EPS = 1e-05
ROOT_HALF = 0.7071067811865476
PHI_SCALE = 0.3989422804014327


def nt(a, b):
    return lax.dot_general(a, b, (((1,), (1,)), ((), ())), preferred_element_type=f32)


def tn(a, b):
    return lax.dot_general(a, b, (((0,), (0,)), ((), ())), preferred_element_type=f32)


def nn(a, b):
    return jnp.dot(a, b, preferred_element_type=f32)


def edges(info_ref):
    length = info_ref[2]
    return 64 * ((length + 127) // 128), length, info_ref[1]


def chosen_rows(info_ref, rows):
    bound, _, part = edges(info_ref)
    row = lax.broadcasted_iota(jnp.int32, (rows, 128), 0) + part * rows
    lane = lax.broadcasted_iota(jnp.int32, (rows, 128), 1)
    return (row < bound) == (lane < 64)


def chosen_cols(info_ref, rows):
    bound, _, part = edges(info_ref)
    row = lax.broadcasted_iota(jnp.int32, (128, rows), 1) + part * rows
    lane = lax.broadcasted_iota(jnp.int32, (128, rows), 0)
    return (row < bound) == (lane < 64)


def attend_kernel(info_ref, x_ref, w_ref, b_ref, q_ref, k_ref, v_ref, p_ref, o_ref):
    pair = pl.program_id(0)
    rows = q_ref.shape[0]
    width = q_ref.shape[1]
    bound, length, part = edges(info_ref)
    zero = jnp.zeros((), bf16)

    @pl.when(pair == 0)
    def _():
        def project(lo, at, count):
            def body(r, _):
                base = pl.multiple_of(at + r * rows, rows)
                out = nn(x_ref[pl.ds(base, rows), :], w_ref[:, lo : lo + 256]) + b_ref[:, lo : lo + 256]
                lane = lo % width
                if lo < width:
                    q_ref[:, lane : lane + 256] = out.astype(bf16) * jnp.asarray(0.125, bf16)
                elif lo < 2 * width:
                    k_ref[pl.ds(base, rows), lane : lane + 256] = out.astype(bf16)
                else:
                    v_ref[pl.ds(base, rows), lane : lane + 256] = out.astype(bf16)
                return 0

            lax.fori_loop(0, count, body, 0)

        for lo in range(0, width, 256):
            project(lo, part * rows, 1)
        for lo in range(width, 3 * width, 256):
            project(lo, 0, x_ref.shape[0] // rows)

    cols = pl.ds(pl.multiple_of(pair * 128, 128), 128)
    queries = q_ref[:, cols]
    pick = chosen_rows(info_ref, rows)
    outs = []
    for w in range(2):
        start = 0 if w == 0 else pl.multiple_of(bound, 64)
        limit = bound if w == 0 else length - bound
        keys = k_ref[pl.ds(start, rows), cols]
        values = v_ref[pl.ds(start, rows), cols]
        these = jnp.where(pick, queries, zero) if w == 0 else jnp.where(pick, zero, queries)
        scores = nt(keys, these)
        inside = lax.broadcasted_iota(jnp.int32, scores.shape, 0) < limit
        scores = jnp.where(inside, scores, NEG_BIG)
        top = jnp.max(scores, 0, keepdims=True)
        weight = jnp.exp(scores - top)
        probs = (weight * (1.0 / jnp.sum(weight, 0, keepdims=True))).astype(bf16)
        p_ref[0, w] = probs
        outs.append(tn(values, probs))
    o_ref[...] = jnp.where(chosen_cols(info_ref, rows), outs[0], outs[1]).astype(bf16)


def attend(info, tokens, w_qkv, bias, seq_len, rows):
    width = w_qkv.shape[0]
    pairs = width // 128
    whole = lambda shape: pl.BlockSpec(shape, lambda i, s: (0,) * len(shape))
    return pl.pallas_call(
        attend_kernel,
        grid_spec=pltpu.PrefetchScalarGridSpec(
            num_scalar_prefetch=1,
            grid=(pairs,),
            in_specs=[
                pl.BlockSpec((seq_len, width), lambda i, s: (s[0], 0)),
                whole((width, 3 * width)),
                whole((1, 3 * width)),
            ],
            out_specs=[
                whole((rows, width)),
                whole((seq_len, width)),
                whole((seq_len, width)),
                pl.BlockSpec((1, 2, rows, rows), lambda i, s: (i, 0, 0, 0)),
                pl.BlockSpec((128, rows), lambda i, s: (i, 0)),
            ],
        ),
        out_shape=[
            jax.ShapeDtypeStruct((rows, width), bf16),
            jax.ShapeDtypeStruct((seq_len, width), bf16),
            jax.ShapeDtypeStruct((seq_len, width), bf16),
            jax.ShapeDtypeStruct((pairs, 2, rows, rows), bf16),
            jax.ShapeDtypeStruct((width, rows), bf16),
        ],
        compiler_params=pltpu.CompilerParams(vmem_limit_bytes=56 << 20),
        name="attend",
    )(info, tokens, w_qkv, bias)


def standard(values):
    centre = values - jnp.mean(values, -1, keepdims=True)
    scale = lax.rsqrt(jnp.mean(centre * centre, -1, keepdims=True) + NORM_EPS)
    return centre * scale, scale


def standard_back(grad, normed, scale, gain):
    inner = grad * gain
    return scale * (
        inner - jnp.mean(inner, -1, keepdims=True) - normed * jnp.mean(inner * normed, -1, keepdims=True)
    )


def col_sum(values):
    return jnp.sum(values, 0, keepdims=True)


def middle_kernel(
    info_ref, o_ref, wo_ref, x_ref, cot_ref, sv_ref, wu_ref, wd_ref, bu_ref,
    out_ref, tu_ref, td_ref, to_ref, go_ref, gz_ref, db_ref, ds_ref,
    hid, low, low_t, n_one, r_one, acc, act, slope, g_low,
):
    step = pl.program_id(0)
    chunks = pl.num_programs(0) // 2
    rows, width = hid.shape
    piece = 128

    def by_rows(fn):
        def body(r, _):
            fn(pl.ds(pl.multiple_of(r * piece, piece), piece), r)
            return 0

        lax.fori_loop(0, rows // piece, body, 0)

    @pl.when(step == 0)
    def _():
        acc[...] = tn(o_ref[...], wo_ref[...])

        def norm(at, r):
            z_one = x_ref[at, :].astype(f32) + acc[at, :] + sv_ref[0:1, :]
            normed, scale = standard(z_one)
            hidden = normed * sv_ref[2:3, :] + sv_ref[3:4, :]
            n_one[at, :] = normed
            r_one[at, :] = jnp.broadcast_to(scale, (piece, 128))
            hid[at, :] = hidden
            low[at, :] = hidden.astype(bf16)
            acc[at, :] = jnp.zeros((piece, width), f32)

        by_rows(norm)
        low_t[...] = low[...].T

    @pl.when(step < chunks)
    def _():
        pre = nn(low[...], wu_ref[...]) + bu_ref[...]
        phi = 0.5 * (1.0 + lax.erf(pre * ROOT_HALF))
        density = jnp.exp(-0.5 * pre * pre) * PHI_SCALE
        here = (pre * phi).astype(bf16)
        act[step] = here
        slope[step] = (phi + pre * density).astype(bf16)
        acc[...] += nn(here, wd_ref[...])

    @pl.when(step == chunks)
    def _():
        ds_ref[...] = jnp.zeros_like(ds_ref)
        _, length, part = edges(info_ref)

        def norm(at, r):
            z_two = hid[at, :] + acc[at, :] + sv_ref[1:2, :]
            normed, scale = standard(z_two)
            row = lax.broadcasted_iota(jnp.int32, (piece, 1), 0) + part * rows + r * piece
            valid = (row < length).astype(f32)
            out_ref[at, :] = ((normed * sv_ref[4:5, :] + sv_ref[5:6, :]) * valid).astype(bf16)
            grad = cot_ref[at, :].astype(f32) * valid
            back = standard_back(grad, normed, scale, sv_ref[4:5, :])
            ds_ref[4:5, :] += col_sum(grad * normed)
            ds_ref[5:6, :] += col_sum(grad)
            ds_ref[1:2, :] += col_sum(back)
            g_low[at, :] = back.astype(bf16)
            acc[at, :] = back

        by_rows(norm)

    @pl.when(step >= chunks)
    def _():
        at = step - chunks
        grad_act = nt(g_low[...], wd_ref[...])
        grad_pre = grad_act * slope[at].astype(f32)
        grad_low = grad_pre.astype(bf16)
        db_ref[...] = col_sum(grad_low.astype(f32))
        acc[...] += nt(grad_low, wu_ref[...])
        down = tn(act[at], g_low[...])
        for r in range(4):
            for g in range(width // 384):
                cut = [
                    down[96 * r : 96 * r + 96, 384 * g + 128 * k : 384 * g + 128 * k + 128]
                    for k in range(3)
                ]
                for t, tile in enumerate(split_four(cut)):
                    td_ref[0, 0, r * (width // 96) + 4 * g + t] = tile.astype(bf16)
        up = nn(low_t[...], grad_low)
        for r in range(width // 96):
            cut = [up[96 * r : 96 * r + 96, 128 * k : 128 * k + 128] for k in range(3)]
            for t, tile in enumerate(split_four(cut)):
                tu_ref[0, r, 0, t] = tile.astype(bf16)

    @pl.when(step == 2 * chunks - 1)
    def _():
        def norm(at, r):
            grad = acc[at, :]
            normed = n_one[at, :]
            back = standard_back(grad, normed, r_one[at, 0:1], sv_ref[2:3, :])
            ds_ref[2:3, :] += col_sum(grad * normed)
            ds_ref[3:4, :] += col_sum(grad)
            ds_ref[0:1, :] += col_sum(back)
            gz_ref[at, :] = back
            g_low[at, :] = back.astype(bf16)

        by_rows(norm)
        go_ref[...] = nt(g_low[...], wo_ref[...]).astype(bf16)
        for g in range(width // 384):
            outer = nn(o_ref[...], g_low[:, 384 * g : 384 * g + 384])
            for r in range(width // 96):
                cut = [outer[96 * r : 96 * r + 96, 128 * k : 128 * k + 128] for k in range(3)]
                for t, tile in enumerate(split_four(cut)):
                    to_ref[r, 4 * g + t] = tile.astype(bf16)


def middle(info, o_t, w_out, tokens, cotangent, shared, w_up, w_down, bias_up, rows):
    width = w_out.shape[0]
    hidden = w_up.shape[1]
    cut = 384
    chunks = hidden // cut
    groups = hidden // 768
    whole = lambda shape: pl.BlockSpec(shape, lambda i, s: (0,) * len(shape))
    back = lambda i: jnp.maximum(i - chunks, 0)
    dma_rows = pl.BlockSpec((rows, width), lambda i, s: (s[3], 0))
    tiles = width // 96
    return pl.pallas_call(
        middle_kernel,
        grid_spec=pltpu.PrefetchScalarGridSpec(
            num_scalar_prefetch=1,
            grid=(2 * chunks,),
            in_specs=[
                whole((width, rows)),
                whole((width, width)),
                dma_rows,
                dma_rows,
                whole((6, width)),
                pl.BlockSpec((width, cut), lambda i, s: (0, i % chunks)),
                pl.BlockSpec((cut, width), lambda i, s: (i % chunks, 0)),
                pl.BlockSpec((1, cut), lambda i, s: (0, i % chunks)),
            ],
            out_specs=[
                whole((rows, width)),
                pl.BlockSpec(
                    (1, tiles, 1, 4, 96, 128), lambda i, s: (back(i) // 2, 0, back(i) % 2, 0, 0, 0)
                ),
                pl.BlockSpec(
                    (1, 1, 4 * tiles, 96, 128), lambda i, s: (back(i) // 2, back(i) % 2, 0, 0, 0)
                ),
                whole((tiles, tiles, 96, 128)),
                whole((rows, width)),
                whole((rows, width)),
                pl.BlockSpec((1, cut), lambda i, s: (0, back(i))),
                whole((6, width)),
            ],
            scratch_shapes=[
                pltpu.VMEM((rows, width), f32),
                pltpu.VMEM((rows, width), bf16),
                pltpu.VMEM((width, rows), bf16),
                pltpu.VMEM((rows, width), f32),
                pltpu.VMEM((rows, 128), f32),
                pltpu.VMEM((rows, width), f32),
                pltpu.VMEM((chunks, rows, cut), bf16),
                pltpu.VMEM((chunks, rows, cut), bf16),
                pltpu.VMEM((rows, width), bf16),
            ],
        ),
        out_shape=[
            jax.ShapeDtypeStruct((rows, width), bf16),
            jax.ShapeDtypeStruct((groups, tiles, 2, 4, 96, 128), bf16),
            jax.ShapeDtypeStruct((groups, 2, 4 * tiles, 96, 128), bf16),
            jax.ShapeDtypeStruct((tiles, tiles, 96, 128), bf16),
            jax.ShapeDtypeStruct((rows, width), bf16),
            jax.ShapeDtypeStruct((rows, width), f32),
            jax.ShapeDtypeStruct((1, hidden), f32),
            jax.ShapeDtypeStruct((6, width), f32),
        ],
        compiler_params=pltpu.CompilerParams(vmem_limit_bytes=56 << 20),
        name="middle",
    )(info, o_t, w_out, tokens, cotangent, shared, w_up, w_down, bias_up)


def attend_back_kernel(
    info_ref, go_ref, q_ref, k_ref, v_ref, p_ref, o_ref, x_ref, w_ref, gz_ref,
    tq_ref, own_ref, other_ref, bias_ref, dq, dk, dv,
):
    pair = pl.program_id(0)
    rows, width = dq.shape
    seq_len = dk.shape[0]
    bound, length, part = edges(info_ref)
    zero = jnp.zeros((), bf16)
    cols = pl.ds(pl.multiple_of(pair * 128, 128), 128)
    pick = chosen_rows(info_ref, rows)
    pick_t = chosen_cols(info_ref, rows)
    queries = q_ref[:, cols]
    grads = go_ref[...]
    grads_t = grads.astype(f32).T
    inner = grads_t * o_ref[...].astype(f32)
    outs = []
    dk[rows:, cols] = jnp.zeros((seq_len - rows, 128), bf16)
    dv[rows:, cols] = jnp.zeros((seq_len - rows, 128), bf16)
    for w in range(2):
        start = 0 if w == 0 else pl.multiple_of(bound, 64)
        keys = k_ref[pl.ds(start, rows), cols]
        values = v_ref[pl.ds(start, rows), cols]
        mine = (lambda a: jnp.where(pick, a, zero)) if w == 0 else (lambda a: jnp.where(pick, zero, a))
        mine_t = (lambda a: jnp.where(pick_t, a, 0.0)) if w == 0 else (lambda a: jnp.where(pick_t, 0.0, a))
        dot_sum = jnp.sum(mine_t(inner), 0, keepdims=True)
        grad_probs = nn(values, mine_t(grads_t).astype(bf16))
        probs = p_ref[0, w]
        grad_scores = (probs.astype(f32) * (grad_probs - dot_sum)).astype(bf16)
        dv[pl.ds(start, rows), cols] = nn(probs, mine(grads)).astype(bf16)
        dk[pl.ds(start, rows), cols] = nn(grad_scores, mine(queries)).astype(bf16)
        outs.append(tn(keys, grad_scores))
    dq[:, cols] = (jnp.where(pick_t, outs[0], outs[1]) * 0.125).T.astype(bf16)

    @pl.when(pair == pl.num_programs(0) - 1)
    def _():
        here = pl.ds(pl.multiple_of(part * rows, rows), rows)
        there = pl.ds(pl.multiple_of((1 - part) * rows, rows), rows)
        bias_ref[0:1, :] = col_sum(dq[...].astype(f32))
        bias_ref[1:2, :] = col_sum(dv[...].astype(f32))
        own_ref[...] = (
            gz_ref[...]
            + nt(dq[...], w_ref[:, :width])
            + nt(dk[here, :], w_ref[:, width : 2 * width])
            + nt(dv[here, :], w_ref[:, 2 * width :])
        )
        other_ref[...] = (
            nt(dk[there, :], w_ref[:, width : 2 * width]) + nt(dv[there, :], w_ref[:, 2 * width :])
        ).astype(bf16)
        for index, (grad, source) in enumerate(((dq, here), (dk, pl.ds(0, seq_len)), (dv, pl.ds(0, seq_len)))):
            for g in range(width // 384):
                outer = tn(x_ref[source, :], grad[:, 384 * g : 384 * g + 384])
                for r in range(width // 96):
                    cut = [outer[96 * r : 96 * r + 96, 128 * k : 128 * k + 128] for k in range(3)]
                    for t, tile in enumerate(split_four(cut)):
                        p, n = tile_qkv(r, index * (width // 96) + 4 * g + t)
                        tq_ref[p, n] = tile.astype(bf16)


def attend_back(info, g_o, q, k, v, probs, o_t, tokens, w_qkv, g_z):
    rows, width = q.shape
    seq_len = k.shape[0]
    pairs = width // 128
    whole = lambda shape: pl.BlockSpec(shape, lambda i, s: (0,) * len(shape))
    return pl.pallas_call(
        attend_back_kernel,
        grid_spec=pltpu.PrefetchScalarGridSpec(
            num_scalar_prefetch=1,
            grid=(pairs,),
            in_specs=[
                pl.BlockSpec((rows, 128), lambda i, s: (0, i)),
                whole((rows, width)),
                whole((seq_len, width)),
                whole((seq_len, width)),
                pl.BlockSpec((1, 2, rows, rows), lambda i, s: (i, 0, 0, 0)),
                pl.BlockSpec((128, rows), lambda i, s: (i, 0)),
                pl.BlockSpec((seq_len, width), lambda i, s: (s[0], 0)),
                whole((width, 3 * width)),
                whole((rows, width)),
            ],
            out_specs=[
                whole((4, 48, 96, 128)),
                whole((rows, width)),
                whole((rows, width)),
                whole((2, width)),
            ],
            scratch_shapes=[
                pltpu.VMEM((rows, width), bf16),
                pltpu.VMEM((seq_len, width), bf16),
                pltpu.VMEM((seq_len, width), bf16),
            ],
        ),
        out_shape=[
            jax.ShapeDtypeStruct((4, 48, 96, 128), bf16),
            jax.ShapeDtypeStruct((rows, width), f32),
            jax.ShapeDtypeStruct((rows, width), bf16),
            jax.ShapeDtypeStruct((2, width), f32),
        ],
        compiler_params=pltpu.CompilerParams(vmem_limit_bytes=56 << 20),
        name="attend_back",
    )(info, g_o, q, k, v, probs, o_t, tokens, w_qkv, g_z)
def pack_kernel(order_ref, tq_ref, to_ref, tu_ref, td_ref, w_ref, tiles, sems):
    p, d = pl.program_id(0), pl.program_id(1)
    slot = p % 2

    def loads(group, at):
        first = 0
        for i, src in enumerate((tq_ref, to_ref, tu_ref, td_ref)):
            count = src.shape[1]
            yield pltpu.make_async_copy(
                src.at[group], tiles.at[at, pl.ds(first, count)], sems.at[at, i]
            )
            first += count

    @pl.when((p == 0) & (d == 0))
    def _():
        for copy in loads(0, 0):
            copy.start()

    @pl.when(d == 0)
    def _():
        for copy in loads(p, slot):
            copy.wait()

        @pl.when(p + 1 < pl.num_programs(0))
        def _():
            for copy in loads(p + 1, 1 - slot):
                copy.start()

    for q in range(6):
        four = [tiles[slot, order_ref[d * 24 + 4 * q + t]].astype(f32) for t in range(4)]
        for k, block in enumerate(pack_four(four)):
            w_ref[0, 0, 3 * q + k] = block.astype(bf16)


def pack(order, tq, to, tu, td):
    owners = order.shape[0] // 24
    anywhere = pl.BlockSpec(memory_space=pl.ANY)
    return pl.pallas_call(
        pack_kernel,
        grid_spec=pltpu.PrefetchScalarGridSpec(
            num_scalar_prefetch=1,
            grid=(4, owners),
            in_specs=[anywhere] * 4,
            out_specs=pl.BlockSpec((1, 1, 18, 96, 128), lambda p, d, s: (p, d, 0, 0, 0)),
            scratch_shapes=[
                pltpu.VMEM((2, order.shape[0], 96, 128), bf16),
                pltpu.SemaphoreType.DMA((2, 4)),
            ],
        ),
        out_shape=jax.ShapeDtypeStruct((4, owners, 18, 96, 128), bf16),
        compiler_params=pltpu.CompilerParams(vmem_limit_bytes=40 << 20),
        name="pack",
    )(order, tq, to, tu, td)


def scatter_kernel(
    nz, w_ref, own_ref, other_ref, local_ref, shared_ref,
    tile_o, dx_o, local_o, shared_o,
    A, R, XD, YD, X, Y, Z, dx_in, la, lb, sa, sb,
    lsem, cs, cr, xds, xdr, yds, ydr, xs, xr, ys, yr, zs, zr, dxs, vs, vr,
):
    net = Net(nz)
    z, x, y, c, m, d = net.z, net.x, net.y, net.c, net.m, net.d
    my = (1 - y) * 2 + c
    far = (lax.rem(z + 2, nz) * 2 + x, m)
    near = ((z + 1 - 2 * (z % 2)) * 2 + x, m)
    net.enter()
    half = 9
    low, high = pl.ds(0, half), pl.ds(half, half)
    kinds = ((m, x), (m, 1 - x), (my, x), (my, 1 - x))
    flip = 1 - 2 * c

    def load(zo, kind):
        mo, xo = kinds[kind]
        return pltpu.make_async_copy(w_ref.at[mo, zo * 2 + xo], A.at[zo, kind], lsem.at[zo, kind])

    def c_copy(zo, kind):
        mo, xo = kinds[kind]
        return send(
            w_ref.at[mo + flip, zo * 2 + xo], R.at[zo, kind], cs.at[zo, kind], cr.at[zo, kind], net.cn
        )

    def xd_copy(zo):
        return send(A.at[zo, 3, low], XD.at[zo], xds.at[zo], xdr.at[zo], net.xn)

    def yd_copy(zo):
        return send(A.at[zo, 3, high], YD.at[zo], yds.at[zo], ydr.at[zo], net.yn)

    def x_copy(zo):
        return send(A.at[zo, 1], X.at[zo], xs.at[zo], xr.at[zo], net.xn)

    def y_copy(zo):
        return send(A.at[zo, 2], Y.at[zo], ys.at[zo], yr.at[zo], net.yn)

    def z_copy(zo, direction):
        return send(
            A.at[zo, 0], Z.at[zo, direction], zs.at[zo], zr.at[zo, direction],
            net.up if direction == 0 else net.dn,
        )

    dx_copy = send(other_ref, dx_in, dxs.at[0], dxs.at[1], net.cn)
    peers = (net.cn, net.xn, net.yn, near, far)

    def v_copies(k):
        return (
            send(la.at[k], lb.at[k], vs.at[k, 0], vr.at[k, 0], peers[k]),
            send(sa.at[k], sb.at[k], vs.at[k, 1], vr.at[k, 1], peers[k]),
        )

    def v_start(k):
        for copy in v_copies(k):
            copy.start()

    def v_finish(k):
        for copy in v_copies(k):
            copy.wait_recv()
        la[k + 1] = la[k] + lb[k]
        sa[k + 1] = sa[k] + sb[k]

    def add(zo, kind, other, lo=0, n=18):
        def body(i, _):
            A[zo, kind, lo + i] = (A[zo, kind, lo + i].astype(f32) + other(i)).astype(bf16)
            return 0

        lax.fori_loop(0, n, body, 0)

    def each(step, fn):
        if step == 0:
            fn(z, 0)
            return

        @pl.when(z >= step)
        def _():
            fn(z - step, 1)

        @pl.when(z + step < nz)
        def _():
            fn(z + step, -1)

    def begin(zo, side):
        for kind in (3, 1, 2, 0):
            load(zo, kind).start()
            c_copy(zo, kind).start()

    def phase_one(zo, side):
        for kind in (3, 1, 2, 0):
            load(zo, kind).wait()
            c_copy(zo, kind).wait_recv()
            add(zo, kind, lambda i: R[zo, kind, i].astype(f32))
            if kind == 3:
                xd_copy(zo).start()
                yd_copy(zo).start()

    def phase_two(zo, side):
        yd_copy(zo).wait_recv()
        add(zo, 1, lambda i: YD[zo, i].astype(f32), half, half)
        x_copy(zo).start()
        xd_copy(zo).wait_recv()
        add(zo, 2, lambda i: XD[zo, i].astype(f32), 0, half)
        y_copy(zo).start()

    def phase_three(zo, side):
        x_copy(zo).wait_recv()
        y_copy(zo).wait_recv()
        add(zo, 0, lambda i: X[zo, i].astype(f32) + Y[zo, i].astype(f32))
        if isinstance(side, int) and side == 0:
            return
        if side == -1:
            @pl.when(net.has_dn)
            def _():
                z_copy(zo, 0).wait_recv()
                add(zo, 0, lambda i: Z[zo, 0, i].astype(f32))

            z_copy(zo, 0).start()
        else:
            @pl.when(net.has_up)
            def _():
                z_copy(zo, 1).wait_recv()
                add(zo, 0, lambda i: Z[zo, 1, i].astype(f32))

            z_copy(zo, 1).start()

    la[0] = local_ref[...]
    sa[0] = shared_ref[...]
    v_start(0)
    for step in range(nz - 1, -1, -1):
        each(step, begin)
    dx_copy.start()
    for turn_no in range(nz + 2):
        if turn_no < nz:
            each(nz - 1 - turn_no, phase_one)
        if 0 <= turn_no - 1 < nz:
            each(nz - turn_no, phase_two)
        if 0 <= turn_no - 2:
            each(nz + 1 - turn_no, phase_three)
        if turn_no < 5:
            v_finish(turn_no)
            if turn_no < 4:
                v_start(turn_no + 1)
    local_o[...] = la[5]
    shared_o[...] = sa[5]
    dx_copy.wait_recv()

    def join(r, _):
        at = pl.ds(pl.multiple_of(r * 128, 128), 128)
        dx_o[at, :] = own_ref[at, :] + dx_in[at, :].astype(f32)
        return 0

    lax.fori_loop(0, own_ref.shape[0] // 128, join, 0)

    @pl.when(net.has_dn)
    def _():
        z_copy(z, 0).wait_recv()

    @pl.when(net.has_up)
    def _():
        z_copy(z, 1).wait_recv()

    def finish(q, _):
        blocks = []
        for k in range(3):
            at = 3 * q + k
            total = A[z, 0, at].astype(f32)
            total = total + jnp.where(net.has_dn, Z[z, 0, at].astype(f32), 0.0)
            total = total + jnp.where(net.has_up, Z[z, 1, at].astype(f32), 0.0)
            tile_o[4 * q + k] = total
            blocks.append(total)
        tile_o[4 * q + 3] = fourth_of(blocks)
        return 0

    lax.fori_loop(0, 6, finish, 0)

    def sent(zo, side):
        for kind in range(4):
            c_copy(zo, kind).wait_send()
        xd_copy(zo).wait_send()
        yd_copy(zo).wait_send()
        x_copy(zo).wait_send()
        y_copy(zo).wait_send()
        if isinstance(side, int) and side == 0:
            return
        z_copy(zo, 0).wait_send()

    for step in range(nz):
        each(step, sent)
    dx_copy.wait_send()
    for k in range(5):
        for copy in v_copies(k):
            copy.wait_send()


def scatter_grads(nz, wire, own, other, local, shared):
    dma = pltpu.SemaphoreType.DMA
    vm = pl.BlockSpec(memory_space=pltpu.VMEM)
    block = lambda *lead: pltpu.VMEM((*lead, 96, 128), bf16)
    return pl.pallas_call(
        functools.partial(scatter_kernel, nz),
        out_shape=[
            jax.ShapeDtypeStruct((24, 96, 128), f32),
            jax.ShapeDtypeStruct(own.shape, f32),
            jax.ShapeDtypeStruct(local.shape, f32),
            jax.ShapeDtypeStruct(shared.shape, f32),
        ],
        in_specs=[pl.BlockSpec(memory_space=pl.ANY), vm, vm, vm, vm],
        out_specs=[vm] * 4,
        scratch_shapes=[
            block(nz, 4, 18), block(nz, 4, 18), block(nz, 9), block(nz, 9), block(nz, 18), block(nz, 18),
            block(nz, 2, 18), pltpu.VMEM(other.shape, bf16),
            pltpu.VMEM((6, *local.shape), f32), pltpu.VMEM((5, *local.shape), f32),
            pltpu.VMEM((6, *shared.shape), f32), pltpu.VMEM((5, *shared.shape), f32),
            dma((nz, 4)), dma((nz, 4)), dma((nz, 4)),
        ]
        + [dma((nz,))] * 9
        + [dma((nz, 2)), dma((2,)), dma((5, 2)), dma((5, 2))],
        compiler_params=pltpu.CompilerParams(
            collective_id=1, has_side_effects=True, vmem_limit_bytes=56 << 20
        ),
        name="scatter_grads",
    )(wire, own, other, local, shared)


STEP = 5
BETA_ONE = 0.5
BETA_TWO = 0.5
ADAM_EPS = 1e-08
RATE_TILES = 0.04
RATE_VECTORS = 0.2
DECAY = 0.01
HIGH = lax.Precision.HIGHEST


def adam(grad, first, second):
    first_new = BETA_ONE * first + (1.0 - BETA_ONE) * grad
    second_new = BETA_TWO * second + (1.0 - BETA_TWO) * grad * grad
    step_dir = (
        first_new
        / (1.0 - BETA_ONE**STEP)
        / (jnp.sqrt(second_new / (1.0 - BETA_TWO**STEP)) + ADAM_EPS)
    )
    return (first_new, second_new, step_dir)


def from_tiles(tile_set, row_count, col_count):
    edge = tile_set.shape[-1]
    return (
        tile_set.reshape(row_count // edge, col_count // edge, edge, edge)
        .transpose(0, 2, 1, 3)
        .reshape(row_count, col_count)
    )


def plain_weights(tile_order, master, local):
    tiles = lax.all_gather(master.astype(bf16), "dp", axis=0, tiled=True)
    tiles = lax.all_gather(tiles, "mp", axis=0)
    count = tile_order.shape[0]
    inverse = jnp.zeros((count,), jnp.int32).at[tile_order].set(jnp.arange(count, dtype=jnp.int32))
    natural = tiles[:, inverse]
    dense = []
    for rows, cols, where in GRIDS:
        pieces = []
        for r in range(rows):
            pick = [where(r, j) for j in range(cols)]
            groups = jnp.asarray([p for p, _ in pick], jnp.int32)
            numbers = jnp.asarray([n for _, n in pick], jnp.int32)
            pieces.append(natural[groups, numbers].transpose(1, 0, 2).reshape(96, cols * 96))
        dense.append(jnp.concatenate(pieces, 0))
    return (*dense, lax.all_gather(local, "mp", axis=0))


def plain_scatter(order, tq, to, tu, td, own, other, local, shared):
    tiles = jnp.concatenate([tq, to, tu, td], 1)[:, order, :, :96].astype(f32)
    mine = lax.psum_scatter(tiles, "mp", scatter_dimension=0, tiled=False)
    owned = lax.psum_scatter(mine, "dp", scatter_dimension=0, tiled=True)
    count = lax.axis_size("mp")
    swapped = lax.ppermute(other, "mp", [(i, i ^ 1) for i in range(count)])
    local_sum, shared_sum = lax.psum((local, shared), ("dp", "mp"))
    return owned, own + swapped.astype(f32), local_sum, shared_sum


def shards(
    tokens,
    cotangent,
    lengths,
    tile_order,
    master,
    first_moment,
    second_moment,
    basis_left,
    basis_right,
    local_vec,
    local_first,
    local_second,
    shared_vec,
    shared_first,
    shared_second,
):
    group_count = lax.axis_size("mp")
    group_index = lax.axis_index("mp")
    owners = lax.axis_size("dp")
    row_total, width = tokens.shape
    seq_len = row_total // lengths.shape[0]
    rows = row_total // group_count
    per_owner = master.shape[1]
    nz = owners // 2
    routed = per_owner == 24 and nz == 4 and group_count == 4

    seq = group_index * rows // seq_len
    part = group_index * rows % seq_len // rows
    length = lax.dynamic_index_in_dim(lengths, seq, 0, keepdims=False)
    info = jnp.stack([seq, part, length, group_index]).astype(jnp.int32)

    if routed:
        w_qkv, w_out, w_up, w_down, vectors = gather_weights(
            nz, slot_sources(tile_order, per_owner), master[0], local_vec
        )
    else:
        w_qkv, w_out, w_up, w_down, vectors = plain_weights(tile_order, master[0], local_vec)
    vectors = vectors[:, 0]
    attn = width // group_count
    bias_q = vectors[:, :attn].reshape(1, width)
    bias_v = vectors[:, attn : 2 * attn].reshape(1, width)
    bias_qkv = jnp.concatenate([bias_q, jnp.zeros_like(bias_q), bias_v], 1)
    bias_up = vectors[:, 2 * attn :].reshape(1, -1)

    q, k, v, probs, o_t = attend(info, tokens, w_qkv, bias_qkv, seq_len, rows)
    output, tu, td, to, g_o, g_z, d_up, shared_terms = middle(
        info, o_t, w_out, tokens, cotangent, shared_vec, w_up, w_down, bias_up, rows
    )
    tq, own, other, d_bias = attend_back(info, g_o, q, k, v, probs, o_t, tokens, w_qkv, g_z)
    local_terms = jnp.concatenate(
        [d_bias.reshape(2, group_count, attn)[0], d_bias.reshape(2, group_count, attn)[1],
         d_up.reshape(group_count, -1)], 1
    )
    to = to.reshape(4, 16, 96, 128)
    tu = tu.reshape(4, 64, 96, 128)
    td = td.reshape(4, 64, 96, 128)
    if routed:
        owned, input_grad, local_sum, shared_grad = scatter_grads(
            nz, pack(tile_order, tq, to, tu, td), own, other, local_terms, shared_terms
        )
        owned = owned[:, :, :96]
    else:
        owned, input_grad, local_sum, shared_grad = plain_scatter(
            tile_order, tq, to, tu, td, own, other, local_terms, shared_terms
        )
    local_grad = lax.dynamic_slice_in_dim(local_sum, group_index, 1, 0)
    left_basis = basis_left[0]
    right_basis = basis_right[0]
    rotated = jnp.einsum("ski,skl->sil", left_basis, owned, precision=HIGH)
    rotated = jnp.einsum("sil,slj->sij", rotated, right_basis, precision=HIGH)
    tile_first, tile_second, direction = adam(rotated, first_moment[0], second_moment[0])
    turned = jnp.einsum("sik,skl->sil", left_basis, direction, precision=HIGH)
    turned = jnp.einsum("sil,sjl->sij", turned, right_basis, precision=HIGH)
    tile_weight = master[0] - RATE_TILES * (turned + DECAY * master[0])
    local_first_new, local_second_new, local_dir = adam(local_grad, local_first, local_second)
    shared_first_new, shared_second_new, shared_dir = adam(shared_grad, shared_first, shared_second)
    return (
        output,
        input_grad,
        owned[None],
        tile_first[None],
        tile_second[None],
        tile_weight[None],
        local_grad,
        local_first_new,
        local_second_new,
        local_vec - RATE_VECTORS * local_dir,
        shared_grad,
        shared_first_new,
        shared_second_new,
        shared_vec - RATE_VECTORS * shared_dir,
    )


def solution(mesh):
    placed = (
        P("dp", None),
        P("dp", None),
        P("dp"),
        P(),
        P("mp", "dp", None, None),
        P("mp", "dp", None, None),
        P("mp", "dp", None, None),
        P("mp", "dp", None, None),
        P("mp", "dp", None, None),
        P("mp", None),
        P("mp", None),
        P("mp", None),
        P(),
        P(),
        P(),
    )
    return jax.shard_map(
        shards,
        mesh=mesh,
        in_specs=placed,
        out_specs=(
            P(("dp", "mp"), None),
            P(("dp", "mp"), None),
            P("mp", "dp", None, None),
            P("mp", "dp", None, None),
            P("mp", "dp", None, None),
            P("mp", "dp", None, None),
            P("mp", None),
            P("mp", None),
            P("mp", None),
            P("mp", None),
            P(),
            P(),
            P(),
            P(),
        ),
        check_vma=False,
    )
```

```python
import functools
import jax
import jax.numpy as jnp
from jax import lax
from jax.experimental import pallas as pl
from jax.experimental.pallas import tpu as pltpu
from jax.sharding import PartitionSpec as P

MESH = pl.DeviceIdType.MESH
f32 = jnp.float32
bf16 = jnp.bfloat16


def lanes_of(shape):
    return lax.broadcasted_iota(jnp.int32, shape, len(shape) - 1)


def turn(v, amount):
    return pltpu.roll(v, amount, v.ndim - 1)


def free_of(j):
    return (3 * j + 3) % 4


def part_of(group, number):
    return jnp.where(number < 48, 2 * group + number % 2, number) % 4


def groups_of(shape):
    return lanes_of(shape) // 32


def to_wire(tile, free):
    rest = tile[72:96]
    side = jnp.concatenate([turn(rest, 96), turn(rest, 64), turn(rest, 32)], 0)
    return jnp.where(groups_of(side.shape) == free, side, tile[:72])


def rest_of(wire, free):
    group = groups_of((24, 128))
    first, second, third = turn(wire[:24], 32), turn(wire[24:48], 64), turn(wire[48:72], 96)
    return jnp.where(
        group == (free + 1) % 4, first, jnp.where(group == (free + 2) % 4, second, third)
    )


def turned(tile, j, sign):
    out = tile
    for k in range(1, 4):
        out = jnp.where(j == k, turn(tile, sign * 96 * k % 128), out)
    return out


def join_four(tiles):
    lane = lanes_of(tiles[0].shape)
    a, b, c, d = tiles
    return [jnp.where(lane < 96, a, b), jnp.where(lane < 64, b, c), jnp.where(lane < 32, c, d)]


def split_four(pieces):
    lane = lanes_of(pieces[0].shape)
    a, b, c = pieces
    return [a, jnp.where(lane < 64, b, a), jnp.where(lane < 32, c, b), c]


def place():
    d, m = lax.axis_index("dp"), lax.axis_index("mp")
    return d // 2, d % 2, m // 2, m % 2


class Net:
    def __init__(self, nz):
        self.nz = nz
        self.z, self.x, self.y, self.c = place()
        self.d = self.z * 2 + self.x
        self.m = self.y * 2 + self.c
        self.xn = (self.z * 2 + 1 - self.x, self.m)
        self.yn = (self.d, (1 - self.y) * 2 + self.c)
        self.cn = (self.d, self.y * 2 + 1 - self.c)
        self.up = (self.d + 2, self.m)
        self.dn = (self.d - 2, self.m)
        self.has_up = self.z < nz - 1
        self.has_dn = self.z > 0

    def enter(self):
        bar = pltpu.get_barrier_semaphore()
        others = [(lax.rem(self.z + k, self.nz) * 2 + self.x, self.m) for k in range(1, self.nz)]
        peers = [self.xn, self.yn, self.cn] + others
        for peer in peers:
            pl.semaphore_signal(bar, inc=1, device_id=peer, device_id_type=MESH)
        pl.semaphore_wait(bar, len(peers))


def send(src, dst, ss, rs, peer):
    return pltpu.make_async_remote_copy(
        src_ref=src, dst_ref=dst, send_sem=ss, recv_sem=rs, device_id=peer, device_id_type=MESH
    )


def tile_qkv(r, j):
    return (j % 8) // 2, r * 6 + (j // 8) * 2 + j % 2


def tile_out(r, j):
    return r // 2, 48 + (r % 2) * 8 + j


def tile_up(r, j):
    return j // 8, 64 + r * 8 + j % 8


def tile_down(r, j):
    return r // 8, 128 + (r % 8) * 8 + j


GRIDS = ((8, 24, tile_qkv), (8, 8, tile_out), (8, 32, tile_up), (32, 8, tile_down))


def gather_kernel(
    nz, order_ref, src_ref, master_ref, local_ref, o_qkv, o_out, o_up, o_down, o_local,
    G, H, LV, d_qkv, d_out, d_up, d_down,
    zs, zr, xs, xr, ys, yr, xds, xdr, yds, ydr, cs, cr, outs, lvs, lvr,
):
    net = Net(nz)
    z, x, y, c, m = net.z, net.x, net.y, net.c, net.m
    my = (1 - y) * 2 + c
    net.enter()
    full = 24
    half = 12
    LV[m] = local_ref[...]
    lv_y = send(LV.at[m], LV.at[m], lvs.at[0], lvr.at[0], net.yn)
    lv_c = send(LV.at[m], LV.at[m], lvs.at[1], lvr.at[1], net.cn)
    lv_d = send(LV.at[my], LV.at[my], lvs.at[2], lvr.at[2], net.cn)
    lv_y.start()
    lv_c.start()

    def slot(mo, zo, xo, lo=0, n=full):
        return G.at[mo, pl.ds((zo * 2 + xo) * full + lo, n)]

    def stage(i, _):
        tile = jnp.concatenate([master_ref[i], jnp.zeros((96, 32), f32)], axis=-1)
        j = part_of(m, order_ref[net.d * full + i])
        tile = turned(tile, j, 1)
        G[m, net.d * full + i] = to_wire(tile, free_of(j)).astype(bf16)
        H[m, net.d * full + i] = tile[72:96].astype(bf16)
        return 0

    lax.fori_loop(0, full, stage, 0)

    def unwrap(mo, zo, xo):
        base = (zo * 2 + xo) * full

        def body(i, _):
            for k in range(4):
                at = base + 4 * i + k
                free = free_of(part_of(mo, order_ref[at]))
                H[mo, at] = rest_of(G[mo, at].astype(f32), free).astype(bf16)
            return 0

        lax.fori_loop(0, full // 4, body, 0)

    def z_copy(zo, direction):
        s = slot(m, zo, x)
        peer = net.up if direction == 0 else net.dn
        return send(s, s, zs.at[zo, direction], zr.at[zo], peer)

    def c_copy(zo, kind):
        mo = (m, m, my, my)[kind]
        xo = (x, 1 - x, x, 1 - x)[kind]
        s = slot(mo, zo, xo)
        return send(s, s, cs.at[zo, kind], cr.at[zo, kind], net.cn)

    def c_arrival(zo, kind):
        mo = (m, m, my, my)[kind] + 1 - 2 * c
        xo = (x, 1 - x, x, 1 - x)[kind]
        s = slot(mo, zo, xo)
        return send(s, s, cs.at[zo, kind], cr.at[zo, kind], net.cn)

    def x_copy(zo, xo):
        s = slot(m, zo, xo)
        return send(s, s, xs.at[zo], xr.at[zo], net.xn)

    def y_copy(zo, mo):
        s = slot(mo, zo, x)
        return send(s, s, ys.at[zo], yr.at[zo], net.yn)

    def xd_copy(zo, xo):
        s = slot(my, zo, xo, 0, half)
        return send(s, s, xds.at[zo], xdr.at[zo], net.xn)

    def yd_copy(zo, mo):
        s = slot(mo, zo, 1 - x, half, half)
        return send(s, s, yds.at[zo], ydr.at[zo], net.yn)

    def fan(zo):
        x_copy(zo, x).start()
        y_copy(zo, m).start()
        c_copy(zo, 0).start()

    def diag(zo):
        x_copy(zo, 1 - x).wait_recv()
        yd_copy(zo, m).start()
        c_copy(zo, 1).start()
        y_copy(zo, my).wait_recv()
        xd_copy(zo, x).start()
        c_copy(zo, 2).start()

    def fin(zo):
        xd_copy(zo, 1 - x).wait_recv()
        yd_copy(zo, my).wait_recv()
        c_copy(zo, 3).start()

    def each(step, fn):
        if step == 0:
            fn(z, 0)
            return

        @pl.when(z >= step)
        def _():
            fn(z - step, 1)

        @pl.when(z + step < nz)
        def _():
            fn(z + step, -1)

    def arrive(zo, side):
        if isinstance(side, int) and side == 0:
            @pl.when(net.has_up)
            def _():
                z_copy(zo, 0).start()

            @pl.when(net.has_dn)
            def _():
                z_copy(zo, 1).start()
        elif side == 1:
            z_copy(zo, 0).wait_recv()

            @pl.when(net.has_up)
            def _():
                z_copy(zo, 0).start()
        else:
            z_copy(zo, 1).wait_recv()

            @pl.when(net.has_dn)
            def _():
                z_copy(zo, 1).start()
        fan(zo)

    def open_some(zo, side):
        if not (isinstance(side, int) and side == 0):
            unwrap(m, zo, x)
        unwrap(m, zo, 1 - x)
        unwrap(my, zo, x)
        for kind in range(3):
            c_arrival(zo, kind).wait_recv()
            mo, xo = ((m, x), (m, 1 - x), (my, x))[kind]
            unwrap(mo + 1 - 2 * c, zo, xo)

    def open_last(zo, side):
        unwrap(my, zo, 1 - x)
        c_arrival(zo, 3).wait_recv()
        unwrap(my + 1 - 2 * c, zo, 1 - x)

    for step in range(nz + 2):
        if step < nz:
            each(step, arrive)
        if 0 <= step - 1 < nz:
            each(step - 1, lambda zo, side: diag(zo))
        if 0 <= step - 2:
            each(step - 2, lambda zo, side: fin(zo))
        if 0 <= step - 1 < nz:
            each(step - 1, open_some)
        if 0 <= step - 2:
            each(step - 2, open_last)
    send(LV.at[my], LV.at[my], lvs.at[0], lvr.at[0], net.yn).wait_recv()
    lv_d.start()
    mc = m + 1 - 2 * c
    send(LV.at[mc], LV.at[mc], lvs.at[1], lvr.at[1], net.cn).wait_recv()
    mc = my + 1 - 2 * c
    send(LV.at[mc], LV.at[mc], lvs.at[2], lvr.at[2], net.cn).wait_recv()
    o_local[...] = LV[...]
    lv_y.wait_send()
    lv_c.wait_send()
    lv_d.wait_send()
    def sent(zo, side):
        x_copy(zo, x).wait_send()
        y_copy(zo, m).wait_send()
        yd_copy(zo, m).wait_send()
        xd_copy(zo, x).wait_send()
        for kind in range(4):
            c_copy(zo, kind).wait_send()
        if side == 0 or side == 1:
            @pl.when(net.has_up)
            def _():
                z_copy(zo, 0).wait_send()
        if side == 0 or side == -1:
            @pl.when(net.has_dn)
            def _():
                z_copy(zo, 1).wait_send()

    for step in range(nz):
        each(step, sent)

    copies = []
    for i, ((rows, cols, where), dense, out) in enumerate(
        zip(GRIDS, (d_qkv, d_out, d_up, d_down), (o_qkv, o_out, o_up, o_down))
    ):
        def fill(r, _):
            for g in range(cols // 4):
                tiles = []
                for t in range(4):
                    p, n = where(r, 4 * g + t)
                    at = src_ref[n]
                    tiles.append(
                        jnp.concatenate([G[p, at].astype(f32), H[p, at].astype(f32)], 0)
                    )
                for k, piece in enumerate(join_four(tiles)):
                    dense[pl.ds(pl.multiple_of(r * 96, 96), 96), pl.ds(384 * g + 128 * k, 128)] = (
                        piece.astype(bf16)
                    )
            return 0

        lax.fori_loop(0, rows, fill, 0)
        copy = pltpu.make_async_copy(dense, out, outs.at[i])
        copy.start()
        copies.append(copy)
    for copy in copies:
        copy.wait()


def gather_weights(nz, order, src, master, local):
    dma = pltpu.SemaphoreType.DMA
    shapes = [(r * 96, c * 96) for r, c, _ in GRIDS]
    return pl.pallas_call(
        functools.partial(gather_kernel, nz),
        out_shape=[jax.ShapeDtypeStruct(s, bf16) for s in shapes]
        + [jax.ShapeDtypeStruct((4, *local.shape), f32)],
        in_specs=[pl.BlockSpec(memory_space=pltpu.SMEM)] * 2
        + [pl.BlockSpec(memory_space=pltpu.VMEM)] * 2,
        out_specs=[pl.BlockSpec(memory_space=pl.ANY)] * 4 + [pl.BlockSpec(memory_space=pltpu.VMEM)],
        scratch_shapes=[pltpu.VMEM((4, 2 * nz * 24, 72, 128), bf16), pltpu.VMEM((4, 2 * nz * 24, 24, 128), bf16),
            pltpu.VMEM((4, *local.shape), f32)]
        + [pltpu.VMEM(s, bf16) for s in shapes]
        + [dma((nz, 2)), dma((nz,))]
        + [dma((nz,))] * 8
        + [dma((nz, 4)), dma((nz, 4)), dma((4,)), dma((3,)), dma((3,))],
        compiler_params=pltpu.CompilerParams(
            collective_id=0, has_side_effects=True, vmem_limit_bytes=56 << 20
        ),
        name="gather_weights",
    )(order, src, master, local)


def slot_of_tile(tile_order):
    count = tile_order.shape[0]
    slots = jnp.arange(count, dtype=jnp.int32)
    return jnp.sum(jnp.where(tile_order[None, :] == slots[:, None], slots[None, :], 0), 1)


NEG_BIG = -1e30
NORM_EPS = 1e-05
ROOT_HALF = 0.7071067811865476
PHI_SCALE = 0.3989422804014327


def nt(a, b):
    return lax.dot_general(a, b, (((1,), (1,)), ((), ())), preferred_element_type=f32)


def tn(a, b):
    return lax.dot_general(a, b, (((0,), (0,)), ((), ())), preferred_element_type=f32)


def nn(a, b):
    return jnp.dot(a, b, preferred_element_type=f32)


def standard(values):
    centre = values - jnp.mean(values, -1, keepdims=True)
    scale = lax.rsqrt(jnp.mean(centre * centre, -1, keepdims=True) + NORM_EPS)
    return centre * scale, scale


def standard_back(grad, normed, scale, gain):
    inner = grad * gain
    return scale * (
        inner - jnp.mean(inner, -1, keepdims=True) - normed * jnp.mean(inner * normed, -1, keepdims=True)
    )


def col_sum(values):
    return jnp.sum(values, 0, keepdims=True)


def layer_kernel(
    tokens_ref, cot_ref, lengths_ref, vec_ref, sv_ref, wq_ref, wo_ref, wu_ref, wd_ref,
    out_ref, tq_ref, to_ref, tu_ref, td_ref, own_ref, other_ref, dl_ref, ds_ref,
    x, cot, wqkv, wout, wup, wdown, bias, q, k, v, probs, o_t, hid, low, low_t, n_one, r_one, acc,
    act, slope, g_low, g_o, dq, dk, dv, out, other, su, sd, so, sq, loads, stores, su_sem, sd_sem, sq_sem,
):
    rows, width = q.shape
    seq_len = k.shape[0]
    chunks, _, cut = act.shape
    tiles = width // 96
    pairs = width // 128
    piece = 128
    zero = jnp.zeros((), bf16)
    member = lax.axis_index("mp")
    share = seq_len // rows
    seq, part = member // share, member % share
    length = lengths_ref[seq]
    bound = 64 * ((length + 127) // 128)
    start_b = pl.multiple_of(bound, 64)
    here = pl.ds(pl.multiple_of(part * rows, rows), rows)
    there = pl.ds(pl.multiple_of((1 - part) * rows, rows), rows)

    def load(src, dst, i):
        copy = pltpu.make_async_copy(src, dst, loads.at[i])
        copy.start()
        return copy

    get_x = load(tokens_ref.at[pl.ds(pl.multiple_of(seq * seq_len, seq_len), seq_len)], x, 0)
    get_q = load(wq_ref, wqkv, 1)
    get_o = load(wo_ref, wout, 2)
    get_u = load(wu_ref, wup, 3)
    get_d = load(wd_ref, wdown, 4)
    get_c = load(cot_ref.at[pl.ds(pl.multiple_of(member * rows, rows), rows)], cot, 5)

    groups = vec_ref.shape[0]
    third = width // groups
    bias[:, :width] = jnp.concatenate([vec_ref[p][:, :third] for p in range(groups)], 1)
    bias[:, width:] = jnp.concatenate([vec_ref[p][:, third : 2 * third] for p in range(groups)], 1)

    get_x.wait()
    get_q.wait()
    for lo in range(0, width, 256):
        got = nn(x[here, :], wqkv[:, lo : lo + 256]) + bias[:, lo : lo + 256]
        q[:, lo : lo + 256] = got.astype(bf16) * jnp.asarray(0.125, bf16)

    def project(r, _):
        at = pl.ds(pl.multiple_of(r * rows, rows), rows)
        for lo in range(0, width, 256):
            k[at, lo : lo + 256] = nn(x[at, :], wqkv[:, width + lo : width + lo + 256]).astype(bf16)
            got = nn(x[at, :], wqkv[:, 2 * width + lo : 2 * width + lo + 256])
            v[at, lo : lo + 256] = (got + bias[:, width + lo : width + lo + 256]).astype(bf16)
        return 0

    lax.fori_loop(0, share, project, 0)

    def picks(shape, rows_at):
        row = lax.broadcasted_iota(jnp.int32, shape, rows_at) + part * rows
        lane = lax.broadcasted_iota(jnp.int32, shape, 1 - rows_at)
        return (row < bound) == (lane < 64)

    windows = ((0, bound), (start_b, length - bound))

    def forward(pair, _):
        cols = pl.ds(pl.multiple_of(pair * 128, 128), 128)
        queries = q[:, cols]
        pick = picks((rows, 128), 0)
        outs = []
        for w, (start, limit) in enumerate(windows):
            these = jnp.where(pick, queries, zero) if w == 0 else jnp.where(pick, zero, queries)
            scores = nt(k[pl.ds(start, rows), cols], these)
            inside = lax.broadcasted_iota(jnp.int32, scores.shape, 0) < limit
            scores = jnp.where(inside, scores, NEG_BIG)
            weight = jnp.exp(scores - jnp.max(scores, 0, keepdims=True))
            low_probs = (weight * (1.0 / jnp.sum(weight, 0, keepdims=True))).astype(bf16)
            probs[2 * pair + w] = low_probs
            outs.append(tn(v[pl.ds(start, rows), cols], low_probs))
        o_t[cols, :] = jnp.where(picks((128, rows), 1), outs[0], outs[1]).astype(bf16)
        return 0

    lax.fori_loop(0, pairs, forward, 0)

    def by_rows(fn):
        def body(r, _):
            fn(pl.ds(pl.multiple_of(r * piece, piece), piece), r)
            return 0

        lax.fori_loop(0, rows // piece, body, 0)

    get_o.wait()
    acc[...] = tn(o_t[...], wout[...])

    def norm_one(at, r):
        mine = pl.ds(pl.multiple_of(part * rows + r * piece, piece), piece)
        z_one = x[mine, :].astype(f32) + acc[at, :] + sv_ref[0:1, :]
        normed, scale = standard(z_one)
        hidden = normed * sv_ref[2:3, :] + sv_ref[3:4, :]
        n_one[at, :] = normed
        r_one[at, :] = jnp.broadcast_to(scale, (piece, 128))
        hid[at, :] = hidden
        low[at, :] = hidden.astype(bf16)
        acc[at, :] = jnp.zeros((piece, width), f32)

    by_rows(norm_one)
    low_t[...] = low[...].T
    get_u.wait()
    get_d.wait()

    def feed(i, _):
        at = pl.ds(pl.multiple_of(i * cut, cut), cut)
        half = chunks // groups
        shift = pl.multiple_of(2 * third + (i % half) * cut, 128)
        pre = nn(low[...], wup[:, at]) + vec_ref[i // half, :, pl.ds(shift, cut)]
        phi = 0.5 * (1.0 + lax.erf(pre * ROOT_HALF))
        density = jnp.exp(-0.5 * pre * pre) * PHI_SCALE
        active = (pre * phi).astype(bf16)
        act[i] = active
        slope[i] = (phi + pre * density).astype(bf16)
        acc[...] += nn(active, wdown[at, :])
        return 0

    lax.fori_loop(0, chunks, feed, 0)
    get_c.wait()
    ds_ref[...] = jnp.zeros_like(ds_ref)

    def norm_two(at, r):
        z_two = hid[at, :] + acc[at, :] + sv_ref[1:2, :]
        normed, scale = standard(z_two)
        row = lax.broadcasted_iota(jnp.int32, (piece, 1), 0) + part * rows + r * piece
        valid = (row < length).astype(f32)
        out[at, :] = ((normed * sv_ref[4:5, :] + sv_ref[5:6, :]) * valid).astype(bf16)
        grad = cot[at, :].astype(f32) * valid
        back = standard_back(grad, normed, scale, sv_ref[4:5, :])
        ds_ref[4:5, :] += col_sum(grad * normed)
        ds_ref[5:6, :] += col_sum(grad)
        ds_ref[1:2, :] += col_sum(back)
        g_low[at, :] = back.astype(bf16)
        acc[at, :] = back

    by_rows(norm_two)
    put_out = pltpu.make_async_copy(out, out_ref, stores.at[0])
    put_out.start()

    def put_u(i):
        half = chunks // groups
        return pltpu.make_async_copy(su.at[i % 2], tu_ref.at[i // half, :, i % half], su_sem.at[i % 2])

    def put_d(i):
        half = chunks // groups
        return pltpu.make_async_copy(sd.at[i % 2], td_ref.at[i // half, i % half], sd_sem.at[i % 2])

    def cuts(full, r):
        return split_four(
            [full[96 * r : 96 * r + 96, 128 * n : 128 * n + 128].astype(bf16) for n in range(3)]
        )

    def feed_back(i, _):
        at = pl.ds(pl.multiple_of(i * cut, cut), cut)

        @pl.when(i >= 2)
        def _():
            put_u(i - 2).wait()
            put_d(i - 2).wait()

        half = chunks // groups
        shift = pl.multiple_of(2 * third + (i % half) * cut, 128)
        grad_low = (nt(g_low[...], wdown[at, :]) * slope[i].astype(f32)).astype(bf16)
        dl_ref[i // half, :, pl.ds(shift, cut)] = col_sum(grad_low.astype(f32))
        acc[...] += nt(grad_low, wup[:, at])
        for g in range(width // 384):
            down = tn(act[i], g_low[:, 384 * g : 384 * g + 384])
            for r in range(4):
                for t, tile in enumerate(cuts(down, r)):
                    sd[i % 2, r * tiles + 4 * g + t] = tile
        up = nn(low_t[...], grad_low)
        for r in range(tiles):
            for t, tile in enumerate(cuts(up, r)):
                su[i % 2, r, t] = tile
        put_u(i).start()
        put_d(i).start()
        return 0

    lax.fori_loop(0, chunks, feed_back, 0)

    def norm_back(at, r):
        grad = acc[at, :]
        normed = n_one[at, :]
        back = standard_back(grad, normed, r_one[at, 0:1], sv_ref[2:3, :])
        ds_ref[2:3, :] += col_sum(grad * normed)
        ds_ref[3:4, :] += col_sum(grad)
        ds_ref[0:1, :] += col_sum(back)
        acc[at, :] = back
        g_low[at, :] = back.astype(bf16)

    by_rows(norm_back)
    g_o[...] = nt(g_low[...], wout[...]).astype(bf16)
    for g in range(width // 384):
        outer = nn(o_t[...], g_low[:, 384 * g : 384 * g + 384])
        for r in range(tiles):
            for t, tile in enumerate(cuts(outer, r)):
                so[r, 4 * g + t] = tile
    put_o = pltpu.make_async_copy(so, to_ref, stores.at[1])
    put_o.start()
    dk[...] = jnp.zeros_like(dk)
    dv[...] = jnp.zeros_like(dv)

    def backward(pair, _):
        cols = pl.ds(pl.multiple_of(pair * 128, 128), 128)
        pick, pick_t = picks((rows, 128), 0), picks((128, rows), 1)
        queries, grads = q[:, cols], g_o[:, cols]
        grads_t = grads.astype(f32).T
        inner = grads_t * o_t[cols, :].astype(f32)
        outs = []
        for w, (start, _) in enumerate(windows):
            at = pl.ds(start, rows)
            mine = (lambda a: jnp.where(pick, a, zero)) if w == 0 else (lambda a: jnp.where(pick, zero, a))
            mine_t = (lambda a: jnp.where(pick_t, a, 0.0)) if w == 0 else (lambda a: jnp.where(pick_t, 0.0, a))
            dot_sum = jnp.sum(mine_t(inner), 0, keepdims=True)
            grad_probs = nn(v[at, cols], mine_t(grads_t).astype(bf16))
            these = probs[2 * pair + w]
            grad_scores = (these.astype(f32) * (grad_probs - dot_sum)).astype(bf16)
            dv[at, cols] = nn(these, mine(grads)).astype(bf16)
            dk[at, cols] = nn(grad_scores, mine(queries)).astype(bf16)
            outs.append(tn(k[at, cols], grad_scores))
        dq[:, cols] = (jnp.where(pick_t, outs[0], outs[1]) * 0.125).T.astype(bf16)
        return 0

    lax.fori_loop(0, pairs, backward, 0)

    other[...] = (
        nt(dk[there, :], wqkv[:, width : 2 * width]) + nt(dv[there, :], wqkv[:, 2 * width :])
    ).astype(bf16)
    put_x = pltpu.make_async_copy(other, other_ref, stores.at[2])
    put_x.start()
    hid[...] = (
        acc[...]
        + nt(dq[...], wqkv[:, :width])
        + nt(dk[here, :], wqkv[:, width : 2 * width])
        + nt(dv[here, :], wqkv[:, 2 * width :])
    )
    put_own = pltpu.make_async_copy(hid, own_ref, stores.at[3])
    put_own.start()
    sum_q = col_sum(dq[...].astype(f32))
    sum_v = col_sum(dv[...].astype(f32))
    for p in range(groups):
        dl_ref[p, :, :third] = sum_q[:, third * p : third * p + third]
        dl_ref[p, :, third : 2 * third] = sum_v[:, third * p : third * p + third]

    everyone = pl.ds(0, seq_len)
    puts = []
    for index, (grad, source) in enumerate(((dq, here), (dk, everyone), (dv, everyone))):
        for g in range(width // 384):
            outer = tn(x[source, :], grad[:, 384 * g : 384 * g + 384])
            count = index * (width // 384) + g
            if count >= 2:
                puts[count - 2].wait()
            for r in range(tiles):
                for t, tile in enumerate(cuts(outer, r)):
                    sq[count % 2, t // 2, r, t % 2] = tile
            put = pltpu.make_async_copy(
                sq.at[count % 2], tq_ref.at[pl.ds(2 * g, 2), :, index], sq_sem.at[count % 2]
            )
            put.start()
            puts.append(put)
    for i in (chunks - 2, chunks - 1):
        put_u(i).wait()
        put_d(i).wait()
    for put in (put_out, put_o, put_x, put_own, puts[-2], puts[-1]):
        put.wait()


def layer(tokens, cotangent, lengths, vectors, shared, w_qkv, w_out, w_up, w_down, rows):
    width = w_out.shape[0]
    hidden = w_up.shape[1]
    seq_len = tokens.shape[0] // lengths.shape[0]
    cut = 384
    chunks = hidden // cut
    groups = vectors.shape[0]
    half = chunks // groups
    tiles = width // 96
    anywhere = pl.BlockSpec(memory_space=pl.ANY)
    vm = pl.BlockSpec(memory_space=pltpu.VMEM)
    smem = pl.BlockSpec(memory_space=pltpu.SMEM)
    out = jax.ShapeDtypeStruct
    V = pltpu.VMEM
    dma = pltpu.SemaphoreType.DMA
    tall, wide, long = (rows, width), (width, rows), (seq_len, width)
    return pl.pallas_call(
        layer_kernel,
        in_specs=[anywhere, anywhere, smem, vm, vm] + [anywhere] * 4,
        out_specs=[anywhere] * 7 + [vm, vm],
        out_shape=[
            out(tall, bf16),
            out((groups, tiles, 3, 2, 96, 128), bf16),
            out((tiles, tiles, 96, 128), bf16),
            out((groups, tiles, half, 4, 96, 128), bf16),
            out((groups, half, 4 * tiles, 96, 128), bf16),
            out(tall, f32),
            out(tall, bf16),
            out(vectors.shape, f32),
            out(shared.shape, f32),
        ],
        scratch_shapes=[
            V(long, bf16), V(tall, bf16), V(w_qkv.shape, bf16), V(w_out.shape, bf16), V(w_up.shape, bf16),
            V(w_down.shape, bf16), V((1, 2 * width), f32), V(tall, bf16), V(long, bf16), V(long, bf16),
            V((width // 64, rows, rows), bf16), V(wide, bf16), V(tall, f32), V(tall, bf16), V(wide, bf16),
            V(tall, f32), V((rows, 128), f32), V(tall, f32), V((chunks, rows, cut), bf16),
            V((chunks, rows, cut), bf16), V(tall, bf16), V(tall, bf16), V(tall, bf16), V(long, bf16),
            V(long, bf16), V(tall, bf16), V(tall, bf16), V((2, tiles, 4, 96, 128), bf16),
            V((2, 4 * tiles, 96, 128), bf16), V((tiles, tiles, 96, 128), bf16),
            V((2, 2, tiles, 2, 96, 128), bf16), dma((6,)), dma((4,)), dma((2,)), dma((2,)), dma((2,)),
        ],
        compiler_params=pltpu.CompilerParams(vmem_limit_bytes=60 << 20),
        name="layer",
    )(tokens, cotangent, lengths, vectors, shared, w_qkv, w_out, w_up, w_down)


def scatter_kernel(
    nz, order_ref, tq_ref, to_ref, tu_ref, td_ref, own_ref, other_ref, local_ref, shared_ref,
    tile_o, dx_o, local_o, shared_o,
    T, S, A, R, XD, YD, X, Y, Z, dx_in, la, lb, sa, sb,
    tsem, cs, cr, xds, xdr, yds, ydr, xs, xr, ys, yr, zs, zr, dxs, vs, vr,
):
    net = Net(nz)
    z, x, y, c, m, d = net.z, net.x, net.y, net.c, net.m, net.d
    my = (1 - y) * 2 + c
    far = (lax.rem(z + 2, nz) * 2 + x, m)
    near = ((z + 1 - 2 * (z % 2)) * 2 + x, m)
    full, half = 24, 12
    low, high = pl.ds(0, half), pl.ds(half, half)
    loads = []
    first = 0
    for i, src in enumerate((tq_ref, to_ref, tu_ref, td_ref)):
        copy = pltpu.make_async_copy(src, T.at[:, pl.ds(first, src.shape[1])], tsem.at[i])
        copy.start()
        loads.append(copy)
        first += src.shape[1]
    net.enter()
    kinds = ((m, x), (m, 1 - x), (my, x), (my, 1 - x))
    flip = 1 - 2 * c

    def c_copy(zo, kind):
        return send(S.at[zo, kind], R.at[zo, kind], cs.at[zo, kind], cr.at[zo, kind], net.cn)

    def fill(ref, zo, kind, shift):
        mo, xo = kinds[kind]
        base = (zo * 2 + xo) * full

        def body(i, _):
            for j in range(4):
                number = order_ref[base + 4 * i + j]
                tile = T[mo + shift, number].astype(f32)
                ref[zo, kind, 4 * i + j] = to_wire(
                    tile, free_of(part_of(mo + shift, number))
                ).astype(bf16)
            return 0

        lax.fori_loop(0, full // 4, body, 0)

    def xd_copy(zo):
        return send(A.at[zo, 3, low], XD.at[zo], xds.at[zo], xdr.at[zo], net.xn)

    def yd_copy(zo):
        return send(A.at[zo, 3, high], YD.at[zo], yds.at[zo], ydr.at[zo], net.yn)

    def x_copy(zo):
        return send(A.at[zo, 1], X.at[zo], xs.at[zo], xr.at[zo], net.xn)

    def y_copy(zo):
        return send(A.at[zo, 2], Y.at[zo], ys.at[zo], yr.at[zo], net.yn)

    def z_copy(zo, direction):
        return send(
            A.at[zo, 0], Z.at[zo, direction], zs.at[zo], zr.at[zo, direction],
            net.up if direction == 0 else net.dn,
        )

    dx_copy = send(other_ref, dx_in, dxs.at[0], dxs.at[1], net.cn)
    peers = (net.cn, net.xn, net.yn, near, far)

    def v_copies(k):
        return (
            send(la.at[k], lb.at[k], vs.at[k, 0], vr.at[k, 0], peers[k]),
            send(sa.at[k], sb.at[k], vs.at[k, 1], vr.at[k, 1], peers[k]),
        )

    def v_start(k):
        for copy in v_copies(k):
            copy.start()

    def v_finish(k):
        for copy in v_copies(k):
            copy.wait_recv()
        la[k + 1] = la[k] + lb[k]
        sa[k + 1] = sa[k] + sb[k]

    def add(zo, kind, other, lo=0, n=24):
        def body(i, _):
            A[zo, kind, lo + i] = (A[zo, kind, lo + i].astype(f32) + other(i)).astype(bf16)
            return 0

        lax.fori_loop(0, n, body, 0)

    def each(step, fn):
        if step == 0:
            fn(z, 0)
            return

        @pl.when(z >= step)
        def _():
            fn(z - step, 1)

        @pl.when(z + step < nz)
        def _():
            fn(z + step, -1)

    def begin(zo, side):
        for kind in (3, 1, 2, 0):
            fill(S, zo, kind, flip)
            c_copy(zo, kind).start()

    def phase_one(zo, side):
        for kind in (3, 1, 2, 0):
            fill(A, zo, kind, 0)
            c_copy(zo, kind).wait_recv()
            add(zo, kind, lambda i: R[zo, kind, i].astype(f32))
            if kind == 3:
                xd_copy(zo).start()
                yd_copy(zo).start()

    def phase_two(zo, side):
        yd_copy(zo).wait_recv()
        add(zo, 1, lambda i: YD[zo, i].astype(f32), half, half)
        x_copy(zo).start()
        xd_copy(zo).wait_recv()
        add(zo, 2, lambda i: XD[zo, i].astype(f32), 0, half)
        y_copy(zo).start()

    def phase_three(zo, side):
        x_copy(zo).wait_recv()
        y_copy(zo).wait_recv()
        add(zo, 0, lambda i: X[zo, i].astype(f32) + Y[zo, i].astype(f32))
        if isinstance(side, int) and side == 0:
            return
        if side == -1:
            @pl.when(net.has_dn)
            def _():
                z_copy(zo, 0).wait_recv()
                add(zo, 0, lambda i: Z[zo, 0, i].astype(f32))

            z_copy(zo, 0).start()
        else:
            @pl.when(net.has_up)
            def _():
                z_copy(zo, 1).wait_recv()
                add(zo, 0, lambda i: Z[zo, 1, i].astype(f32))

            z_copy(zo, 1).start()

    la[0] = local_ref[...]
    sa[0] = shared_ref[...]
    v_start(0)
    for copy in loads:
        copy.wait()
    for step in range(nz - 1, -1, -1):
        each(step, begin)
    dx_copy.start()
    for turn_no in range(nz + 2):
        if turn_no < nz:
            each(nz - 1 - turn_no, phase_one)
        if 0 <= turn_no - 1 < nz:
            each(nz - turn_no, phase_two)
        if 0 <= turn_no - 2:
            each(nz + 1 - turn_no, phase_three)
        if turn_no < 5:
            v_finish(turn_no)
            if turn_no < 4:
                v_start(turn_no + 1)
    local_o[...] = la[5]
    shared_o[...] = sa[5]
    dx_copy.wait_recv()

    def join(r, _):
        at = pl.ds(pl.multiple_of(r * 128, 128), 128)
        dx_o[at, :] = own_ref[at, :] + dx_in[at, :].astype(f32)
        return 0

    lax.fori_loop(0, own_ref.shape[0] // 128, join, 0)

    @pl.when(net.has_dn)
    def _():
        z_copy(z, 0).wait_recv()

    @pl.when(net.has_up)
    def _():
        z_copy(z, 1).wait_recv()

    def finish(i, _):
        total = A[z, 0, i].astype(f32)
        total = total + jnp.where(net.has_dn, Z[z, 0, i].astype(f32), 0.0)
        total = total + jnp.where(net.has_up, Z[z, 1, i].astype(f32), 0.0)
        j = part_of(m, order_ref[d * full + i])
        tile = jnp.concatenate([total, rest_of(total, free_of(j))], 0)
        tile_o[i] = turned(tile, j, -1)
        return 0

    lax.fori_loop(0, full, finish, 0)

    def sent(zo, side):
        for kind in range(4):
            c_copy(zo, kind).wait_send()
        xd_copy(zo).wait_send()
        yd_copy(zo).wait_send()
        x_copy(zo).wait_send()
        y_copy(zo).wait_send()
        if isinstance(side, int) and side == 0:
            return
        z_copy(zo, 0).wait_send()

    for step in range(nz):
        each(step, sent)
    dx_copy.wait_send()
    for k in range(5):
        for copy in v_copies(k):
            copy.wait_send()


def scatter_grads(nz, order, parts, own, other, local, shared):
    dma = pltpu.SemaphoreType.DMA
    vm = pl.BlockSpec(memory_space=pltpu.VMEM)
    block = lambda *lead: pltpu.VMEM((*lead, 72, 128), bf16)
    anywhere = pl.BlockSpec(memory_space=pl.ANY)
    return pl.pallas_call(
        functools.partial(scatter_kernel, nz),
        out_shape=[
            jax.ShapeDtypeStruct((24, 96, 128), f32),
            jax.ShapeDtypeStruct(own.shape, f32),
            jax.ShapeDtypeStruct(local.shape, f32),
            jax.ShapeDtypeStruct(shared.shape, f32),
        ],
        in_specs=[pl.BlockSpec(memory_space=pltpu.SMEM)] + [anywhere] * 4 + [vm] * 4,
        out_specs=[vm] * 4,
        scratch_shapes=[
            pltpu.VMEM((4, 48 * nz, 96, 128), bf16), block(nz, 4, 24), block(nz, 4, 24), block(nz, 4, 24),
            block(nz, 12), block(nz, 12), block(nz, 24), block(nz, 24), block(nz, 2, 24), pltpu.VMEM(other.shape, bf16),
            pltpu.VMEM((6, *local.shape), f32), pltpu.VMEM((5, *local.shape), f32),
            pltpu.VMEM((6, *shared.shape), f32), pltpu.VMEM((5, *shared.shape), f32),
            dma((4,)), dma((nz, 4)), dma((nz, 4)),
        ]
        + [dma((nz,))] * 9
        + [dma((nz, 2)), dma((2,)), dma((5, 2)), dma((5, 2))],
        compiler_params=pltpu.CompilerParams(
            collective_id=1, has_side_effects=True, vmem_limit_bytes=56 << 20
        ),
        name="scatter_grads",
    )(order, *parts, own, other, local, shared)


STEP = 5
BETA_ONE = 0.5
BETA_TWO = 0.5
ADAM_EPS = 1e-08
RATE_TILES = 0.04
RATE_VECTORS = 0.2
DECAY = 0.01
HIGH = lax.Precision.HIGHEST


def adam(grad, first, second):
    first_new = BETA_ONE * first + (1.0 - BETA_ONE) * grad
    second_new = BETA_TWO * second + (1.0 - BETA_TWO) * grad * grad
    step_dir = (
        first_new
        / (1.0 - BETA_ONE**STEP)
        / (jnp.sqrt(second_new / (1.0 - BETA_TWO**STEP)) + ADAM_EPS)
    )
    return (first_new, second_new, step_dir)


def from_tiles(tile_set, row_count, col_count):
    edge = tile_set.shape[-1]
    return (
        tile_set.reshape(row_count // edge, col_count // edge, edge, edge)
        .transpose(0, 2, 1, 3)
        .reshape(row_count, col_count)
    )


def plain_weights(tile_order, master, local):
    tiles = lax.all_gather(master.astype(bf16), "dp", axis=0, tiled=True)
    tiles = lax.all_gather(tiles, "mp", axis=0)
    count = tile_order.shape[0]
    inverse = jnp.zeros((count,), jnp.int32).at[tile_order].set(jnp.arange(count, dtype=jnp.int32))
    natural = tiles[:, inverse]
    dense = []
    for rows, cols, where in GRIDS:
        pieces = []
        for r in range(rows):
            pick = [where(r, j) for j in range(cols)]
            groups = jnp.asarray([p for p, _ in pick], jnp.int32)
            numbers = jnp.asarray([n for _, n in pick], jnp.int32)
            pieces.append(natural[groups, numbers].transpose(1, 0, 2).reshape(96, cols * 96))
        dense.append(jnp.concatenate(pieces, 0))
    return (*dense, lax.all_gather(local, "mp", axis=0))


def plain_scatter(order, parts, own, other, local, shared):
    tiles = jnp.concatenate(parts, 1)[:, order]
    mine = lax.psum_scatter(tiles, "mp", scatter_dimension=0, tiled=False).astype(f32)
    turns = part_of(lax.axis_index("mp"), order)[:, None, None]
    back = mine
    for k in range(1, 4):
        back = jnp.where(turns == k, jnp.roll(mine, -96 * k, -1), back)
    owned = lax.psum_scatter(back[..., :96], "dp", scatter_dimension=0, tiled=True)
    count = lax.axis_size("mp")
    swapped = lax.ppermute(other, "mp", [(i, i ^ 1) for i in range(count)])
    local_sum, shared_sum = lax.psum((local, shared), ("dp", "mp"))
    return owned, own + swapped.astype(f32), local_sum, shared_sum


def shards(
    tokens,
    cotangent,
    lengths,
    tile_order,
    master,
    first_moment,
    second_moment,
    basis_left,
    basis_right,
    local_vec,
    local_first,
    local_second,
    shared_vec,
    shared_first,
    shared_second,
):
    group_count = lax.axis_size("mp")
    group_index = lax.axis_index("mp")
    owners = lax.axis_size("dp")
    row_total, width = tokens.shape
    rows = row_total // group_count
    per_owner = master.shape[1]
    nz = owners // 2
    routed = per_owner == 24 and nz == 4 and group_count == 4

    if routed:
        w_qkv, w_out, w_up, w_down, vectors = gather_weights(
            nz, tile_order, slot_of_tile(tile_order), master[0], local_vec
        )
    else:
        w_qkv, w_out, w_up, w_down, vectors = plain_weights(tile_order, master[0], local_vec)
    output, tq, to, tu, td, own, other, local_terms, shared_terms = layer(
        tokens, cotangent, lengths, vectors, shared_vec, w_qkv, w_out, w_up, w_down, rows
    )
    parts = [t.reshape(group_count, -1, 96, 128) for t in (tq, to, tu, td)]
    if routed:
        owned, input_grad, local_sum, shared_grad = scatter_grads(
            nz, tile_order, parts, own, other, local_terms, shared_terms
        )
        owned = owned[:, :, :96]
    else:
        owned, input_grad, local_sum, shared_grad = plain_scatter(
            tile_order, parts, own, other, local_terms, shared_terms
        )
    local_grad = lax.dynamic_slice_in_dim(local_sum[:, 0], group_index, 1, 0)
    left_basis = basis_left[0]
    right_basis = basis_right[0]
    rotated = jnp.einsum("ski,skl->sil", left_basis, owned, precision=HIGH)
    rotated = jnp.einsum("sil,slj->sij", rotated, right_basis, precision=HIGH)
    tile_first, tile_second, direction = adam(rotated, first_moment[0], second_moment[0])
    turned = jnp.einsum("sik,skl->sil", left_basis, direction, precision=HIGH)
    turned = jnp.einsum("sil,sjl->sij", turned, right_basis, precision=HIGH)
    tile_weight = master[0] - RATE_TILES * (turned + DECAY * master[0])
    local_first_new, local_second_new, local_dir = adam(local_grad, local_first, local_second)
    shared_first_new, shared_second_new, shared_dir = adam(shared_grad, shared_first, shared_second)
    return (
        output,
        input_grad,
        owned[None],
        tile_first[None],
        tile_second[None],
        tile_weight[None],
        local_grad,
        local_first_new,
        local_second_new,
        local_vec - RATE_VECTORS * local_dir,
        shared_grad,
        shared_first_new,
        shared_second_new,
        shared_vec - RATE_VECTORS * shared_dir,
    )


def solution(mesh):
    placed = (
        P("dp", None),
        P("dp", None),
        P("dp"),
        P(),
        P("mp", "dp", None, None),
        P("mp", "dp", None, None),
        P("mp", "dp", None, None),
        P("mp", "dp", None, None),
        P("mp", "dp", None, None),
        P("mp", None),
        P("mp", None),
        P("mp", None),
        P(),
        P(),
        P(),
    )
    return jax.shard_map(
        shards,
        mesh=mesh,
        in_specs=placed,
        out_specs=(
            P(("dp", "mp"), None),
            P(("dp", "mp"), None),
            P("mp", "dp", None, None),
            P("mp", "dp", None, None),
            P("mp", "dp", None, None),
            P("mp", "dp", None, None),
            P("mp", None),
            P("mp", None),
            P("mp", None),
            P("mp", None),
            P(),
            P(),
            P(),
            P(),
        ),
        check_vma=False,
    )
```

```python
import functools
import jax
import jax.numpy as jnp
from jax import lax
from jax.experimental import pallas as pl
from jax.experimental.pallas import tpu as pltpu
from jax.sharding import PartitionSpec as P

MESH = pl.DeviceIdType.MESH
f32 = jnp.float32
bf16 = jnp.bfloat16


def lanes_of(shape):
    return lax.broadcasted_iota(jnp.int32, shape, len(shape) - 1)


def turn(v, amount):
    return pltpu.roll(v, amount, v.ndim - 1)


def free_of(j):
    return (3 * j + 3) % 4


def part_of(group, number):
    return jnp.where(number < 48, 2 * group + number % 2, number) % 4


def groups_of(shape):
    return lanes_of(shape) // 32


def to_wire(tile, free):
    rest = tile[72:96]
    side = jnp.concatenate([turn(rest, 96), turn(rest, 64), turn(rest, 32)], 0)
    return jnp.where(groups_of(side.shape) == free, side, tile[:72])


def rest_of(wire, free):
    group = groups_of((24, 128))
    first, second, third = turn(wire[:24], 32), turn(wire[24:48], 64), turn(wire[48:72], 96)
    return jnp.where(
        group == (free + 1) % 4, first, jnp.where(group == (free + 2) % 4, second, third)
    )


def turned(tile, j, sign):
    out = tile
    for k in range(1, 4):
        out = jnp.where(j == k, turn(tile, sign * 96 * k % 128), out)
    return out


def join_four(wires):
    lane, group = lanes_of((72, 128)), groups_of((24, 128))
    a, b, c, d = wires
    tops = [jnp.where(lane < 96, a, b), jnp.where(lane < 64, b, c), jnp.where(lane < 32, c, d)]
    rests = []
    for i in range(3):
        at = slice(24 * i, 24 * i + 24)
        mixed = jnp.where(
            group == 3, a[at], jnp.where(group == 2, b[at], jnp.where(group == 1, c[at], d[at]))
        )
        rests.append(turn(mixed, 32 * (i + 1)))
    pieces = []
    for k in range(3):
        index = (group + k) % 3
        rest = jnp.where(index == 0, rests[0], jnp.where(index == 1, rests[1], rests[2]))
        pieces.append(jnp.concatenate([tops[k], rest], 0))
    return pieces


def split_four(pieces):
    lane, group = lanes_of((72, 128)), groups_of((24, 128))
    a, b, c = (p[:72] for p in pieces)
    rests = [p[72:] for p in pieces]
    sides = []
    for i in range(3):
        mixed = jnp.where(
            group % 3 == 0,
            rests[i],
            jnp.where(group == 1, rests[(i - 1) % 3], rests[(i - 2) % 3]),
        )
        sides.append(turn(mixed, 96 - 32 * i))
    side = jnp.concatenate(sides, 0)
    tops = [a, jnp.where(lane < 64, b, a), jnp.where(lane < 32, c, b), c]
    return [jnp.where(lane // 32 == 3 - t, side, tops[t]) for t in range(4)]


def place():
    d, m = lax.axis_index("dp"), lax.axis_index("mp")
    return d // 2, d % 2, m // 2, m % 2


class Net:
    def __init__(self, nz):
        self.nz = nz
        self.z, self.x, self.y, self.c = place()
        self.d = self.z * 2 + self.x
        self.m = self.y * 2 + self.c
        self.xn = (self.z * 2 + 1 - self.x, self.m)
        self.yn = (self.d, (1 - self.y) * 2 + self.c)
        self.cn = (self.d, self.y * 2 + 1 - self.c)
        self.up = (self.d + 2, self.m)
        self.dn = (self.d - 2, self.m)
        self.has_up = self.z < nz - 1
        self.has_dn = self.z > 0

    def peers(self):
        others = [(lax.rem(self.z + k, self.nz) * 2 + self.x, self.m) for k in range(1, self.nz)]
        return [self.xn, self.yn, self.cn] + others

    def greet(self):
        for peer in self.peers():
            pl.semaphore_signal(
                pltpu.get_barrier_semaphore(), inc=1, device_id=peer, device_id_type=MESH
            )

    def await_all(self):
        pl.semaphore_wait(pltpu.get_barrier_semaphore(), len(self.peers()))


def send(src, dst, ss, rs, peer):
    return pltpu.make_async_remote_copy(
        src_ref=src, dst_ref=dst, send_sem=ss, recv_sem=rs, device_id=peer, device_id_type=MESH
    )


def tile_qkv(r, j):
    return (j % 8) // 2, r * 6 + (j // 8) * 2 + j % 2


def tile_out(r, j):
    return r // 2, 48 + (r % 2) * 8 + j


def tile_up(r, j):
    return j // 8, 64 + r * 8 + j % 8


def tile_down(r, j):
    return r // 8, 128 + (r % 8) * 8 + j


GRIDS = ((8, 24, tile_qkv), (8, 8, tile_out), (8, 32, tile_up), (32, 8, tile_down))


def gather_kernel(
    nz, order_ref, src_ref, master_ref, local_ref, o_qkv, o_out, o_up, o_down, o_local,
    G, LV, d_qkv, d_out, d_up, d_down,
    zs, zr, xs, xr, ys, yr, xds, xdr, yds, ydr, cs, cr, zxs, zxr, cxs, cxr, outs, lvs, lvr,
):
    net = Net(nz)
    z, x, y, c, m = net.z, net.x, net.y, net.c, net.m
    my = (1 - y) * 2 + c
    full, late = 24, 5
    early = full - late
    net.greet()

    def stage(i, _):
        tile = jnp.concatenate([master_ref[i], jnp.zeros((96, 32), f32)], axis=-1)
        j = part_of(m, order_ref[net.d * full + i])
        tile = turned(tile, j, 1)
        G[m, net.d * full + i] = to_wire(tile, free_of(j)).astype(bf16)
        return 0

    lax.fori_loop(0, full, stage, 0)
    LV[m] = local_ref[...]
    net.await_all()
    lv_y = send(LV.at[m], LV.at[m], lvs.at[0], lvr.at[0], net.yn)
    lv_c = send(LV.at[m], LV.at[m], lvs.at[1], lvr.at[1], net.cn)
    lv_d = send(LV.at[my], LV.at[my], lvs.at[2], lvr.at[2], net.cn)

    def slot(mo, zo, xo, lo=0, n=full):
        return G.at[mo, pl.ds((zo * 2 + xo) * full + lo, n)]

    def is_own(side):
        return isinstance(side, int) and side == 0

    def split(side):
        return (full, full // 2) if is_own(side) else (early, early // 2 + 1)

    kinds = ((m, x), (m, 1 - x), (my, x), (my, 1 - x))
    flip = 1 - 2 * c

    def z_copy(zo, direction):
        s = slot(m, zo, x)
        peer = net.up if direction == 0 else net.dn
        return send(s, s, zs.at[zo, direction], zr.at[zo], peer)

    def late_copies(zo, direction):
        peer = net.up if direction == 0 else net.dn
        for k in range(3):
            mo, xo = kinds[k + 1]
            s = slot(mo, zo, xo, early, late)
            yield send(s, s, zxs.at[zo, k, direction], zxr.at[zo, k], peer)

    def c_copy(zo, kind, side, shift=0):
        mo, xo = kinds[kind]
        s = slot(mo + shift, zo, xo, 0, full if kind == 0 or is_own(side) else early)
        return send(s, s, cs.at[zo, kind], cr.at[zo, kind], net.cn)

    def c_late(zo, k, shift=0):
        mo, xo = kinds[k + 1]
        s = slot(mo + shift, zo, xo, early, late)
        return send(s, s, cxs.at[zo, k], cxr.at[zo, k], net.cn)

    def x_copy(zo, xo, side):
        s = slot(m, zo, xo, 0, split(side)[0])
        return send(s, s, xs.at[zo], xr.at[zo], net.xn)

    def y_copy(zo, mo, side):
        s = slot(mo, zo, x, 0, split(side)[0])
        return send(s, s, ys.at[zo], yr.at[zo], net.yn)

    def xd_copy(zo, xo, side):
        s = slot(my, zo, xo, 0, split(side)[1])
        return send(s, s, xds.at[zo], xdr.at[zo], net.xn)

    def yd_copy(zo, mo, side):
        count, lo = split(side)
        s = slot(mo, zo, 1 - x, lo, count - lo)
        return send(s, s, yds.at[zo], ydr.at[zo], net.yn)

    def each(step, fn):
        if step == 0:
            fn(z, 0)
            return

        @pl.when(z >= step)
        def _():
            fn(z - step, 1)

        @pl.when(z + step < nz)
        def _():
            fn(z + step, -1)

    def onward(side, copies):
        if is_own(side) or side == 1:
            @pl.when(net.has_up)
            def _():
                for copy in copies(0):
                    copy.start()

        if is_own(side) or side == -1:
            @pl.when(net.has_dn)
            def _():
                for copy in copies(1):
                    copy.start()

    def arrive(zo, side):
        if not is_own(side):
            z_copy(zo, 0).wait_recv()
        onward(side, lambda direction: [z_copy(zo, direction)])
        x_copy(zo, x, side).start()
        y_copy(zo, m, side).start()
        c_copy(zo, 0, side).start()

    def diag(zo, side):
        x_copy(zo, 1 - x, side).wait_recv()
        yd_copy(zo, m, side).start()
        c_copy(zo, 1, side).start()
        y_copy(zo, my, side).wait_recv()
        xd_copy(zo, x, side).start()
        c_copy(zo, 2, side).start()

    def fin(zo, side):
        xd_copy(zo, 1 - x, side).wait_recv()
        yd_copy(zo, my, side).wait_recv()
        c_copy(zo, 3, side).start()

    def last(zo, side):
        if not is_own(side):
            for copy in late_copies(zo, 0):
                copy.wait_recv()
        onward(side, lambda direction: late_copies(zo, direction))
        if not is_own(side):
            for k in range(3):
                c_late(zo, k).start()

    def other_core(zo, side):
        for kind in range(4):
            c_copy(zo, kind, side, flip).wait_recv()
            if kind and not is_own(side):
                c_late(zo, kind - 1, flip).wait_recv()

    each(0, arrive)
    lv_y.start()
    lv_c.start()
    each(1, arrive)
    each(0, diag)
    send(LV.at[my], LV.at[my], lvs.at[0], lvr.at[0], net.yn).wait_recv()
    lv_d.start()
    each(2, arrive)
    each(1, diag)
    each(0, fin)
    each(0, last)
    each(3, arrive)
    each(1, fin)
    each(1, last)
    each(2, diag)
    each(2, last)
    each(2, fin)
    each(3, diag)
    each(3, last)
    each(3, fin)
    for step in range(nz):
        each(step, other_core)
    mc = m + flip
    send(LV.at[mc], LV.at[mc], lvs.at[1], lvr.at[1], net.cn).wait_recv()
    mc = my + flip
    send(LV.at[mc], LV.at[mc], lvs.at[2], lvr.at[2], net.cn).wait_recv()
    o_local[...] = LV[...]

    copies = []
    for i, ((rows, cols, where), dense, out) in enumerate(
        zip(GRIDS, (d_qkv, d_out, d_up, d_down), (o_qkv, o_out, o_up, o_down))
    ):
        def fill(r, _):
            for g in range(cols // 4):
                tiles = []
                for t in range(4):
                    p, n = where(r, 4 * g + t)
                    tiles.append(G[p, src_ref[n]].astype(f32))
                for k, piece in enumerate(join_four(tiles)):
                    dense[pl.ds(pl.multiple_of(r * 96, 96), 96), pl.ds(384 * g + 128 * k, 128)] = (
                        piece.astype(bf16)
                    )
            return 0

        lax.fori_loop(0, rows, fill, 0)
        copy = pltpu.make_async_copy(dense, out, outs.at[i])
        copy.start()
        copies.append(copy)

    def sent(zo, side):
        x_copy(zo, x, side).wait_send()
        y_copy(zo, m, side).wait_send()
        yd_copy(zo, m, side).wait_send()
        xd_copy(zo, x, side).wait_send()
        for kind in range(4):
            c_copy(zo, kind, side).wait_send()
        if not is_own(side):
            for k in range(3):
                c_late(zo, k).wait_send()

        def done(direction):
            z_copy(zo, direction).wait_send()
            for copy in late_copies(zo, direction):
                copy.wait_send()

        if is_own(side) or side == 1:
            pl.when(net.has_up)(lambda: done(0))
        if is_own(side) or side == -1:
            pl.when(net.has_dn)(lambda: done(1))

    for step in range(nz):
        each(step, sent)
    lv_y.wait_send()
    lv_c.wait_send()
    lv_d.wait_send()
    for copy in copies:
        copy.wait()


def gather_weights(nz, order, src, master, local):
    dma = pltpu.SemaphoreType.DMA
    shapes = [(r * 96, c * 96) for r, c, _ in GRIDS]
    return pl.pallas_call(
        functools.partial(gather_kernel, nz),
        out_shape=[jax.ShapeDtypeStruct(s, bf16) for s in shapes]
        + [jax.ShapeDtypeStruct((4, *local.shape), f32)],
        in_specs=[pl.BlockSpec(memory_space=pltpu.SMEM)] * 2
        + [pl.BlockSpec(memory_space=pltpu.VMEM)] * 2,
        out_specs=[pl.BlockSpec(memory_space=pl.ANY)] * 4 + [pl.BlockSpec(memory_space=pltpu.VMEM)],
        scratch_shapes=[pltpu.VMEM((4, 2 * nz * 24, 72, 128), bf16), pltpu.VMEM((4, *local.shape), f32)]
        + [pltpu.VMEM(s, bf16) for s in shapes]
        + [dma((nz, 2)), dma((nz,))]
        + [dma((nz,))] * 8
        + [dma((nz, 4)), dma((nz, 4)), dma((nz, 3, 2)), dma((nz, 3)), dma((nz, 3)), dma((nz, 3))]
        + [dma((4,)), dma((3,)), dma((3,))],
        compiler_params=pltpu.CompilerParams(
            collective_id=0, has_side_effects=True, vmem_limit_bytes=56 << 20
        ),
        name="gather_weights",
    )(order, src, master, local)


def slot_of_tile(tile_order):
    count = tile_order.shape[0]
    slots = jnp.arange(count, dtype=jnp.int32)
    return jnp.sum(jnp.where(tile_order[None, :] == slots[:, None], slots[None, :], 0), 1)


NEG_BIG = -1e30
NORM_EPS = 1e-05
ROOT_HALF = 0.7071067811865476
PHI_SCALE = 0.3989422804014327


def nt(a, b):
    return lax.dot_general(a, b, (((1,), (1,)), ((), ())), preferred_element_type=f32)


def tn(a, b):
    return lax.dot_general(a, b, (((0,), (0,)), ((), ())), preferred_element_type=f32)


def nn(a, b):
    return jnp.dot(a, b, preferred_element_type=f32)


def standard(values):
    centre = values - jnp.mean(values, -1, keepdims=True)
    scale = lax.rsqrt(jnp.mean(centre * centre, -1, keepdims=True) + NORM_EPS)
    return centre * scale, scale


def standard_back(grad, normed, scale, gain):
    inner = grad * gain
    return scale * (
        inner - jnp.mean(inner, -1, keepdims=True) - normed * jnp.mean(inner * normed, -1, keepdims=True)
    )


def col_sum(values):
    return jnp.sum(values, 0, keepdims=True)


def layer_kernel(
    tokens_ref, cot_ref, lengths_ref, vec_ref, sv_ref, wq_ref, wo_ref, wu_ref, wd_ref,
    out_ref, tq_ref, to_ref, tu_ref, td_ref, own_ref, other_ref, dl_ref, ds_ref,
    x, cot, wqkv, wout, wup, wdown, bias, q, k, v, probs, o_t, hid, low, low_t, n_one, r_one, acc,
    act, slope, g_low, g_o, dq, dk, dv, out, other, su, sd, so, sq, loads, stores, su_sem, sd_sem, sq_sem,
):
    rows, width = q.shape
    seq_len = k.shape[0]
    chunks, _, cut = act.shape
    tiles = width // 96
    pairs = width // 128
    piece = 128
    zero = jnp.zeros((), bf16)
    member = lax.axis_index("mp")
    share = seq_len // rows
    seq, part = member // share, member % share
    length = lengths_ref[seq]
    bound = 64 * ((length + 127) // 128)
    start_b = pl.multiple_of(bound, 64)
    here = pl.ds(pl.multiple_of(part * rows, rows), rows)
    there = pl.ds(pl.multiple_of((1 - part) * rows, rows), rows)

    def load(src, dst, i):
        copy = pltpu.make_async_copy(src, dst, loads.at[i])
        copy.start()
        return copy

    get_x = load(tokens_ref.at[pl.ds(pl.multiple_of(seq * seq_len, seq_len), seq_len)], x, 0)
    get_q = load(wq_ref, wqkv, 1)
    get_o = load(wo_ref, wout, 2)
    get_u = load(wu_ref, wup, 3)
    get_d = load(wd_ref, wdown, 4)
    get_c = load(cot_ref.at[pl.ds(pl.multiple_of(member * rows, rows), rows)], cot, 5)

    groups = vec_ref.shape[0]
    third = width // groups
    bias[:, :width] = jnp.concatenate([vec_ref[p][:, :third] for p in range(groups)], 1)
    bias[:, width:] = jnp.concatenate([vec_ref[p][:, third : 2 * third] for p in range(groups)], 1)

    get_x.wait()
    get_q.wait()
    for lo in range(0, width, 256):
        got = nn(x[here, :], wqkv[:, lo : lo + 256]) + bias[:, lo : lo + 256]
        q[:, lo : lo + 256] = got.astype(bf16) * jnp.asarray(0.125, bf16)

    def project(r, _):
        at = pl.ds(pl.multiple_of(r * rows, rows), rows)
        for lo in range(0, width, 256):
            k[at, lo : lo + 256] = nn(x[at, :], wqkv[:, width + lo : width + lo + 256]).astype(bf16)
            got = nn(x[at, :], wqkv[:, 2 * width + lo : 2 * width + lo + 256])
            v[at, lo : lo + 256] = (got + bias[:, width + lo : width + lo + 256]).astype(bf16)
        return 0

    lax.fori_loop(0, share, project, 0)

    def picks(shape, rows_at):
        row = lax.broadcasted_iota(jnp.int32, shape, rows_at) + part * rows
        lane = lax.broadcasted_iota(jnp.int32, shape, 1 - rows_at)
        return (row < bound) == (lane < 64)

    windows = ((0, bound), (start_b, length - bound))

    def forward(pair, _):
        cols = pl.ds(pl.multiple_of(pair * 128, 128), 128)
        queries = q[:, cols]
        pick = picks((rows, 128), 0)
        outs = []
        for w, (start, limit) in enumerate(windows):
            these = jnp.where(pick, queries, zero) if w == 0 else jnp.where(pick, zero, queries)
            scores = nt(k[pl.ds(start, rows), cols], these)
            inside = lax.broadcasted_iota(jnp.int32, scores.shape, 0) < limit
            scores = jnp.where(inside, scores, NEG_BIG)
            weight = jnp.exp(scores - jnp.max(scores, 0, keepdims=True))
            low_probs = (weight * (1.0 / jnp.sum(weight, 0, keepdims=True))).astype(bf16)
            probs[2 * pair + w] = low_probs
            outs.append(tn(v[pl.ds(start, rows), cols], low_probs))
        o_t[cols, :] = jnp.where(picks((128, rows), 1), outs[0], outs[1]).astype(bf16)
        return 0

    lax.fori_loop(0, pairs, forward, 0)

    def by_rows(fn):
        def body(r, _):
            fn(pl.ds(pl.multiple_of(r * piece, piece), piece), r)
            return 0

        lax.fori_loop(0, rows // piece, body, 0)

    get_o.wait()
    acc[...] = tn(o_t[...], wout[...])

    def norm_one(at, r):
        mine = pl.ds(pl.multiple_of(part * rows + r * piece, piece), piece)
        z_one = x[mine, :].astype(f32) + acc[at, :] + sv_ref[0:1, :]
        normed, scale = standard(z_one)
        hidden = normed * sv_ref[2:3, :] + sv_ref[3:4, :]
        n_one[at, :] = normed
        r_one[at, :] = jnp.broadcast_to(scale, (piece, 128))
        hid[at, :] = hidden
        low[at, :] = hidden.astype(bf16)
        acc[at, :] = jnp.zeros((piece, width), f32)

    by_rows(norm_one)
    low_t[...] = low[...].T
    get_u.wait()
    get_d.wait()

    def feed(i, _):
        at = pl.ds(pl.multiple_of(i * cut, cut), cut)
        half = chunks // groups
        shift = pl.multiple_of(2 * third + (i % half) * cut, 128)
        pre = nn(low[...], wup[:, at]) + vec_ref[i // half, :, pl.ds(shift, cut)]
        phi = 0.5 * (1.0 + lax.erf(pre * ROOT_HALF))
        density = jnp.exp(-0.5 * pre * pre) * PHI_SCALE
        active = (pre * phi).astype(bf16)
        act[i] = active
        slope[i] = (phi + pre * density).astype(bf16)
        acc[...] += nn(active, wdown[at, :])
        return 0

    lax.fori_loop(0, chunks, feed, 0)
    get_c.wait()
    ds_ref[...] = jnp.zeros_like(ds_ref)

    def norm_two(at, r):
        z_two = hid[at, :] + acc[at, :] + sv_ref[1:2, :]
        normed, scale = standard(z_two)
        row = lax.broadcasted_iota(jnp.int32, (piece, 1), 0) + part * rows + r * piece
        valid = (row < length).astype(f32)
        out[at, :] = ((normed * sv_ref[4:5, :] + sv_ref[5:6, :]) * valid).astype(bf16)
        grad = cot[at, :].astype(f32) * valid
        back = standard_back(grad, normed, scale, sv_ref[4:5, :])
        ds_ref[4:5, :] += col_sum(grad * normed)
        ds_ref[5:6, :] += col_sum(grad)
        ds_ref[1:2, :] += col_sum(back)
        g_low[at, :] = back.astype(bf16)
        acc[at, :] = back

    by_rows(norm_two)
    put_out = pltpu.make_async_copy(out, out_ref, stores.at[0])
    put_out.start()

    def put_u(i):
        half = chunks // groups
        return pltpu.make_async_copy(su.at[i % 2], tu_ref.at[i // half, :, i % half], su_sem.at[i % 2])

    def put_d(i):
        half = chunks // groups
        return pltpu.make_async_copy(sd.at[i % 2], td_ref.at[i // half, i % half], sd_sem.at[i % 2])

    def cuts(full, r):
        pieces = [full[96 * r : 96 * r + 96, 128 * n : 128 * n + 128] for n in range(3)]
        return [wire.astype(bf16) for wire in split_four(pieces)]

    def feed_back(i, _):
        at = pl.ds(pl.multiple_of(i * cut, cut), cut)

        @pl.when(i >= 2)
        def _():
            put_u(i - 2).wait()
            put_d(i - 2).wait()

        half = chunks // groups
        shift = pl.multiple_of(2 * third + (i % half) * cut, 128)
        grad_low = (nt(g_low[...], wdown[at, :]) * slope[i].astype(f32)).astype(bf16)
        dl_ref[i // half, :, pl.ds(shift, cut)] = col_sum(grad_low.astype(f32))
        acc[...] += nt(grad_low, wup[:, at])
        for g in range(width // 384):
            down = tn(act[i], g_low[:, 384 * g : 384 * g + 384])
            for r in range(4):
                for t, tile in enumerate(cuts(down, r)):
                    sd[i % 2, r * tiles + 4 * g + t] = tile
        up = nn(low_t[...], grad_low)
        for r in range(tiles):
            for t, tile in enumerate(cuts(up, r)):
                su[i % 2, r, t] = tile
        put_u(i).start()
        put_d(i).start()
        return 0

    lax.fori_loop(0, chunks, feed_back, 0)

    def norm_back(at, r):
        grad = acc[at, :]
        normed = n_one[at, :]
        back = standard_back(grad, normed, r_one[at, 0:1], sv_ref[2:3, :])
        ds_ref[2:3, :] += col_sum(grad * normed)
        ds_ref[3:4, :] += col_sum(grad)
        ds_ref[0:1, :] += col_sum(back)
        acc[at, :] = back
        g_low[at, :] = back.astype(bf16)

    by_rows(norm_back)
    g_o[...] = nt(g_low[...], wout[...]).astype(bf16)
    for g in range(width // 384):
        outer = nn(o_t[...], g_low[:, 384 * g : 384 * g + 384])
        for r in range(tiles):
            for t, tile in enumerate(cuts(outer, r)):
                so[r, 4 * g + t] = tile
    put_o = pltpu.make_async_copy(so, to_ref, stores.at[1])
    put_o.start()
    dk[...] = jnp.zeros_like(dk)
    dv[...] = jnp.zeros_like(dv)

    def backward(pair, _):
        cols = pl.ds(pl.multiple_of(pair * 128, 128), 128)
        pick, pick_t = picks((rows, 128), 0), picks((128, rows), 1)
        queries, grads = q[:, cols], g_o[:, cols]
        grads_t = grads.astype(f32).T
        inner = grads_t * o_t[cols, :].astype(f32)
        outs = []
        for w, (start, _) in enumerate(windows):
            at = pl.ds(start, rows)
            mine = (lambda a: jnp.where(pick, a, zero)) if w == 0 else (lambda a: jnp.where(pick, zero, a))
            mine_t = (lambda a: jnp.where(pick_t, a, 0.0)) if w == 0 else (lambda a: jnp.where(pick_t, 0.0, a))
            dot_sum = jnp.sum(mine_t(inner), 0, keepdims=True)
            grad_probs = nn(v[at, cols], mine_t(grads_t).astype(bf16))
            these = probs[2 * pair + w]
            grad_scores = (these.astype(f32) * (grad_probs - dot_sum)).astype(bf16)
            dv[at, cols] = nn(these, mine(grads)).astype(bf16)
            dk[at, cols] = nn(grad_scores, mine(queries)).astype(bf16)
            outs.append(tn(k[at, cols], grad_scores))
        dq[:, cols] = (jnp.where(pick_t, outs[0], outs[1]) * 0.125).T.astype(bf16)
        return 0

    lax.fori_loop(0, pairs, backward, 0)

    other[...] = (
        nt(dk[there, :], wqkv[:, width : 2 * width]) + nt(dv[there, :], wqkv[:, 2 * width :])
    ).astype(bf16)
    put_x = pltpu.make_async_copy(other, other_ref, stores.at[2])
    put_x.start()
    hid[...] = (
        acc[...]
        + nt(dq[...], wqkv[:, :width])
        + nt(dk[here, :], wqkv[:, width : 2 * width])
        + nt(dv[here, :], wqkv[:, 2 * width :])
    )
    put_own = pltpu.make_async_copy(hid, own_ref, stores.at[3])
    put_own.start()
    sum_q = col_sum(dq[...].astype(f32))
    sum_v = col_sum(dv[...].astype(f32))
    for p in range(groups):
        dl_ref[p, :, :third] = sum_q[:, third * p : third * p + third]
        dl_ref[p, :, third : 2 * third] = sum_v[:, third * p : third * p + third]

    everyone = pl.ds(0, seq_len)
    puts = []
    for index, (grad, source) in enumerate(((dq, here), (dk, everyone), (dv, everyone))):
        for g in range(width // 384):
            outer = tn(x[source, :], grad[:, 384 * g : 384 * g + 384])
            count = index * (width // 384) + g
            if count >= 2:
                puts[count - 2].wait()
            for r in range(tiles):
                for t, tile in enumerate(cuts(outer, r)):
                    sq[count % 2, t // 2, r, t % 2] = tile
            put = pltpu.make_async_copy(
                sq.at[count % 2], tq_ref.at[pl.ds(2 * g, 2), :, index], sq_sem.at[count % 2]
            )
            put.start()
            puts.append(put)
    for i in (chunks - 2, chunks - 1):
        put_u(i).wait()
        put_d(i).wait()
    for put in (put_out, put_o, put_x, put_own, puts[-2], puts[-1]):
        put.wait()


def layer(tokens, cotangent, lengths, vectors, shared, w_qkv, w_out, w_up, w_down, rows):
    width = w_out.shape[0]
    hidden = w_up.shape[1]
    seq_len = tokens.shape[0] // lengths.shape[0]
    cut = 384
    chunks = hidden // cut
    groups = vectors.shape[0]
    half = chunks // groups
    tiles = width // 96
    anywhere = pl.BlockSpec(memory_space=pl.ANY)
    vm = pl.BlockSpec(memory_space=pltpu.VMEM)
    smem = pl.BlockSpec(memory_space=pltpu.SMEM)
    out = jax.ShapeDtypeStruct
    V = pltpu.VMEM
    dma = pltpu.SemaphoreType.DMA
    tall, wide, long = (rows, width), (width, rows), (seq_len, width)
    return pl.pallas_call(
        layer_kernel,
        in_specs=[anywhere, anywhere, smem, vm, vm] + [anywhere] * 4,
        out_specs=[anywhere] * 7 + [vm, vm],
        out_shape=[
            out(tall, bf16),
            out((groups, tiles, 3, 2, 72, 128), bf16),
            out((tiles, tiles, 72, 128), bf16),
            out((groups, tiles, half, 4, 72, 128), bf16),
            out((groups, half, 4 * tiles, 72, 128), bf16),
            out(tall, f32),
            out(tall, bf16),
            out(vectors.shape, f32),
            out(shared.shape, f32),
        ],
        scratch_shapes=[
            V(long, bf16), V(tall, bf16), V(w_qkv.shape, bf16), V(w_out.shape, bf16), V(w_up.shape, bf16),
            V(w_down.shape, bf16), V((1, 2 * width), f32), V(tall, bf16), V(long, bf16), V(long, bf16),
            V((width // 64, rows, rows), bf16), V(wide, bf16), V(tall, f32), V(tall, bf16), V(wide, bf16),
            V(tall, f32), V((rows, 128), f32), V(tall, f32), V((chunks, rows, cut), bf16),
            V((chunks, rows, cut), bf16), V(tall, bf16), V(tall, bf16), V(tall, bf16), V(long, bf16),
            V(long, bf16), V(tall, bf16), V(tall, bf16), V((2, tiles, 4, 72, 128), bf16),
            V((2, 4 * tiles, 72, 128), bf16), V((tiles, tiles, 72, 128), bf16),
            V((2, 2, tiles, 2, 72, 128), bf16), dma((6,)), dma((4,)), dma((2,)), dma((2,)), dma((2,)),
        ],
        compiler_params=pltpu.CompilerParams(vmem_limit_bytes=60 << 20),
        name="layer",
    )(tokens, cotangent, lengths, vectors, shared, w_qkv, w_out, w_up, w_down)


def scatter_kernel(
    nz, order_ref, tq_ref, to_ref, tu_ref, td_ref, own_ref, other_ref, local_ref, shared_ref,
    tile_o, dx_o, local_o, shared_o,
    TA, TB, S, A, R, XD, YD, X, Y, Z, ZX, dx_in, la, lb, sa, sb,
    tsem, cs, cr, xds, xdr, yds, ydr, xs, xr, ys, yr, zs, zr, zxs, zxr, dxs, vs, vr,
):
    net = Net(nz)
    z, x, y, c, m, d = net.z, net.x, net.y, net.c, net.m, net.d
    my = (1 - y) * 2 + c
    far = (lax.rem(z + 2, nz) * 2 + x, m)
    near = ((z + 1 - 2 * (z % 2)) * 2 + x, m)
    full, late = 24, 5
    early = full - late
    flip = 1 - 2 * c

    def loads(held, core):
        for group in range(2):
            first = 0
            for i, src in enumerate((tq_ref, to_ref, tu_ref, td_ref)):
                count = src.shape[1]
                yield pltpu.make_async_copy(
                    src.at[2 * group + core], held.at[group, pl.ds(first, count)],
                    tsem.at[2 * group + core, i],
                )
                first += count

    for copy in (*loads(TB, 1 - c), *loads(TA, c)):
        copy.start()
    net.greet()
    net.await_all()
    kinds = ((m, x), (m, 1 - x), (my, x), (my, 1 - x))

    def c_copy(zo, kind):
        return send(S.at[zo, kind], R.at[zo, kind], cs.at[zo, kind], cr.at[zo, kind], net.cn)

    def fill(ref, zo, kind, held):
        mo, xo = kinds[kind]
        base = (zo * 2 + xo) * full

        def body(i, _):
            for j in range(4):
                ref[zo, kind, 4 * i + j] = held[mo // 2, order_ref[base + 4 * i + j]]
            return 0

        lax.fori_loop(0, full // 4, body, 0)

    def is_own(side):
        return isinstance(side, int) and side == 0

    def split(side):
        return (full, full // 2) if is_own(side) else (early, early // 2 + 1)

    def xd_copy(zo, side):
        n = split(side)[1]
        return send(
            A.at[zo, 3, pl.ds(0, n)], XD.at[zo, pl.ds(0, n)], xds.at[zo], xdr.at[zo], net.xn
        )

    def yd_copy(zo, side):
        count, lo = split(side)
        n = count - lo
        return send(
            A.at[zo, 3, pl.ds(lo, n)], YD.at[zo, pl.ds(0, n)], yds.at[zo], ydr.at[zo], net.yn
        )

    def x_copy(zo, side):
        n = split(side)[0]
        return send(A.at[zo, 1, pl.ds(0, n)], X.at[zo, pl.ds(0, n)], xs.at[zo], xr.at[zo], net.xn)

    def y_copy(zo, side):
        n = split(side)[0]
        return send(A.at[zo, 2, pl.ds(0, n)], Y.at[zo, pl.ds(0, n)], ys.at[zo], yr.at[zo], net.yn)

    def z_copy(zo, direction):
        peer = net.up if direction == 0 else net.dn
        return send(A.at[zo, 0], Z.at[zo, direction], zs.at[zo], zr.at[zo, direction], peer)

    def late_copies(zo, direction):
        peer = net.up if direction == 0 else net.dn
        for k in range(3):
            yield send(
                A.at[zo, k + 1, pl.ds(early, late)], ZX.at[zo, direction, k],
                zxs.at[zo, k], zxr.at[zo, direction, k], peer,
            )

    dx_copy = send(other_ref, dx_in, dxs.at[0], dxs.at[1], net.cn)
    peers = (net.cn, net.xn, net.yn, near, far)

    def v_copies(k):
        return (
            send(la.at[k], lb.at[k], vs.at[k, 0], vr.at[k, 0], peers[k]),
            send(sa.at[k], sb.at[k], vs.at[k, 1], vr.at[k, 1], peers[k]),
        )

    def v_start(k):
        for copy in v_copies(k):
            copy.start()

    def v_finish(k):
        for copy in v_copies(k):
            copy.wait_recv()
        la[k + 1] = la[k] + lb[k]
        sa[k + 1] = sa[k] + sb[k]

    def add(zo, kind, other, lo=0, n=full):
        def body(i, _):
            A[zo, kind, lo + i] = (A[zo, kind, lo + i].astype(f32) + other(i)).astype(bf16)
            return 0

        lax.fori_loop(0, n, body, 0)

    def each(step, fn):
        if step == 0:
            fn(z, 0)
            return

        @pl.when(z >= step)
        def _():
            fn(z - step, 1)

        @pl.when(z + step < nz)
        def _():
            fn(z + step, -1)

    def begin(zo, side):
        for kind in (3, 1, 2, 0):
            fill(S, zo, kind, TB)
            c_copy(zo, kind).start()

    def begin_own(zo, side):
        for kind in (3, 1, 2, 0):
            fill(A, zo, kind, TA)

    def late_add(zo, direction):
        for k, copy in enumerate(late_copies(zo, direction)):
            copy.wait_recv()
            add(zo, k + 1, lambda i: ZX[zo, direction, k, i].astype(f32), early, late)

    def diagonal(zo, side):
        xd_copy(zo, side).start()
        yd_copy(zo, side).start()

    def phase_one(zo, side):
        for kind in (3, 1, 2, 0):
            c_copy(zo, kind).wait_recv()
            add(zo, kind, lambda i: R[zo, kind, i].astype(f32))
            if kind == 3 and not is_own(side):
                diagonal(zo, side)
        if is_own(side) or side == -1:
            @pl.when(net.has_dn)
            def _():
                late_add(zo, 0)

        if is_own(side) or side == 1:
            @pl.when(net.has_up)
            def _():
                late_add(zo, 1)

        if is_own(side):
            diagonal(zo, side)
        else:
            for copy in late_copies(zo, 0 if side == -1 else 1):
                copy.start()

    def phase_two(zo, side):
        count, lo = split(side)
        yd_copy(zo, side).wait_recv()
        add(zo, 1, lambda i: YD[zo, i].astype(f32), lo, count - lo)
        x_copy(zo, side).start()
        xd_copy(zo, side).wait_recv()
        add(zo, 2, lambda i: XD[zo, i].astype(f32), 0, lo)
        y_copy(zo, side).start()

    def phase_three(zo, side):
        x_copy(zo, side).wait_recv()
        y_copy(zo, side).wait_recv()
        add(zo, 0, lambda i: X[zo, i].astype(f32) + Y[zo, i].astype(f32), 0, split(side)[0])
        if is_own(side):
            return
        if side == -1:
            @pl.when(net.has_dn)
            def _():
                z_copy(zo, 0).wait_recv()
                add(zo, 0, lambda i: Z[zo, 0, i].astype(f32))

            z_copy(zo, 0).start()
        else:
            @pl.when(net.has_up)
            def _():
                z_copy(zo, 1).wait_recv()
                add(zo, 0, lambda i: Z[zo, 1, i].astype(f32))

            z_copy(zo, 1).start()

    la[0] = local_ref[...]
    sa[0] = shared_ref[...]
    v_start(0)
    for copy in loads(TB, 1 - c):
        copy.wait()
    each(nz - 1, begin)
    for copy in loads(TA, c):
        copy.wait()
    each(nz - 1, begin_own)
    for turn_no in range(nz + 2):
        if turn_no + 1 < nz:
            each(nz - 2 - turn_no, begin)
        if turn_no < nz:
            each(nz - 1 - turn_no, phase_one)
        if turn_no + 1 < nz:
            each(nz - 2 - turn_no, begin_own)
        if turn_no == 0:
            dx_copy.start()
        if 0 <= turn_no - 1 < nz:
            each(nz - turn_no, phase_two)
        if 0 <= turn_no - 2:
            each(nz + 1 - turn_no, phase_three)
        if turn_no < 5:
            v_finish(turn_no)
            if turn_no < 4:
                v_start(turn_no + 1)
    local_o[...] = la[5]
    shared_o[...] = sa[5]
    dx_copy.wait_recv()

    def join(r, _):
        at = pl.ds(pl.multiple_of(r * 128, 128), 128)
        dx_o[at, :] = own_ref[at, :] + dx_in[at, :].astype(f32)
        return 0

    lax.fori_loop(0, own_ref.shape[0] // 128, join, 0)

    @pl.when(net.has_dn)
    def _():
        z_copy(z, 0).wait_recv()

    @pl.when(net.has_up)
    def _():
        z_copy(z, 1).wait_recv()

    def finish(i, _):
        total = A[z, 0, i].astype(f32)
        total = total + jnp.where(net.has_dn, Z[z, 0, i].astype(f32), 0.0)
        total = total + jnp.where(net.has_up, Z[z, 1, i].astype(f32), 0.0)
        j = part_of(m, order_ref[d * full + i])
        tile = jnp.concatenate([total, rest_of(total, free_of(j))], 0)
        tile_o[i] = turned(tile, j, -1)
        return 0

    lax.fori_loop(0, full, finish, 0)

    def sent(zo, side):
        for kind in range(4):
            c_copy(zo, kind).wait_send()
        xd_copy(zo, side).wait_send()
        yd_copy(zo, side).wait_send()
        x_copy(zo, side).wait_send()
        y_copy(zo, side).wait_send()
        if is_own(side):
            return
        z_copy(zo, 0).wait_send()
        for copy in late_copies(zo, 0):
            copy.wait_send()

    for step in range(nz):
        each(step, sent)
    dx_copy.wait_send()
    for k in range(5):
        for copy in v_copies(k):
            copy.wait_send()


def scatter_grads(nz, order, parts, own, other, local, shared):
    dma = pltpu.SemaphoreType.DMA
    vm = pl.BlockSpec(memory_space=pltpu.VMEM)
    block = lambda *lead: pltpu.VMEM((*lead, 72, 128), bf16)
    anywhere = pl.BlockSpec(memory_space=pl.ANY)
    return pl.pallas_call(
        functools.partial(scatter_kernel, nz),
        out_shape=[
            jax.ShapeDtypeStruct((24, 96, 128), f32),
            jax.ShapeDtypeStruct(own.shape, f32),
            jax.ShapeDtypeStruct(local.shape, f32),
            jax.ShapeDtypeStruct(shared.shape, f32),
        ],
        in_specs=[pl.BlockSpec(memory_space=pltpu.SMEM)] + [anywhere] * 4 + [vm] * 4,
        out_specs=[vm] * 4,
        scratch_shapes=[
            block(2, 48 * nz), block(2, 48 * nz), block(nz, 4, 24), block(nz, 4, 24), block(nz, 4, 24),
            block(nz, 12), block(nz, 12), block(nz, 24), block(nz, 24), block(nz, 2, 24),
            block(nz, 2, 3, 5), pltpu.VMEM(other.shape, bf16),
            pltpu.VMEM((6, *local.shape), f32), pltpu.VMEM((5, *local.shape), f32),
            pltpu.VMEM((6, *shared.shape), f32), pltpu.VMEM((5, *shared.shape), f32),
            dma((4, 4)), dma((nz, 4)), dma((nz, 4)),
        ]
        + [dma((nz,))] * 9
        + [dma((nz, 2)), dma((nz, 3)), dma((nz, 2, 3)), dma((2,)), dma((5, 2)), dma((5, 2))],
        compiler_params=pltpu.CompilerParams(
            collective_id=1, has_side_effects=True, vmem_limit_bytes=60 << 20
        ),
        name="scatter_grads",
    )(order, *parts, own, other, local, shared)


STEP = 5
BETA_ONE = 0.5
BETA_TWO = 0.5
ADAM_EPS = 1e-08
RATE_TILES = 0.04
RATE_VECTORS = 0.2
DECAY = 0.01


def adam(grad, first, second):
    first_new = BETA_ONE * first + (1.0 - BETA_ONE) * grad
    second_new = BETA_TWO * second + (1.0 - BETA_TWO) * grad * grad
    step_dir = (
        first_new
        / (1.0 - BETA_ONE**STEP)
        / (jnp.sqrt(second_new / (1.0 - BETA_TWO**STEP)) + ADAM_EPS)
    )
    return (first_new, second_new, step_dir)


def update_kernel(
    grad_ref, first_ref, second_ref, left_ref, right_ref, master_ref,
    lg_ref, lv_ref, lf_ref, ls_ref, sg_ref, sv_ref, sf_ref, ss_ref,
    o_grad, o_first, o_second, o_weight, o_lg, o_lf, o_ls, o_lv, o_sg, o_sf, o_ss, o_sv,
):
    @pl.when(pl.program_id(0) == 0)
    def _():
        local = lg_ref[lax.axis_index("mp")]
        first, second, step_dir = adam(local, lf_ref[...], ls_ref[...])
        o_lg[...] = local
        o_lf[...] = first
        o_ls[...] = second
        o_lv[...] = lv_ref[...] - RATE_VECTORS * step_dir
        shared = sg_ref[...]
        first, second, step_dir = adam(shared, sf_ref[...], ss_ref[...])
        o_sg[...] = shared
        o_sf[...] = first
        o_ss[...] = second
        o_sv[...] = sv_ref[...] - RATE_VECTORS * step_dir

    every = range(grad_ref.shape[0])
    edge = left_ref.shape[-1]
    left = [left_ref[i].astype(bf16) for i in every]
    right = [right_ref[i].astype(bf16) for i in every]
    for i in every:
        o_grad[i] = grad_ref[i][:, :edge]
    half = [nn(grad_ref[i][:, :edge].astype(bf16), right[i]).astype(bf16) for i in every]
    rotated = [tn(left[i], half[i]) for i in every]
    moved = [adam(rotated[i], first_ref[i], second_ref[i]) for i in every]
    for i in every:
        o_first[i] = moved[i][0]
        o_second[i] = moved[i][1]
    half = [nn(left[i], moved[i][2].astype(bf16)).astype(bf16) for i in every]
    for i in every:
        turn_back = nt(half[i], right[i])
        master = master_ref[i]
        o_weight[i] = master - RATE_TILES * (turn_back + DECAY * master)


def update(grad, first, second, left, right, master, local, shared):
    count, edge, wide = grad.shape
    part = 6 if count % 6 == 0 else count
    tile = lambda w: pl.BlockSpec((part, edge, w), lambda i: (i, 0, 0))
    whole = lambda v: pl.BlockSpec(v.shape, lambda i: (0,) * v.ndim)
    out = lambda v: jax.ShapeDtypeStruct(v.shape, f32)
    return pl.pallas_call(
        update_kernel,
        grid=(count // part,),
        in_specs=[tile(wide)] + [tile(edge)] * 5 + [whole(v) for v in (*local, *shared)],
        out_specs=[tile(edge)] * 4 + [whole(local[1])] * 4 + [whole(shared[1])] * 4,
        out_shape=[out(first)] * 4 + [out(local[1])] * 4 + [out(shared[1])] * 4,
        compiler_params=pltpu.CompilerParams(vmem_limit_bytes=58 << 20),
        name="update",
    )(grad, first, second, left, right, master, *local, *shared)


def from_tiles(tile_set, row_count, col_count):
    edge = tile_set.shape[-1]
    return (
        tile_set.reshape(row_count // edge, col_count // edge, edge, edge)
        .transpose(0, 2, 1, 3)
        .reshape(row_count, col_count)
    )


def plain_weights(tile_order, master, local):
    tiles = lax.all_gather(master.astype(bf16), "dp", axis=0, tiled=True)
    tiles = lax.all_gather(tiles, "mp", axis=0)
    count = tile_order.shape[0]
    inverse = jnp.zeros((count,), jnp.int32).at[tile_order].set(jnp.arange(count, dtype=jnp.int32))
    natural = tiles[:, inverse]
    dense = []
    for rows, cols, where in GRIDS:
        pieces = []
        for r in range(rows):
            pick = [where(r, j) for j in range(cols)]
            groups = jnp.asarray([p for p, _ in pick], jnp.int32)
            numbers = jnp.asarray([n for _, n in pick], jnp.int32)
            pieces.append(natural[groups, numbers].transpose(1, 0, 2).reshape(96, cols * 96))
        dense.append(jnp.concatenate(pieces, 0))
    return (*dense, lax.all_gather(local, "mp", axis=0))


def plain_scatter(order, parts, own, other, local, shared):
    tiles = jnp.concatenate(parts, 1)[:, order]
    mine = lax.psum_scatter(tiles, "mp", scatter_dimension=0, tiled=False).astype(f32)
    turns = part_of(lax.axis_index("mp"), order)[:, None, None]
    back = mine
    for k in range(1, 4):
        back = jnp.where(turns == k, jnp.roll(mine, -96 * k, -1), back)
    rest = back[..., 96:].reshape(-1, 3, 24, 32).transpose(0, 2, 1, 3).reshape(-1, 24, 96)
    tiles = jnp.concatenate([back[..., :96], rest], 1)
    owned = lax.psum_scatter(tiles, "dp", scatter_dimension=0, tiled=True)
    count = lax.axis_size("mp")
    swapped = lax.ppermute(other, "mp", [(i, i ^ 1) for i in range(count)])
    local_sum, shared_sum = lax.psum((local, shared), ("dp", "mp"))
    return owned, own + swapped.astype(f32), local_sum, shared_sum


def shards(
    tokens,
    cotangent,
    lengths,
    tile_order,
    master,
    first_moment,
    second_moment,
    basis_left,
    basis_right,
    local_vec,
    local_first,
    local_second,
    shared_vec,
    shared_first,
    shared_second,
):
    group_count = lax.axis_size("mp")
    group_index = lax.axis_index("mp")
    owners = lax.axis_size("dp")
    row_total, width = tokens.shape
    rows = row_total // group_count
    per_owner = master.shape[1]
    nz = owners // 2
    routed = per_owner == 24 and nz == 4 and group_count == 4

    if routed:
        w_qkv, w_out, w_up, w_down, vectors = gather_weights(
            nz, tile_order, slot_of_tile(tile_order), master[0], local_vec
        )
    else:
        w_qkv, w_out, w_up, w_down, vectors = plain_weights(tile_order, master[0], local_vec)
    output, tq, to, tu, td, own, other, local_terms, shared_terms = layer(
        tokens, cotangent, lengths, vectors, shared_vec, w_qkv, w_out, w_up, w_down, rows
    )
    parts = [t.reshape(group_count, -1, 72, 128) for t in (tq, to, tu, td)]
    if routed:
        owned, input_grad, local_sum, shared_grad = scatter_grads(
            nz, tile_order, parts, own, other, local_terms, shared_terms
        )
    else:
        owned, input_grad, local_sum, shared_grad = plain_scatter(
            tile_order, parts, own, other, local_terms, shared_terms
        )
    tiles = update(
        owned, first_moment[0], second_moment[0], basis_left[0], basis_right[0], master[0],
        (local_sum, local_vec, local_first, local_second),
        (shared_grad, shared_vec, shared_first, shared_second),
    )
    return (output, input_grad, *(t[None] for t in tiles[:4]), *tiles[4:])


def solution(mesh):
    placed = (
        P("dp", None),
        P("dp", None),
        P("dp"),
        P(),
        P("mp", "dp", None, None),
        P("mp", "dp", None, None),
        P("mp", "dp", None, None),
        P("mp", "dp", None, None),
        P("mp", "dp", None, None),
        P("mp", None),
        P("mp", None),
        P("mp", None),
        P(),
        P(),
        P(),
    )
    return jax.shard_map(
        shards,
        mesh=mesh,
        in_specs=placed,
        out_specs=(
            P(("dp", "mp"), None),
            P(("dp", "mp"), None),
            P("mp", "dp", None, None),
            P("mp", "dp", None, None),
            P("mp", "dp", None, None),
            P("mp", "dp", None, None),
            P("mp", None),
            P("mp", None),
            P("mp", None),
            P("mp", None),
            P(),
            P(),
            P(),
            P(),
        ),
        check_vma=False,
    )
```

```python
import functools
import jax
import jax.numpy as jnp
from jax import lax
from jax.experimental import pallas as pl
from jax.experimental.pallas import tpu as pltpu
from jax.sharding import PartitionSpec as P

MESH = pl.DeviceIdType.MESH
f32 = jnp.float32
bf16 = jnp.bfloat16


def lanes_of(shape):
    return lax.broadcasted_iota(jnp.int32, shape, len(shape) - 1)


def turn(v, amount):
    return pltpu.roll(v, amount, v.ndim - 1)


def free_of(j):
    return (3 * j + 3) % 4


def part_of(group, number):
    return jnp.where(number < 48, 2 * group + number % 2, number) % 4


def groups_of(shape):
    return lanes_of(shape) // 32


def to_wire(tile, free):
    rest = tile[72:96]
    side = jnp.concatenate([turn(rest, 96), turn(rest, 64), turn(rest, 32)], 0)
    return jnp.where(groups_of(side.shape) == free, side, tile[:72])


def rest_of(wire, free):
    group = groups_of((24, 128))
    first, second, third = turn(wire[:24], 32), turn(wire[24:48], 64), turn(wire[48:72], 96)
    return jnp.where(
        group == (free + 1) % 4, first, jnp.where(group == (free + 2) % 4, second, third)
    )


def turned(tile, j, sign):
    out = tile
    for k in range(1, 4):
        out = jnp.where(j == k, turn(tile, sign * 96 * k % 128), out)
    return out


def join_four(wires):
    lane, group = lanes_of((72, 128)), groups_of((24, 128))
    a, b, c, d = wires
    tops = [jnp.where(lane < 96, a, b), jnp.where(lane < 64, b, c), jnp.where(lane < 32, c, d)]
    rests = []
    for i in range(3):
        at = slice(24 * i, 24 * i + 24)
        mixed = jnp.where(
            group == 3, a[at], jnp.where(group == 2, b[at], jnp.where(group == 1, c[at], d[at]))
        )
        rests.append(turn(mixed, 32 * (i + 1)))
    pieces = []
    for k in range(3):
        index = (group + k) % 3
        rest = jnp.where(index == 0, rests[0], jnp.where(index == 1, rests[1], rests[2]))
        pieces.append(jnp.concatenate([tops[k], rest], 0))
    return pieces


def split_four(pieces):
    lane, group = lanes_of((72, 128)), groups_of((24, 128))
    a, b, c = (p[:72] for p in pieces)
    rests = [p[72:] for p in pieces]
    sides = []
    for i in range(3):
        mixed = jnp.where(
            group % 3 == 0,
            rests[i],
            jnp.where(group == 1, rests[(i - 1) % 3], rests[(i - 2) % 3]),
        )
        sides.append(turn(mixed, 96 - 32 * i))
    side = jnp.concatenate(sides, 0)
    tops = [a, jnp.where(lane < 64, b, a), jnp.where(lane < 32, c, b), c]
    return [jnp.where(lane // 32 == 3 - t, side, tops[t]) for t in range(4)]


def place():
    d, m = lax.axis_index("dp"), lax.axis_index("mp")
    return d // 2, d % 2, m // 2, m % 2


class Net:
    def __init__(self, nz):
        self.nz = nz
        self.z, self.x, self.y, self.c = place()
        self.d = self.z * 2 + self.x
        self.m = self.y * 2 + self.c
        self.xn = (self.z * 2 + 1 - self.x, self.m)
        self.yn = (self.d, (1 - self.y) * 2 + self.c)
        self.cn = (self.d, self.y * 2 + 1 - self.c)
        self.up = (self.d + 2, self.m)
        self.dn = (self.d - 2, self.m)
        self.has_up = self.z < nz - 1
        self.has_dn = self.z > 0

    def peers(self):
        others = [(lax.rem(self.z + k, self.nz) * 2 + self.x, self.m) for k in range(1, self.nz)]
        return [self.xn, self.yn, self.cn] + others

    def greet(self):
        for peer in self.peers():
            pl.semaphore_signal(
                pltpu.get_barrier_semaphore(), inc=1, device_id=peer, device_id_type=MESH
            )

    def await_all(self):
        pl.semaphore_wait(pltpu.get_barrier_semaphore(), len(self.peers()))


def send(src, dst, ss, rs, peer):
    return pltpu.make_async_remote_copy(
        src_ref=src, dst_ref=dst, send_sem=ss, recv_sem=rs, device_id=peer, device_id_type=MESH
    )


def tile_qkv(r, j):
    return (j % 8) // 2, r * 6 + (j // 8) * 2 + j % 2


def tile_out(r, j):
    return r // 2, 48 + (r % 2) * 8 + j


def tile_up(r, j):
    return j // 8, 64 + r * 8 + j % 8


def tile_down(r, j):
    return r // 8, 128 + (r % 8) * 8 + j


GRIDS = ((8, 24, tile_qkv), (8, 8, tile_out), (8, 32, tile_up), (32, 8, tile_down))


CHUNKS = ((24, 4),)


def is_own(side):
    return isinstance(side, int) and side == 0


def each(net, step, fn):
    if step == 0:
        fn(net.z, 0)
        return

    @pl.when(net.z >= step)
    def _():
        fn(net.z - step, 1)

    @pl.when(net.z + step < net.nz)
    def _():
        fn(net.z + step, -1)


class Part:
    def __init__(self, net, kinds, index, sems):
        self.net, self.kinds, self.index, self.sems = net, kinds, index, sems
        self.size, self.late = CHUNKS[index]
        self.base = sum(n for n, _ in CHUNKS[:index])
        self.early = self.size - self.late

    def sem(self, i, *at):
        return self.sems[i].at[(self.index, *at)]

    def split(self, side):
        count = self.size if is_own(side) else self.early
        return count, (count + self.index % 2) // 2


class GatherPart(Part):
    def __init__(self, net, kinds, index, G, sems):
        super().__init__(net, kinds, index, sems)
        self.G = G

    def slot(self, kind, zo, lo=0, n=None, shift=0):
        mo, xo = self.kinds[kind]
        n = self.size if n is None else n
        return self.G.at[mo + shift, pl.ds((zo * 2 + xo) * 24 + self.base + lo, n)]

    def go(self, s, i, i_at, j, j_at, peer):
        return send(s, s, self.sem(i, *i_at), self.sem(j, *j_at), peer)

    def toward(self, direction):
        return self.net.up if direction == 0 else self.net.dn

    def z_copy(self, zo, direction):
        return self.go(self.slot(0, zo), 0, (zo, direction), 1, (zo,), self.toward(direction))

    def late_copies(self, zo, direction):
        for k in range(3):
            s = self.slot(k + 1, zo, self.early, self.late)
            yield self.go(s, 12, (zo, k, direction), 13, (zo, k), self.toward(direction))

    def c_copy(self, zo, kind, side, shift=0):
        n = self.size if kind == 0 or is_own(side) else self.early
        return self.go(self.slot(kind, zo, 0, n, shift), 10, (zo, kind), 11, (zo, kind), self.net.cn)

    def c_late(self, zo, k, shift=0):
        s = self.slot(k + 1, zo, self.early, self.late, shift)
        return self.go(s, 14, (zo, k), 15, (zo, k), self.net.cn)

    def x_copy(self, zo, kind, side):
        return self.go(self.slot(kind, zo, 0, self.split(side)[0]), 2, (zo,), 3, (zo,), self.net.xn)

    def y_copy(self, zo, kind, side):
        return self.go(self.slot(kind, zo, 0, self.split(side)[0]), 4, (zo,), 5, (zo,), self.net.yn)

    def xd_copy(self, zo, kind, side):
        return self.go(self.slot(kind, zo, 0, self.split(side)[1]), 6, (zo,), 7, (zo,), self.net.xn)

    def yd_copy(self, zo, kind, side):
        count, lo = self.split(side)
        return self.go(self.slot(kind, zo, lo, count - lo), 8, (zo,), 9, (zo,), self.net.yn)

    def onward(self, side, act):
        if is_own(side) or side == 1:
            pl.when(self.net.has_up)(lambda: act(0))
        if is_own(side) or side == -1:
            pl.when(self.net.has_dn)(lambda: act(1))

    def arrive(self, zo, side):
        if not is_own(side):
            self.z_copy(zo, 0).wait_recv()
        self.onward(side, lambda direction: self.z_copy(zo, direction).start())
        self.x_copy(zo, 0, side).start()
        self.y_copy(zo, 0, side).start()
        self.c_copy(zo, 0, side).start()

    def diag(self, zo, side):
        self.x_copy(zo, 1, side).wait_recv()
        self.yd_copy(zo, 1, side).start()
        self.c_copy(zo, 1, side).start()
        self.y_copy(zo, 2, side).wait_recv()
        self.xd_copy(zo, 2, side).start()
        self.c_copy(zo, 2, side).start()

    def fin(self, zo, side):
        self.xd_copy(zo, 3, side).wait_recv()
        self.yd_copy(zo, 3, side).wait_recv()
        self.c_copy(zo, 3, side).start()

    def last(self, zo, side):
        if not is_own(side):
            for copy in self.late_copies(zo, 0):
                copy.wait_recv()

        def act(direction):
            for copy in self.late_copies(zo, direction):
                copy.start()

        self.onward(side, act)
        if not is_own(side):
            for k in range(3):
                self.c_late(zo, k).start()

    def other_core(self, zo, side):
        flip = 1 - 2 * self.net.c
        for kind in range(4):
            self.c_copy(zo, kind, side, flip).wait_recv()
            if kind and not is_own(side):
                self.c_late(zo, kind - 1, flip).wait_recv()

    def sent(self, zo, side):
        self.x_copy(zo, 0, side).wait_send()
        self.y_copy(zo, 0, side).wait_send()
        self.yd_copy(zo, 1, side).wait_send()
        self.xd_copy(zo, 2, side).wait_send()
        for kind in range(4):
            self.c_copy(zo, kind, side).wait_send()
        if not is_own(side):
            for k in range(3):
                self.c_late(zo, k).wait_send()

        def done(direction):
            self.z_copy(zo, direction).wait_send()
            for copy in self.late_copies(zo, direction):
                copy.wait_send()

        self.onward(side, done)


def gather_kernel(
    nz, order_ref, src_ref, master_ref, local_ref, o_qkv, o_out, o_up, o_down, o_local,
    G, LV, d_qkv, d_out, d_up, d_down,
    outs, lvs, lvr, *sems,
):
    net = Net(nz)
    z, x, y, c, m = net.z, net.x, net.y, net.c, net.m
    my = (1 - y) * 2 + c
    full = 24
    net.greet()

    def stage(i, _):
        tile = jnp.concatenate([master_ref[i], jnp.zeros((96, 32), f32)], axis=-1)
        j = part_of(m, order_ref[net.d * full + i])
        tile = turned(tile, j, 1)
        G[m, net.d * full + i] = to_wire(tile, free_of(j)).astype(bf16)
        return 0

    lax.fori_loop(0, full, stage, 0)
    LV[m] = local_ref[...]
    net.await_all()
    lv_y = send(LV.at[m], LV.at[m], lvs.at[0], lvr.at[0], net.yn)
    lv_c = send(LV.at[m], LV.at[m], lvs.at[1], lvr.at[1], net.cn)
    lv_d = send(LV.at[my], LV.at[my], lvs.at[2], lvr.at[2], net.cn)

    kinds = ((m, x), (m, 1 - x), (my, x), (my, 1 - x))
    flip = 1 - 2 * c
    parts = [GatherPart(net, kinds, i, G, sems) for i in range(len(CHUNKS))]

    def step_of(distance, name, reverse=False):
        def run(zo, side):
            for part in parts:
                getattr(part, name)(zo, side)

        each(net, distance, run)

    def forwarded(zo, side):
        for part in parts:
            part.other_core(zo, side)

    step_of(0, "arrive")
    lv_y.start()
    lv_c.start()
    step_of(1, "arrive")
    step_of(0, "diag")
    send(LV.at[my], LV.at[my], lvs.at[0], lvr.at[0], net.yn).wait_recv()
    lv_d.start()
    step_of(2, "arrive")
    step_of(1, "diag")
    step_of(0, "fin")
    step_of(0, "last")
    step_of(3, "arrive")
    step_of(1, "fin")
    step_of(1, "last")
    step_of(2, "diag")
    step_of(2, "last")
    step_of(2, "fin")
    step_of(3, "diag")
    step_of(3, "last")
    step_of(3, "fin")
    for step in range(nz):
        step_of(step, "other_core")
    mc = m + flip
    send(LV.at[mc], LV.at[mc], lvs.at[1], lvr.at[1], net.cn).wait_recv()
    mc = my + flip
    send(LV.at[mc], LV.at[mc], lvs.at[2], lvr.at[2], net.cn).wait_recv()
    o_local[...] = LV[...]

    copies = []
    for i, ((rows, cols, where), dense, out) in enumerate(
        zip(GRIDS, (d_qkv, d_out, d_up, d_down), (o_qkv, o_out, o_up, o_down))
    ):
        def fill(r, _):
            for g in range(cols // 4):
                tiles = []
                for t in range(4):
                    p, n = where(r, 4 * g + t)
                    tiles.append(G[p, src_ref[n]].astype(f32))
                for k, piece in enumerate(join_four(tiles)):
                    dense[pl.ds(pl.multiple_of(r * 96, 96), 96), pl.ds(384 * g + 128 * k, 128)] = (
                        piece.astype(bf16)
                    )
            return 0

        lax.fori_loop(0, rows, fill, 0)
        copy = pltpu.make_async_copy(dense, out, outs.at[i])
        copy.start()
        copies.append(copy)

    for step in range(nz):
        step_of(step, "sent")
    lv_y.wait_send()
    lv_c.wait_send()
    lv_d.wait_send()
    for copy in copies:
        copy.wait()


def gather_weights(nz, order, src, master, local):
    dma = pltpu.SemaphoreType.DMA
    shapes = [(r * 96, c * 96) for r, c, _ in GRIDS]
    return pl.pallas_call(
        functools.partial(gather_kernel, nz),
        out_shape=[jax.ShapeDtypeStruct(s, bf16) for s in shapes]
        + [jax.ShapeDtypeStruct((4, *local.shape), f32)],
        in_specs=[pl.BlockSpec(memory_space=pltpu.SMEM)] * 2
        + [pl.BlockSpec(memory_space=pltpu.VMEM)] * 2,
        out_specs=[pl.BlockSpec(memory_space=pl.ANY)] * 4 + [pl.BlockSpec(memory_space=pltpu.VMEM)],
        scratch_shapes=[pltpu.VMEM((4, 2 * nz * 24, 72, 128), bf16), pltpu.VMEM((4, *local.shape), f32)]
        + [pltpu.VMEM(s, bf16) for s in shapes]
        + [dma((4,)), dma((3,)), dma((3,))]
        + [dma((len(CHUNKS), nz, *tail)) for tail in ((2,), (), *([()] * 8), (4,), (4,), (3, 2), (3,), (3,), (3,))],
        compiler_params=pltpu.CompilerParams(
            collective_id=0, has_side_effects=True, vmem_limit_bytes=56 << 20
        ),
        name="gather_weights",
    )(order, src, master, local)


def slot_of_tile(tile_order):
    count = tile_order.shape[0]
    slots = jnp.arange(count, dtype=jnp.int32)
    return jnp.sum(jnp.where(tile_order[None, :] == slots[:, None], slots[None, :], 0), 1)


NEG_BIG = -1e30
NORM_EPS = 1e-05
ROOT_HALF = 0.7071067811865476
PHI_SCALE = 0.3989422804014327


def nt(a, b):
    return lax.dot_general(a, b, (((1,), (1,)), ((), ())), preferred_element_type=f32)


def tn(a, b):
    return lax.dot_general(a, b, (((0,), (0,)), ((), ())), preferred_element_type=f32)


def nn(a, b):
    return jnp.dot(a, b, preferred_element_type=f32)


def standard(values):
    centre = values - jnp.mean(values, -1, keepdims=True)
    scale = lax.rsqrt(jnp.mean(centre * centre, -1, keepdims=True) + NORM_EPS)
    return centre * scale, scale


def standard_back(grad, normed, scale, gain):
    inner = grad * gain
    return scale * (
        inner - jnp.mean(inner, -1, keepdims=True) - normed * jnp.mean(inner * normed, -1, keepdims=True)
    )


def col_sum(values):
    return jnp.sum(values, 0, keepdims=True)


def layer_kernel(
    tokens_ref, cot_ref, lengths_ref, vec_ref, sv_ref, wq_ref, wo_ref, wu_ref, wd_ref,
    out_ref, tq_ref, to_ref, tu_ref, td_ref, own_ref, other_ref, dl_ref, ds_ref,
    x, cot, wqkv, wout, wup, wdown, bias, q, k, v, probs, o_t, hid, low, low_t, n_one, r_one, acc,
    act, slope, g_low, g_o, dq, dk, dv, x_t, out, other, su, sd, sq, loads, stores, su_sem, sd_sem, sq_sem,
):
    rows, width = q.shape
    seq_len = k.shape[0]
    chunks, _, cut = act.shape
    tiles = width // 96
    pairs = width // 128
    piece = 512
    zero = jnp.zeros((), bf16)
    member = lax.axis_index("mp")
    share = seq_len // rows
    seq, part = member // share, member % share
    length = lengths_ref[seq]
    bound = 64 * ((length + 127) // 128)
    start_b = pl.multiple_of(bound, 64)
    here = pl.ds(pl.multiple_of(part * rows, rows), rows)
    there = pl.ds(pl.multiple_of((1 - part) * rows, rows), rows)

    def load(src, dst, i):
        copy = pltpu.make_async_copy(src, dst, loads.at[i])
        copy.start()
        return copy

    get_x = load(tokens_ref.at[pl.ds(pl.multiple_of(seq * seq_len, seq_len), seq_len)], x, 0)
    get_q = load(wq_ref, wqkv, 1)
    get_o = load(wo_ref, wout, 2)
    get_u = load(wu_ref, wup, 3)
    get_d = load(wd_ref, wdown, 4)
    get_c = load(cot_ref.at[pl.ds(pl.multiple_of(member * rows, rows), rows)], cot, 5)

    groups = vec_ref.shape[0]
    third = width // groups
    bias[:, :width] = jnp.concatenate([vec_ref[p][:, :third] for p in range(groups)], 1)
    bias[:, width:] = jnp.concatenate([vec_ref[p][:, third : 2 * third] for p in range(groups)], 1)

    get_x.wait()
    get_q.wait()
    for lo in range(0, width, 256):
        got = nn(x[here, :], wqkv[:, lo : lo + 256]) + bias[:, lo : lo + 256]
        q[:, lo : lo + 256] = got.astype(bf16) * jnp.asarray(0.125, bf16)

    def project(r, _):
        at = pl.ds(pl.multiple_of(r * rows, rows), rows)
        for lo in range(0, width, 256):
            k[at, lo : lo + 256] = nn(x[at, :], wqkv[:, width + lo : width + lo + 256]).astype(bf16)
            got = nn(x[at, :], wqkv[:, 2 * width + lo : 2 * width + lo + 256])
            v[at, lo : lo + 256] = (got + bias[:, width + lo : width + lo + 256]).astype(bf16)
        return 0

    lax.fori_loop(0, share, project, 0, unroll=True)

    def picks(shape, rows_at):
        row = lax.broadcasted_iota(jnp.int32, shape, rows_at) + part * rows
        lane = lax.broadcasted_iota(jnp.int32, shape, 1 - rows_at)
        return (row < bound) == (lane < 64)

    windows = ((0, bound), (start_b, length - bound))

    def forward(pair, _):
        cols = pl.ds(pl.multiple_of(pair * 128, 128), 128)
        queries = q[:, cols]
        pick = picks((rows, 128), 0)
        mine = (jnp.where(pick, queries, zero), jnp.where(pick, zero, queries))
        scores = [nt(k[pl.ds(start, rows), cols], mine[w]) for w, (start, _) in enumerate(windows)]
        outs = []
        for w, (start, limit) in enumerate(windows):
            inside = lax.broadcasted_iota(jnp.int32, scores[w].shape, 0) < limit
            masked = jnp.where(inside, scores[w], NEG_BIG)
            weight = jnp.exp(masked - jnp.max(masked, 0, keepdims=True))
            low_probs = (weight * (1.0 / jnp.sum(weight, 0, keepdims=True))).astype(bf16)
            probs[2 * pair + w] = low_probs
            outs.append(tn(v[pl.ds(start, rows), cols], low_probs))
        o_t[cols, :] = jnp.where(picks((128, rows), 1), outs[0], outs[1]).astype(bf16)
        return 0

    lax.fori_loop(0, pairs, forward, 0, unroll=2)

    def by_rows(fn):
        def body(r, _):
            fn(pl.ds(pl.multiple_of(r * piece, piece), piece), r)
            return 0

        lax.fori_loop(0, rows // piece, body, 0)

    get_o.wait()
    acc[...] = tn(o_t[...], wout[...])

    def norm_one(at, r):
        mine = pl.ds(pl.multiple_of(part * rows + r * piece, piece), piece)
        z_one = x[mine, :].astype(f32) + acc[at, :] + sv_ref[0:1, :]
        normed, scale = standard(z_one)
        hidden = normed * sv_ref[2:3, :] + sv_ref[3:4, :]
        n_one[at, :] = normed
        r_one[at, :] = jnp.broadcast_to(scale, (piece, 128))
        hid[at, :] = hidden
        low[at, :] = hidden.astype(bf16)
        acc[at, :] = jnp.zeros((piece, width), f32)

    by_rows(norm_one)
    low_t[...] = low[...].T
    get_u.wait()
    get_d.wait()

    def feed(i, _):
        at = pl.ds(pl.multiple_of(i * cut, cut), cut)
        pre = nn(low[...], wup[:, at]) + vec_ref[i, :, 2 * third :]
        phi = 0.5 * (1.0 + lax.erf(pre * ROOT_HALF))
        density = jnp.exp(-0.5 * pre * pre) * PHI_SCALE
        active = (pre * phi).astype(bf16)
        act[i] = active
        slope[i] = (phi + pre * density).astype(bf16)
        acc[...] += nn(active, wdown[at, :])
        return 0

    lax.fori_loop(0, chunks, feed, 0, unroll=4)
    get_c.wait()
    ds_ref[...] = jnp.zeros_like(ds_ref)

    def norm_two(at, r):
        z_two = hid[at, :] + acc[at, :] + sv_ref[1:2, :]
        normed, scale = standard(z_two)
        row = lax.broadcasted_iota(jnp.int32, (piece, 1), 0) + part * rows + r * piece
        valid = (row < length).astype(f32)
        out[at, :] = ((normed * sv_ref[4:5, :] + sv_ref[5:6, :]) * valid).astype(bf16)
        grad = cot[at, :].astype(f32) * valid
        back = standard_back(grad, normed, scale, sv_ref[4:5, :])
        ds_ref[4:5, :] += col_sum(grad * normed)
        ds_ref[5:6, :] += col_sum(grad)
        ds_ref[1:2, :] += col_sum(back)
        g_low[at, :] = back.astype(bf16)
        acc[at, :] = back

    by_rows(norm_two)
    put_out = pltpu.make_async_copy(out, out_ref, stores.at[0])
    put_out.start()

    def put_u(i):
        return pltpu.make_async_copy(su.at[i % 2], tu_ref.at[i], su_sem.at[i % 2])

    def put_d(i):
        return pltpu.make_async_copy(sd.at[i % 2], td_ref.at[i], sd_sem.at[i % 2])

    def cut_up(grad, keep):
        for r in range(grad.shape[0] // 96):
            for g in range(grad.shape[1] // 384):
                pieces = [
                    grad[96 * r : 96 * r + 96, 384 * g + 128 * n : 384 * g + 128 * n + 128]
                    for n in range(3)
                ]
                for t, wire in enumerate(split_four(pieces)):
                    keep(r, 4 * g + t, wire.astype(bf16))

    def feed_back(i, _):
        at = pl.ds(pl.multiple_of(i * cut, cut), cut)

        @pl.when(i >= 2)
        def _():
            put_u(i - 2).wait()
            put_d(i - 2).wait()

        grad_low = (nt(g_low[...], wdown[at, :]) * slope[i].astype(f32)).astype(bf16)
        dl_ref[i, :, 2 * third :] = col_sum(grad_low.astype(f32))
        acc[...] += nt(grad_low, wup[:, at])

        def keep_down(r, j, wire):
            sd[i % 2, r * tiles + j] = wire

        def keep_up(r, j, wire):
            su[i % 2, r * tiles + j] = wire

        cut_up(tn(act[i], g_low[...]), keep_down)
        cut_up(nn(low_t[...], grad_low), keep_up)
        put_u(i).start()
        put_d(i).start()
        return 0

    lax.fori_loop(0, chunks, feed_back, 0)

    def norm_back(at, r):
        grad = acc[at, :]
        normed = n_one[at, :]
        back = standard_back(grad, normed, r_one[at, 0:1], sv_ref[2:3, :])
        ds_ref[2:3, :] += col_sum(grad * normed)
        ds_ref[3:4, :] += col_sum(grad)
        ds_ref[0:1, :] += col_sum(back)
        acc[at, :] = back
        g_low[at, :] = back.astype(bf16)

    by_rows(norm_back)
    g_o[...] = nt(g_low[...], wout[...]).astype(bf16)

    def keep_out(r, j, wire):
        sd[0, r * tiles + j] = wire

    put_d(chunks - 2).wait()
    cut_up(nn(o_t[...], g_low[...]), keep_out)
    put_o = pltpu.make_async_copy(sd.at[0], to_ref, stores.at[1])
    put_o.start()
    dk[...] = jnp.zeros_like(dk)
    dv[...] = jnp.zeros_like(dv)

    def backward(pair, _):
        cols = pl.ds(pl.multiple_of(pair * 128, 128), 128)
        pick, pick_t = picks((rows, 128), 0), picks((128, rows), 1)
        queries, grads = q[:, cols], g_o[:, cols]
        grads_t = grads.astype(f32).T
        inner = grads_t * o_t[cols, :].astype(f32)
        outs = []
        for w, (start, _) in enumerate(windows):
            at = pl.ds(start, rows)
            mine = (lambda a: jnp.where(pick, a, zero)) if w == 0 else (lambda a: jnp.where(pick, zero, a))
            mine_t = (lambda a: jnp.where(pick_t, a, 0.0)) if w == 0 else (lambda a: jnp.where(pick_t, 0.0, a))
            dot_sum = jnp.sum(mine_t(inner), 0, keepdims=True)
            grad_probs = nn(v[at, cols], mine_t(grads_t).astype(bf16))
            these = probs[2 * pair + w]
            grad_scores = (these.astype(f32) * (grad_probs - dot_sum)).astype(bf16)
            dv[at, cols] = nn(these, mine(grads)).astype(bf16)
            dk[at, cols] = nn(grad_scores, mine(queries)).astype(bf16)
            outs.append(tn(k[at, cols], grad_scores))
        dq[:, cols] = (jnp.where(pick_t, outs[0], outs[1]) * 0.125).T.astype(bf16)
        return 0

    lax.fori_loop(0, pairs, backward, 0, unroll=2)

    other[...] = (
        nt(dk[there, :], wqkv[:, width : 2 * width]) + nt(dv[there, :], wqkv[:, 2 * width :])
    ).astype(bf16)
    put_x = pltpu.make_async_copy(other, other_ref, stores.at[2])
    put_x.start()
    hid[...] = (
        acc[...]
        + nt(dq[...], wqkv[:, :width])
        + nt(dk[here, :], wqkv[:, width : 2 * width])
        + nt(dv[here, :], wqkv[:, 2 * width :])
    )
    put_own = pltpu.make_async_copy(hid, own_ref, stores.at[3])
    put_own.start()
    sum_q = col_sum(dq[...].astype(f32))
    sum_v = col_sum(dv[...].astype(f32))
    for p in range(groups):
        dl_ref[p, :, :third] = sum_q[:, third * p : third * p + third]
        dl_ref[p, :, third : 2 * third] = sum_v[:, third * p : third * p + third]

    x_t[...] = x[...].T
    puts = []
    for index, grad in enumerate((dk, dv, dq)):
        part_no = (1, 2, 0)[index]
        outer = nn(x_t[:, here] if part_no == 0 else x_t[...], grad[...])
        if index >= 2:
            puts[index - 2].wait()

        def keep(r, j, wire):
            sq[index % 2, j // 2, r, j % 2] = wire

        cut_up(outer, keep)
        put = pltpu.make_async_copy(sq.at[index % 2], tq_ref.at[:, :, part_no], sq_sem.at[index % 2])
        put.start()
        puts.append(put)
    for i in (chunks - 2, chunks - 1):
        put_u(i).wait()
    put_d(chunks - 1).wait()
    for put in (put_out, put_o, put_x, put_own, puts[-2], puts[-1]):
        put.wait()


def layer(tokens, cotangent, lengths, vectors, shared, w_qkv, w_out, w_up, w_down, rows):
    width = w_out.shape[0]
    hidden = w_up.shape[1]
    seq_len = tokens.shape[0] // lengths.shape[0]
    groups = vectors.shape[0]
    cut = hidden // groups
    chunks = groups
    tiles = width // 96
    anywhere = pl.BlockSpec(memory_space=pl.ANY)
    vm = pl.BlockSpec(memory_space=pltpu.VMEM)
    smem = pl.BlockSpec(memory_space=pltpu.SMEM)
    out = jax.ShapeDtypeStruct
    V = pltpu.VMEM
    dma = pltpu.SemaphoreType.DMA
    tall, wide, long = (rows, width), (width, rows), (seq_len, width)
    return pl.pallas_call(
        layer_kernel,
        in_specs=[anywhere, anywhere, smem, vm, vm] + [anywhere] * 4,
        out_specs=[anywhere] * 7 + [vm, vm],
        out_shape=[
            out(tall, bf16),
            out((groups, tiles, 3, 2, 72, 128), bf16),
            out((tiles * tiles, 72, 128), bf16),
            out((groups, cut // 96 * tiles, 72, 128), bf16),
            out((groups, cut // 96 * tiles, 72, 128), bf16),
            out(tall, f32),
            out(tall, bf16),
            out(vectors.shape, f32),
            out(shared.shape, f32),
        ],
        scratch_shapes=[
            V(long, bf16), V(tall, bf16), V(w_qkv.shape, bf16), V(w_out.shape, bf16), V(w_up.shape, bf16),
            V(w_down.shape, bf16), V((1, 2 * width), f32), V(tall, bf16), V(long, bf16), V(long, bf16),
            V((width // 64, rows, rows), bf16), V(wide, bf16), V(tall, f32), V(tall, bf16), V(wide, bf16),
            V(tall, f32), V((rows, 128), f32), V(tall, f32), V((chunks, rows, cut), bf16),
            V((chunks, rows, cut), bf16), V(tall, bf16), V(tall, bf16), V(tall, bf16), V(long, bf16),
            V(long, bf16), V((width, seq_len), bf16), V(tall, bf16), V(tall, bf16),
            V((2, cut // 96 * tiles, 72, 128), bf16), V((2, cut // 96 * tiles, 72, 128), bf16),
            V((2, groups, tiles, 2, 72, 128), bf16), dma((6,)), dma((4,)), dma((2,)), dma((2,)), dma((2,)),
        ],
        compiler_params=pltpu.CompilerParams(vmem_limit_bytes=60 << 20),
        name="layer",
    )(tokens, cotangent, lengths, vectors, shared, w_qkv, w_out, w_up, w_down)


class ScatterPart(Part):
    def __init__(self, net, kinds, index, order_ref, held, held_other, bufs, sems):
        super().__init__(net, kinds, index, sems)
        self.order_ref, self.held, self.held_other = order_ref, held, held_other
        self.S, self.A, self.R, self.XD, self.YD, self.X, self.Y, self.Z, self.ZX = bufs

    def at(self, ref, zo, kind, lo=0, n=None):
        return ref.at[zo, kind, pl.ds(self.base + lo, self.size if n is None else n)]

    def line(self, ref, zo, n):
        return ref.at[zo, pl.ds(self.base, n)]

    def toward(self, direction):
        return self.net.up if direction == 0 else self.net.dn

    def c_copy(self, zo, kind):
        return send(
            self.at(self.S, zo, kind), self.at(self.R, zo, kind),
            self.sem(0, zo, kind), self.sem(1, zo, kind), self.net.cn,
        )

    def xd_copy(self, zo, side):
        n = self.split(side)[1]
        return send(
            self.at(self.A, zo, 3, 0, n), self.line(self.XD, zo, n), self.sem(2, zo), self.sem(3, zo), self.net.xn
        )

    def yd_copy(self, zo, side):
        count, lo = self.split(side)
        n = count - lo
        return send(
            self.at(self.A, zo, 3, lo, n), self.line(self.YD, zo, n), self.sem(4, zo), self.sem(5, zo), self.net.yn
        )

    def x_copy(self, zo, side):
        n = self.split(side)[0]
        return send(
            self.at(self.A, zo, 1, 0, n), self.line(self.X, zo, n), self.sem(6, zo), self.sem(7, zo), self.net.xn
        )

    def y_copy(self, zo, side):
        n = self.split(side)[0]
        return send(
            self.at(self.A, zo, 2, 0, n), self.line(self.Y, zo, n), self.sem(8, zo), self.sem(9, zo), self.net.yn
        )

    def z_copy(self, zo, direction):
        return send(
            self.at(self.A, zo, 0), self.at(self.Z, zo, direction),
            self.sem(10, zo), self.sem(11, zo, direction), self.toward(direction),
        )

    def late_copies(self, zo, direction):
        first = sum(n for _, n in CHUNKS[: self.index])
        for k in range(3):
            yield send(
                self.at(self.A, zo, k + 1, self.early, self.late),
                self.ZX.at[zo, direction, k, pl.ds(first, self.late)],
                self.sem(12, zo, k), self.sem(13, zo, direction, k), self.toward(direction),
            )

    def place(self, zo, kind):
        mo, xo = self.kinds[kind]
        return mo // 2, (zo * 2 + xo) * 24

    def begin(self, zo, side):
        for kind in (3, 1, 2, 0):
            row, first = self.place(zo, kind)

            def one(i):
                self.S[zo, kind, i] = self.held_other[row, self.order_ref[first + i]]

            rounds(self.base, self.size, one)
            self.c_copy(zo, kind).start()

    def add(self, zo, kind, other, lo, n):
        def one(i):
            self.A[zo, kind, i] = self.A[zo, kind, i] + other(i)

        rounds(self.base + lo, n, one)

    def late_add(self, zo, direction):
        first = sum(n for _, n in CHUNKS[: self.index]) - self.base - self.early
        for k, copy in enumerate(self.late_copies(zo, direction)):
            copy.wait_recv()
            self.add(
                zo, k + 1, lambda i: self.ZX[zo, direction, k, i + first], self.early, self.late
            )

    def diagonal(self, zo, side):
        self.xd_copy(zo, side).start()
        self.yd_copy(zo, side).start()

    def one(self, zo, side):
        for kind in (3, 1, 2, 0):
            self.c_copy(zo, kind).wait_recv()
            row, first = self.place(zo, kind)

            def both(i):
                self.A[zo, kind, i] = self.held[row, self.order_ref[first + i]] + self.R[zo, kind, i]

            rounds(self.base, self.size, both)
            if kind == 3 and not is_own(side):
                self.diagonal(zo, side)
        if is_own(side) or side == -1:
            pl.when(self.net.has_dn)(lambda: self.late_add(zo, 0))
        if is_own(side) or side == 1:
            pl.when(self.net.has_up)(lambda: self.late_add(zo, 1))
        if is_own(side):
            self.diagonal(zo, side)
        else:
            for copy in self.late_copies(zo, 0 if side == -1 else 1):
                copy.start()

    def two(self, zo, side):
        count, lo = self.split(side)
        self.yd_copy(zo, side).wait_recv()
        self.add(zo, 1, lambda i: self.YD[zo, i - lo], lo, count - lo)
        self.x_copy(zo, side).start()
        self.xd_copy(zo, side).wait_recv()
        self.add(zo, 2, lambda i: self.XD[zo, i], 0, lo)
        self.y_copy(zo, side).start()

    def three(self, zo, side):
        self.x_copy(zo, side).wait_recv()
        self.y_copy(zo, side).wait_recv()
        self.add(
            zo, 0, lambda i: (self.X[zo, i].astype(f32) + self.Y[zo, i].astype(f32)).astype(bf16), 0, self.split(side)[0]
        )
        if is_own(side):
            return

        def more(direction):
            self.z_copy(zo, direction).wait_recv()
            self.add(zo, 0, lambda i: self.Z[zo, direction, i], 0, self.size)

        if side == -1:
            pl.when(self.net.has_dn)(lambda: more(0))
            self.z_copy(zo, 0).start()
        else:
            pl.when(self.net.has_up)(lambda: more(1))
            self.z_copy(zo, 1).start()

    def total(self, zo):
        pl.when(self.net.has_dn)(lambda: self.z_copy(zo, 0).wait_recv())
        pl.when(self.net.has_up)(lambda: self.z_copy(zo, 1).wait_recv())

    def sent(self, zo, side):
        for kind in range(4):
            self.c_copy(zo, kind).wait_send()
        self.xd_copy(zo, side).wait_send()
        self.yd_copy(zo, side).wait_send()
        self.x_copy(zo, side).wait_send()
        self.y_copy(zo, side).wait_send()
        if is_own(side):
            return
        self.z_copy(zo, 0).wait_send()
        for copy in self.late_copies(zo, 0):
            copy.wait_send()


def rounds(first, count, fn):
    wide = next(n for n in (6, 5, 4, 3, 2, 1) if count % n == 0)

    def body(i, _):
        for j in range(wide):
            fn(first + wide * i + j)
        return 0

    lax.fori_loop(0, count // wide, body, 0)


def scatter_kernel(
    nz, order_ref, tq_ref, to_ref, tu_ref, td_ref, own_ref, other_ref, local_ref, shared_ref,
    tile_o, dx_o, local_o, shared_o,
    TA, TB, S, A, R, XD, YD, X, Y, Z, ZX, dx_in, la, lb, sa, sb,
    tsem, dxs, vs, vr, *sems,
):
    net = Net(nz)
    z, x, y, c, m, d = net.z, net.x, net.y, net.c, net.m, net.d
    my = (1 - y) * 2 + c
    far = (lax.rem(z + 2, nz) * 2 + x, m)
    near = ((z + 1 - 2 * (z % 2)) * 2 + x, m)

    def loads(held, core):
        for group in range(2):
            first = 0
            for i, src in enumerate((tq_ref, to_ref, tu_ref, td_ref)):
                count = src.shape[1]
                yield pltpu.make_async_copy(
                    src.at[2 * group + core], held.at[group, pl.ds(first, count)],
                    tsem.at[2 * group + core, i],
                )
                first += count

    for copy in (*loads(TB, 1 - c), *loads(TA, c)):
        copy.start()
    net.greet()
    kinds = ((m, x), (m, 1 - x), (my, x), (my, 1 - x))
    bufs = (S, A, R, XD, YD, X, Y, Z, ZX)
    parts = [ScatterPart(net, kinds, i, order_ref, TA, TB, bufs, sems) for i in range(len(CHUNKS))]

    def step_of(distance, name):
        def run(zo, side):
            for part in parts:
                getattr(part, name)(zo, side)

        each(net, distance, run)

    dx_copy = send(other_ref, dx_in, dxs.at[0], dxs.at[1], net.cn)
    peers = (net.cn, net.xn, net.yn, near, far)

    def v_copies(k):
        return (
            send(la.at[k], lb.at[k], vs.at[k, 0], vr.at[k, 0], peers[k]),
            send(sa.at[k], sb.at[k], vs.at[k, 1], vr.at[k, 1], peers[k]),
        )

    def v_start(k):
        for copy in v_copies(k):
            copy.start()

    def v_finish(k):
        for copy in v_copies(k):
            copy.wait_recv()
        la[k + 1] = la[k] + lb[k]
        sa[k + 1] = sa[k] + sb[k]

    la[0] = local_ref[...]
    sa[0] = shared_ref[...]
    for copy in loads(TB, 1 - c):
        copy.wait()
    net.await_all()
    step_of(nz - 1, "begin")
    for copy in loads(TA, c):
        copy.wait()
    v_start(0)
    for turn_no in range(nz + 2):
        if turn_no + 1 < nz:
            step_of(nz - 2 - turn_no, "begin")
        if turn_no < nz:
            step_of(nz - 1 - turn_no, "one")
        if turn_no == 0:
            dx_copy.start()
        if 0 <= turn_no - 1 < nz:
            step_of(nz - turn_no, "two")
        if 0 <= turn_no - 2:
            step_of(nz + 1 - turn_no, "three")
        if turn_no < 5:
            v_finish(turn_no)
            if turn_no < 4:
                v_start(turn_no + 1)
    local_o[...] = la[5]
    shared_o[...] = sa[5]
    dx_copy.wait_recv()

    def join(r, _):
        at = pl.ds(pl.multiple_of(r * 128, 128), 128)
        dx_o[at, :] = own_ref[at, :] + dx_in[at, :].astype(f32)
        return 0

    lax.fori_loop(0, own_ref.shape[0] // 128, join, 0)
    for part in parts:
        part.total(z)

    def finish(i):
        total = A[z, 0, i].astype(f32)
        total = total + jnp.where(net.has_dn, Z[z, 0, i].astype(f32), 0.0)
        total = total + jnp.where(net.has_up, Z[z, 1, i].astype(f32), 0.0)
        j = part_of(m, order_ref[d * 24 + i])
        tile = jnp.concatenate([total, rest_of(total, free_of(j))], 0)
        tile_o[i] = turned(tile, j, -1)

    rounds(0, 24, finish)
    for step in range(nz):
        step_of(step, "sent")
    dx_copy.wait_send()
    for k in range(5):
        for copy in v_copies(k):
            copy.wait_send()


def scatter_grads(nz, order, parts, own, other, local, shared):
    dma = pltpu.SemaphoreType.DMA
    vm = pl.BlockSpec(memory_space=pltpu.VMEM)
    block = lambda *lead: pltpu.VMEM((*lead, 72, 128), bf16)
    anywhere = pl.BlockSpec(memory_space=pl.ANY)
    return pl.pallas_call(
        functools.partial(scatter_kernel, nz),
        out_shape=[
            jax.ShapeDtypeStruct((24, 96, 128), f32),
            jax.ShapeDtypeStruct(own.shape, f32),
            jax.ShapeDtypeStruct(local.shape, f32),
            jax.ShapeDtypeStruct(shared.shape, f32),
        ],
        in_specs=[pl.BlockSpec(memory_space=pltpu.SMEM)] + [anywhere] * 4 + [vm] * 4,
        out_specs=[vm] * 4,
        scratch_shapes=[
            block(2, 48 * nz), block(2, 48 * nz), block(nz, 4, 24), block(nz, 4, 24), block(nz, 4, 24),
            block(nz, 24), block(nz, 24), block(nz, 24), block(nz, 24), block(nz, 2, 24),
            block(nz, 2, 3, sum(late for _, late in CHUNKS)), pltpu.VMEM(other.shape, bf16),
            pltpu.VMEM((6, *local.shape), f32), pltpu.VMEM((5, *local.shape), f32),
            pltpu.VMEM((6, *shared.shape), f32), pltpu.VMEM((5, *shared.shape), f32),
            dma((4, 4)), dma((2,)), dma((5, 2)), dma((5, 2)),
        ]
        + [
            dma((len(CHUNKS), nz, *tail))
            for tail in ((4,), (4,), *([()] * 9), (2,), (3,), (2, 3))
        ],
        compiler_params=pltpu.CompilerParams(
            collective_id=1, has_side_effects=True, vmem_limit_bytes=60 << 20
        ),
        name="scatter_grads",
    )(order, *parts, own, other, local, shared)


STEP = 5
BETA_ONE = 0.5
BETA_TWO = 0.5
ADAM_EPS = 1e-08
RATE_TILES = 0.04
RATE_VECTORS = 0.2
DECAY = 0.01


def adam(grad, first, second):
    first_new = BETA_ONE * first + (1.0 - BETA_ONE) * grad
    second_new = BETA_TWO * second + (1.0 - BETA_TWO) * grad * grad
    step_dir = (
        first_new
        / (1.0 - BETA_ONE**STEP)
        / (jnp.sqrt(second_new / (1.0 - BETA_TWO**STEP)) + ADAM_EPS)
    )
    return (first_new, second_new, step_dir)


def update_kernel(
    grad_ref, first_ref, second_ref, left_ref, right_ref, master_ref,
    lg_ref, lv_ref, lf_ref, ls_ref, sg_ref, sv_ref, sf_ref, ss_ref,
    o_grad, o_first, o_second, o_weight, o_lg, o_lf, o_ls, o_lv, o_sg, o_sf, o_ss, o_sv,
):
    @pl.when(pl.program_id(0) == 0)
    def _():
        local = lg_ref[lax.axis_index("mp")]
        first, second, step_dir = adam(local, lf_ref[...], ls_ref[...])
        o_lg[...] = local
        o_lf[...] = first
        o_ls[...] = second
        o_lv[...] = lv_ref[...] - RATE_VECTORS * step_dir
        shared = sg_ref[...]
        first, second, step_dir = adam(shared, sf_ref[...], ss_ref[...])
        o_sg[...] = shared
        o_sf[...] = first
        o_ss[...] = second
        o_sv[...] = sv_ref[...] - RATE_VECTORS * step_dir

    every = range(grad_ref.shape[0])
    edge = left_ref.shape[-1]
    left = [left_ref[i].astype(bf16) for i in every]
    right = [right_ref[i].astype(bf16) for i in every]
    for i in every:
        o_grad[i] = grad_ref[i][:, :edge]
    half = [nn(grad_ref[i][:, :edge].astype(bf16), right[i]).astype(bf16) for i in every]
    rotated = [tn(left[i], half[i]) for i in every]
    moved = [adam(rotated[i], first_ref[i], second_ref[i]) for i in every]
    for i in every:
        o_first[i] = moved[i][0]
        o_second[i] = moved[i][1]
    half = [nn(left[i], moved[i][2].astype(bf16)).astype(bf16) for i in every]
    for i in every:
        turn_back = nt(half[i], right[i])
        master = master_ref[i]
        o_weight[i] = master - RATE_TILES * (turn_back + DECAY * master)


def update(grad, first, second, left, right, master, local, shared):
    count, edge, wide = grad.shape
    part = 6 if count % 6 == 0 else count
    tile = lambda w: pl.BlockSpec((part, edge, w), lambda i: (i, 0, 0))
    whole = lambda v: pl.BlockSpec(v.shape, lambda i: (0,) * v.ndim)
    out = lambda v: jax.ShapeDtypeStruct(v.shape, f32)
    return pl.pallas_call(
        update_kernel,
        grid=(count // part,),
        in_specs=[tile(wide)] + [tile(edge)] * 5 + [whole(v) for v in (*local, *shared)],
        out_specs=[tile(edge)] * 4 + [whole(local[1])] * 4 + [whole(shared[1])] * 4,
        out_shape=[out(first)] * 4 + [out(local[1])] * 4 + [out(shared[1])] * 4,
        compiler_params=pltpu.CompilerParams(vmem_limit_bytes=58 << 20),
        name="update",
    )(grad, first, second, left, right, master, *local, *shared)


def from_tiles(tile_set, row_count, col_count):
    edge = tile_set.shape[-1]
    return (
        tile_set.reshape(row_count // edge, col_count // edge, edge, edge)
        .transpose(0, 2, 1, 3)
        .reshape(row_count, col_count)
    )


def plain_weights(tile_order, master, local):
    tiles = lax.all_gather(master.astype(bf16), "dp", axis=0, tiled=True)
    tiles = lax.all_gather(tiles, "mp", axis=0)
    count = tile_order.shape[0]
    inverse = jnp.zeros((count,), jnp.int32).at[tile_order].set(jnp.arange(count, dtype=jnp.int32))
    natural = tiles[:, inverse]
    dense = []
    for rows, cols, where in GRIDS:
        pieces = []
        for r in range(rows):
            pick = [where(r, j) for j in range(cols)]
            groups = jnp.asarray([p for p, _ in pick], jnp.int32)
            numbers = jnp.asarray([n for _, n in pick], jnp.int32)
            pieces.append(natural[groups, numbers].transpose(1, 0, 2).reshape(96, cols * 96))
        dense.append(jnp.concatenate(pieces, 0))
    return (*dense, lax.all_gather(local, "mp", axis=0))


def plain_scatter(order, parts, own, other, local, shared):
    tiles = jnp.concatenate(parts, 1)[:, order]
    mine = lax.psum_scatter(tiles, "mp", scatter_dimension=0, tiled=False).astype(f32)
    turns = part_of(lax.axis_index("mp"), order)[:, None, None]
    back = mine
    for k in range(1, 4):
        back = jnp.where(turns == k, jnp.roll(mine, -96 * k, -1), back)
    rest = back[..., 96:].reshape(-1, 3, 24, 32).transpose(0, 2, 1, 3).reshape(-1, 24, 96)
    tiles = jnp.concatenate([back[..., :96], rest], 1)
    owned = lax.psum_scatter(tiles, "dp", scatter_dimension=0, tiled=True)
    count = lax.axis_size("mp")
    swapped = lax.ppermute(other, "mp", [(i, i ^ 1) for i in range(count)])
    local_sum, shared_sum = lax.psum((local, shared), ("dp", "mp"))
    return owned, own + swapped.astype(f32), local_sum, shared_sum


def shards(
    tokens,
    cotangent,
    lengths,
    tile_order,
    master,
    first_moment,
    second_moment,
    basis_left,
    basis_right,
    local_vec,
    local_first,
    local_second,
    shared_vec,
    shared_first,
    shared_second,
):
    group_count = lax.axis_size("mp")
    group_index = lax.axis_index("mp")
    owners = lax.axis_size("dp")
    row_total, width = tokens.shape
    rows = row_total // group_count
    per_owner = master.shape[1]
    nz = owners // 2
    routed = per_owner == 24 and nz == 4 and group_count == 4

    if routed:
        w_qkv, w_out, w_up, w_down, vectors = gather_weights(
            nz, tile_order, slot_of_tile(tile_order), master[0], local_vec
        )
    else:
        w_qkv, w_out, w_up, w_down, vectors = plain_weights(tile_order, master[0], local_vec)
    output, tq, to, tu, td, own, other, local_terms, shared_terms = layer(
        tokens, cotangent, lengths, vectors, shared_vec, w_qkv, w_out, w_up, w_down, rows
    )
    parts = [t.reshape(group_count, -1, 72, 128) for t in (tq, to, tu, td)]
    if routed:
        owned, input_grad, local_sum, shared_grad = scatter_grads(
            nz, tile_order, parts, own, other, local_terms, shared_terms
        )
    else:
        owned, input_grad, local_sum, shared_grad = plain_scatter(
            tile_order, parts, own, other, local_terms, shared_terms
        )
    tiles = update(
        owned, first_moment[0], second_moment[0], basis_left[0], basis_right[0], master[0],
        (local_sum, local_vec, local_first, local_second),
        (shared_grad, shared_vec, shared_first, shared_second),
    )
    return (output, input_grad, *(t[None] for t in tiles[:4]), *tiles[4:])


def solution(mesh):
    placed = (
        P("dp", None),
        P("dp", None),
        P("dp"),
        P(),
        P("mp", "dp", None, None),
        P("mp", "dp", None, None),
        P("mp", "dp", None, None),
        P("mp", "dp", None, None),
        P("mp", "dp", None, None),
        P("mp", None),
        P("mp", None),
        P("mp", None),
        P(),
        P(),
        P(),
    )
    return jax.shard_map(
        shards,
        mesh=mesh,
        in_specs=placed,
        out_specs=(
            P(("dp", "mp"), None),
            P(("dp", "mp"), None),
            P("mp", "dp", None, None),
            P("mp", "dp", None, None),
            P("mp", "dp", None, None),
            P("mp", "dp", None, None),
            P("mp", None),
            P("mp", None),
            P("mp", None),
            P("mp", None),
            P(),
            P(),
            P(),
            P(),
        ),
        check_vma=False,
    )
```

```python
import functools
import jax
import jax.numpy as jnp
from jax import lax
from jax.experimental import pallas as pl
from jax.experimental.pallas import tpu as pltpu
from jax.sharding import PartitionSpec as P

MESH = pl.DeviceIdType.MESH
f32 = jnp.float32
bf16 = jnp.bfloat16


def lanes_of(shape):
    return lax.broadcasted_iota(jnp.int32, shape, len(shape) - 1)


def turn(v, amount):
    return pltpu.roll(v, amount, v.ndim - 1)


def free_of(j):
    return (3 * j + 3) % 4


def part_of(group, number):
    return jnp.where(number < 48, 2 * group + number % 2, number) % 4


def groups_of(shape):
    return lanes_of(shape) // 32


def to_wire(tile, free):
    rest = tile[72:96]
    side = jnp.concatenate([turn(rest, 96), turn(rest, 64), turn(rest, 32)], 0)
    return jnp.where(groups_of(side.shape) == free, side, tile[:72])


def rest_of(wire, free):
    group = groups_of((24, 128))
    first, second, third = turn(wire[:24], 32), turn(wire[24:48], 64), turn(wire[48:72], 96)
    return jnp.where(
        group == (free + 1) % 4, first, jnp.where(group == (free + 2) % 4, second, third)
    )


def turned(tile, j, sign):
    half = (j == 1) | (j == 2) if sign > 0 else j >= 2
    out = jnp.where(half, turn(tile, 64), tile)
    return jnp.where(j % 2 == 1, turn(out, 32), out)


def join_four(wires):
    lane, group = lanes_of((72, 128)), groups_of((24, 128))
    a, b, c, d = wires
    tops = [jnp.where(lane < 96, a, b), jnp.where(lane < 64, b, c), jnp.where(lane < 32, c, d)]
    rests = []
    for i in range(3):
        at = slice(24 * i, 24 * i + 24)
        mixed = jnp.where(
            group == 3, a[at], jnp.where(group == 2, b[at], jnp.where(group == 1, c[at], d[at]))
        )
        rests.append(turn(mixed, 32 * (i + 1)))
    pieces = []
    for k in range(3):
        index = (group + k) % 3
        rest = jnp.where(index == 0, rests[0], jnp.where(index == 1, rests[1], rests[2]))
        pieces.append(jnp.concatenate([tops[k], rest], 0))
    return pieces


def split_four(pieces):
    lane, group = lanes_of((72, 128)), groups_of((24, 128))
    a, b, c = (p[:72] for p in pieces)
    rests = [p[72:] for p in pieces]
    sides = []
    for i in range(3):
        mixed = jnp.where(
            group % 3 == 0,
            rests[i],
            jnp.where(group == 1, rests[(i - 1) % 3], rests[(i - 2) % 3]),
        )
        sides.append(turn(mixed, 96 - 32 * i))
    side = jnp.concatenate(sides, 0)
    tops = [a, jnp.where(lane < 64, b, a), jnp.where(lane < 32, c, b), c]
    return [jnp.where(lane // 32 == 3 - t, side, tops[t]) for t in range(4)]


def place():
    d, m = lax.axis_index("dp"), lax.axis_index("mp")
    return d // 2, d % 2, m // 2, m % 2


class Net:
    def __init__(self, nz):
        self.nz = nz
        self.z, self.x, self.y, self.c = place()
        self.d = self.z * 2 + self.x
        self.m = self.y * 2 + self.c
        self.xn = (self.z * 2 + 1 - self.x, self.m)
        self.yn = (self.d, (1 - self.y) * 2 + self.c)
        self.cn = (self.d, self.y * 2 + 1 - self.c)
        self.up = (self.d + 2, self.m)
        self.dn = (self.d - 2, self.m)
        self.has_up = self.z < nz - 1
        self.has_dn = self.z > 0

    def peers(self):
        others = [(lax.rem(self.z + k, self.nz) * 2 + self.x, self.m) for k in range(1, self.nz)]
        return [self.xn, self.yn, self.cn] + others

    def greet(self):
        for peer in self.peers():
            pl.semaphore_signal(
                pltpu.get_barrier_semaphore(), inc=1, device_id=peer, device_id_type=MESH
            )

    def await_all(self):
        pl.semaphore_wait(pltpu.get_barrier_semaphore(), len(self.peers()))


def send(src, dst, ss, rs, peer):
    return pltpu.make_async_remote_copy(
        src_ref=src, dst_ref=dst, send_sem=ss, recv_sem=rs, device_id=peer, device_id_type=MESH
    )


def tile_qkv(r, j):
    return (j % 8) // 2, r * 6 + (j // 8) * 2 + j % 2


def tile_out(r, j):
    return r // 2, 48 + (r % 2) * 8 + j


def tile_up(r, j):
    return j // 8, 64 + r * 8 + j % 8


def tile_down(r, j):
    return r // 8, 128 + (r % 8) * 8 + j


GRIDS = ((8, 24, tile_qkv), (8, 8, tile_out), (8, 32, tile_up), (32, 8, tile_down))


CHUNKS = ((24, 4),)


def is_own(side):
    return isinstance(side, int) and side == 0


def each(net, step, fn):
    if step == 0:
        fn(net.z, 0)
        return

    @pl.when(net.z >= step)
    def _():
        fn(net.z - step, 1)

    @pl.when(net.z + step < net.nz)
    def _():
        fn(net.z + step, -1)


class Part:
    def __init__(self, net, kinds, index, sems):
        self.net, self.kinds, self.index, self.sems = net, kinds, index, sems
        self.size, self.late = CHUNKS[index]
        self.base = sum(n for n, _ in CHUNKS[:index])
        self.early = self.size - self.late

    def sem(self, i, *at):
        return self.sems[i].at[(self.index, *at)]

    def split(self, side):
        count = self.size if is_own(side) else self.early
        return count, (count + self.index % 2) // 2


class GatherPart(Part):
    def __init__(self, net, kinds, index, G, sems):
        super().__init__(net, kinds, index, sems)
        self.G = G

    def slot(self, kind, zo, lo=0, n=None, shift=0):
        mo, xo = self.kinds[kind]
        n = self.size if n is None else n
        return self.G.at[mo + shift, pl.ds((zo * 2 + xo) * 24 + self.base + lo, n)]

    def go(self, s, i, i_at, j, j_at, peer):
        return send(s, s, self.sem(i, *i_at), self.sem(j, *j_at), peer)

    def toward(self, direction):
        return self.net.up if direction == 0 else self.net.dn

    def z_copy(self, zo, direction):
        return self.go(self.slot(0, zo), 0, (zo, direction), 1, (zo,), self.toward(direction))

    def late_copies(self, zo, direction):
        for k in range(3):
            s = self.slot(k + 1, zo, self.early, self.late)
            yield self.go(s, 12, (zo, k, direction), 13, (zo, k), self.toward(direction))

    def c_copy(self, zo, kind, side, shift=0):
        n = self.size if kind == 0 or is_own(side) else self.early
        return self.go(self.slot(kind, zo, 0, n, shift), 10, (zo, kind), 11, (zo, kind), self.net.cn)

    def c_late(self, zo, k, shift=0):
        s = self.slot(k + 1, zo, self.early, self.late, shift)
        return self.go(s, 14, (zo, k), 15, (zo, k), self.net.cn)

    def x_copy(self, zo, kind, side):
        return self.go(self.slot(kind, zo, 0, self.split(side)[0]), 2, (zo,), 3, (zo,), self.net.xn)

    def y_copy(self, zo, kind, side):
        return self.go(self.slot(kind, zo, 0, self.split(side)[0]), 4, (zo,), 5, (zo,), self.net.yn)

    def xd_copy(self, zo, kind, side):
        return self.go(self.slot(kind, zo, 0, self.split(side)[1]), 6, (zo,), 7, (zo,), self.net.xn)

    def yd_copy(self, zo, kind, side):
        count, lo = self.split(side)
        return self.go(self.slot(kind, zo, lo, count - lo), 8, (zo,), 9, (zo,), self.net.yn)

    def onward(self, side, act):
        if is_own(side) or side == 1:
            pl.when(self.net.has_up)(lambda: act(0))
        if is_own(side) or side == -1:
            pl.when(self.net.has_dn)(lambda: act(1))

    def arrive(self, zo, side):
        if not is_own(side):
            self.z_copy(zo, 0).wait_recv()
        self.onward(side, lambda direction: self.z_copy(zo, direction).start())
        self.x_copy(zo, 0, side).start()
        self.y_copy(zo, 0, side).start()
        self.c_copy(zo, 0, side).start()

    def diag(self, zo, side):
        self.x_copy(zo, 1, side).wait_recv()
        self.yd_copy(zo, 1, side).start()
        self.c_copy(zo, 1, side).start()
        self.y_copy(zo, 2, side).wait_recv()
        self.xd_copy(zo, 2, side).start()
        self.c_copy(zo, 2, side).start()

    def fin(self, zo, side):
        self.xd_copy(zo, 3, side).wait_recv()
        self.yd_copy(zo, 3, side).wait_recv()
        self.c_copy(zo, 3, side).start()

    def last(self, zo, side):
        if not is_own(side):
            for copy in self.late_copies(zo, 0):
                copy.wait_recv()

        def act(direction):
            for copy in self.late_copies(zo, direction):
                copy.start()

        self.onward(side, act)
        if not is_own(side):
            for k in range(3):
                self.c_late(zo, k).start()

    def other_core(self, zo, side):
        flip = 1 - 2 * self.net.c
        for kind in range(4):
            self.c_copy(zo, kind, side, flip).wait_recv()
            if kind and not is_own(side):
                self.c_late(zo, kind - 1, flip).wait_recv()

    def sent(self, zo, side):
        self.x_copy(zo, 0, side).wait_send()
        self.y_copy(zo, 0, side).wait_send()
        self.yd_copy(zo, 1, side).wait_send()
        self.xd_copy(zo, 2, side).wait_send()
        for kind in range(4):
            self.c_copy(zo, kind, side).wait_send()
        if not is_own(side):
            for k in range(3):
                self.c_late(zo, k).wait_send()

        def done(direction):
            self.z_copy(zo, direction).wait_send()
            for copy in self.late_copies(zo, direction):
                copy.wait_send()

        self.onward(side, done)


def gather_kernel(
    nz, order_ref, row_ref, master_ref, local_ref, o_qkv, o_out, o_up, o_down, o_local,
    G, src_ref, inverse, LV, d_qkv, d_out, d_up, d_down,
    outs, lvs, lvr, inv_sem, *sems,
):
    net = Net(nz)
    z, x, y, c, m = net.z, net.x, net.y, net.c, net.m
    my = (1 - y) * 2 + c
    full = 24
    net.greet()

    def stage(i, _):
        tile = jnp.concatenate([master_ref[i], jnp.zeros((96, 32), f32)], axis=-1)
        j = part_of(m, order_ref[net.d * full + i])
        tile = turned(tile, j, 1)
        G[m, net.d * full + i] = to_wire(tile, free_of(j)).astype(bf16)
        return 0

    lax.fori_loop(0, full, stage, 0)
    LV[m] = local_ref[...]
    net.await_all()
    lv_y = send(LV.at[m], LV.at[m], lvs.at[0], lvr.at[0], net.yn)
    lv_c = send(LV.at[m], LV.at[m], lvs.at[1], lvr.at[1], net.cn)
    lv_d = send(LV.at[my], LV.at[my], lvs.at[2], lvr.at[2], net.cn)

    kinds = ((m, x), (m, 1 - x), (my, x), (my, 1 - x))
    flip = 1 - 2 * c
    parts = [GatherPart(net, kinds, i, G, sems) for i in range(len(CHUNKS))]

    def step_of(distance, name, reverse=False):
        def run(zo, side):
            for part in parts:
                getattr(part, name)(zo, side)

        each(net, distance, run)

    def forwarded(zo, side):
        for part in parts:
            part.other_core(zo, side)

    step_of(0, "arrive")
    lv_y.start()
    lv_c.start()
    step_of(1, "arrive")
    step_of(0, "diag")
    send(LV.at[my], LV.at[my], lvs.at[0], lvr.at[0], net.yn).wait_recv()
    lv_d.start()
    step_of(2, "arrive")
    step_of(1, "diag")
    step_of(0, "fin")
    step_of(0, "last")
    step_of(3, "arrive")
    step_of(1, "fin")
    step_of(1, "last")
    step_of(2, "diag")
    step_of(2, "last")
    step_of(2, "fin")
    step_of(3, "diag")
    step_of(3, "last")
    step_of(3, "fin")
    for step in range(nz):
        step_of(step, "other_core")
    count = row_ref.shape[1]
    down = lax.broadcasted_iota(jnp.int32, (count, count), 0)
    along = lax.broadcasted_iota(jnp.int32, (count, count), 1)
    column = jnp.sum(jnp.where(down == along, row_ref[...], 0), 1, keepdims=True)
    inverse[...] = jnp.max(jnp.where(column == along, down, 0), 0, keepdims=True)
    to_scalars = pltpu.make_async_copy(inverse, src_ref, inv_sem.at[0])
    to_scalars.start()
    mc = m + flip
    send(LV.at[mc], LV.at[mc], lvs.at[1], lvr.at[1], net.cn).wait_recv()
    mc = my + flip
    send(LV.at[mc], LV.at[mc], lvs.at[2], lvr.at[2], net.cn).wait_recv()
    o_local[...] = LV[...]
    to_scalars.wait()

    copies = []
    for i, ((rows, cols, where), dense, out) in enumerate(
        zip(GRIDS, (d_qkv, d_out, d_up, d_down), (o_qkv, o_out, o_up, o_down))
    ):
        def fill(r, _):
            for g in range(cols // 4):
                tiles = []
                for t in range(4):
                    p, n = where(r, 4 * g + t)
                    tiles.append(G[p, src_ref[0, n]].astype(f32))
                for k, piece in enumerate(join_four(tiles)):
                    dense[pl.ds(pl.multiple_of(r * 96, 96), 96), pl.ds(384 * g + 128 * k, 128)] = (
                        piece.astype(bf16)
                    )
            band = pl.ds(pl.multiple_of(r * 96, 96), 96)
            pltpu.make_async_copy(dense.at[band], out.at[band], outs.at[i]).start()
            return 0

        lax.fori_loop(0, rows, fill, 0)
        copies.append(pltpu.make_async_copy(dense, out, outs.at[i]))

    for step in range(nz):
        step_of(step, "sent")
    lv_y.wait_send()
    lv_c.wait_send()
    lv_d.wait_send()
    for copy in copies:
        copy.wait()


def gather_weights(nz, order, master, local):
    dma = pltpu.SemaphoreType.DMA
    shapes = [(r * 96, c * 96) for r, c, _ in GRIDS]
    return pl.pallas_call(
        functools.partial(gather_kernel, nz),
        out_shape=[jax.ShapeDtypeStruct(s, bf16) for s in shapes]
        + [jax.ShapeDtypeStruct((4, *local.shape), f32)],
        in_specs=[pl.BlockSpec(memory_space=pltpu.SMEM)] + [pl.BlockSpec(memory_space=pltpu.VMEM)] * 3,
        out_specs=[pl.BlockSpec(memory_space=pl.ANY)] * 4 + [pl.BlockSpec(memory_space=pltpu.VMEM)],
        scratch_shapes=[pltpu.VMEM((4, 2 * nz * 24, 72, 128), bf16), pltpu.SMEM((1, 2 * nz * 24), jnp.int32),
            pltpu.VMEM((1, 2 * nz * 24), jnp.int32), pltpu.VMEM((4, *local.shape), f32)]
        + [pltpu.VMEM(s, bf16) for s in shapes]
        + [dma((4,)), dma((3,)), dma((3,)), dma((1,))]
        + [dma((len(CHUNKS), nz, *tail)) for tail in ((2,), (), *([()] * 8), (4,), (4,), (3, 2), (3,), (3,), (3,))],
        compiler_params=pltpu.CompilerParams(
            collective_id=0, has_side_effects=True, vmem_limit_bytes=56 << 20
        ),
        name="gather_weights",
    )(order, order.reshape(1, -1), master, local)


NEG_BIG = -1e30
NORM_EPS = 1e-05
ROOT_HALF = 0.7071067811865476
PHI_SCALE = 0.3989422804014327


def nt(a, b):
    return lax.dot_general(a, b, (((1,), (1,)), ((), ())), preferred_element_type=f32)


def tn(a, b):
    return lax.dot_general(a, b, (((0,), (0,)), ((), ())), preferred_element_type=f32)


def nn(a, b):
    return jnp.dot(a, b, preferred_element_type=f32)


def standard(values):
    centre = values - jnp.mean(values, -1, keepdims=True)
    scale = lax.rsqrt(jnp.mean(centre * centre, -1, keepdims=True) + NORM_EPS)
    return centre * scale, scale


def standard_back(grad, normed, scale, gain):
    inner = grad * gain
    return scale * (
        inner - jnp.mean(inner, -1, keepdims=True) - normed * jnp.mean(inner * normed, -1, keepdims=True)
    )


def col_sum(values):
    return jnp.sum(values, 0, keepdims=True)


def layer_kernel(
    tokens_ref, cot_ref, lengths_ref, vec_ref, sv_ref, wq_ref, wo_ref, wu_ref, wd_ref,
    out_ref, tq_ref, to_ref, tu_ref, td_ref, own_ref, other_ref, dl_ref, ds_ref,
    x, cot, wqkv, wout, wup, wdown, bias, q, k, v, probs, o_t, hid, low, low_t, n_one, r_one, acc,
    act, slope, g_low, g_o, dq, dk, dv, x_t, out, other, su, sd, sq, loads, stores, su_sem, sd_sem, sq_sem,
):
    rows, width = q.shape
    seq_len = k.shape[0]
    chunks, _, cut = act.shape
    tiles = width // 96
    pairs = width // 128
    piece = 512
    zero = jnp.zeros((), bf16)
    member = lax.axis_index("mp")
    share = seq_len // rows
    seq, part = member // share, member % share
    length = lengths_ref[seq]
    bound = 64 * ((length + 127) // 128)
    start_b = pl.multiple_of(bound, 64)
    here = pl.ds(pl.multiple_of(part * rows, rows), rows)
    there = pl.ds(pl.multiple_of((1 - part) * rows, rows), rows)

    def load(src, dst, i):
        copy = pltpu.make_async_copy(src, dst, loads.at[i])
        copy.start()
        return copy

    get_x = load(tokens_ref.at[pl.ds(pl.multiple_of(seq * seq_len, seq_len), seq_len)], x, 0)
    get_qkv = [
        load(wq_ref.at[:, pl.ds(i * width, width)], wqkv.at[:, pl.ds(i * width, width)], 6 + i)
        for i in range(3)
    ]
    get_o = load(wo_ref, wout, 2)
    get_u = load(wu_ref, wup, 3)
    get_d = load(wd_ref, wdown, 4)
    get_c = load(cot_ref.at[pl.ds(pl.multiple_of(member * rows, rows), rows)], cot, 5)

    groups = vec_ref.shape[0]
    third = width // groups
    bias[:, :width] = jnp.concatenate([vec_ref[p][:, :third] for p in range(groups)], 1)
    bias[:, width:] = jnp.concatenate([vec_ref[p][:, third : 2 * third] for p in range(groups)], 1)

    get_x.wait()
    get_qkv[0].wait()
    for lo in range(0, width, 256):
        got = nn(x[here, :], wqkv[:, lo : lo + 256]) + bias[:, lo : lo + 256]
        q[:, lo : lo + 256] = got.astype(bf16) * jnp.asarray(0.125, bf16)

    get_qkv[1].wait()
    get_qkv[2].wait()

    def project(r, _):
        at = pl.ds(pl.multiple_of(r * rows, rows), rows)
        for lo in range(0, width, 256):
            k[at, lo : lo + 256] = nn(x[at, :], wqkv[:, width + lo : width + lo + 256]).astype(bf16)
            got = nn(x[at, :], wqkv[:, 2 * width + lo : 2 * width + lo + 256])
            v[at, lo : lo + 256] = (got + bias[:, width + lo : width + lo + 256]).astype(bf16)
        return 0

    lax.fori_loop(0, share, project, 0, unroll=True)

    def picks(shape, rows_at):
        row = lax.broadcasted_iota(jnp.int32, shape, rows_at) + part * rows
        lane = lax.broadcasted_iota(jnp.int32, shape, 1 - rows_at)
        return (row < bound) == (lane < 64)

    windows = ((0, bound), (start_b, length - bound))

    def forward(pair, _):
        cols = pl.ds(pl.multiple_of(pair * 128, 128), 128)
        queries = q[:, cols]
        pick = picks((rows, 128), 0)
        mine = (jnp.where(pick, queries, zero), jnp.where(pick, zero, queries))
        scores = [nt(k[pl.ds(start, rows), cols], mine[w]) for w, (start, _) in enumerate(windows)]
        outs = []
        for w, (start, limit) in enumerate(windows):
            inside = lax.broadcasted_iota(jnp.int32, scores[w].shape, 0) < limit
            masked = jnp.where(inside, scores[w], NEG_BIG)
            weight = jnp.exp(masked - jnp.max(masked, 0, keepdims=True))
            low_probs = (weight * (1.0 / jnp.sum(weight, 0, keepdims=True))).astype(bf16)
            probs[2 * pair + w] = low_probs
            outs.append(tn(v[pl.ds(start, rows), cols], low_probs))
        o_t[cols, :] = jnp.where(picks((128, rows), 1), outs[0], outs[1]).astype(bf16)
        return 0

    lax.fori_loop(0, pairs, forward, 0, unroll=3)

    def by_rows(fn):
        def body(r, _):
            fn(pl.ds(pl.multiple_of(r * piece, piece), piece), r)
            return 0

        lax.fori_loop(0, rows // piece, body, 0)

    get_o.wait()
    acc[...] = tn(o_t[...], wout[...])

    def norm_one(at, r):
        mine = pl.ds(pl.multiple_of(part * rows + r * piece, piece), piece)
        z_one = x[mine, :].astype(f32) + acc[at, :] + sv_ref[0:1, :]
        normed, scale = standard(z_one)
        hidden = normed * sv_ref[2:3, :] + sv_ref[3:4, :]
        n_one[at, :] = normed
        r_one[at, :] = jnp.broadcast_to(scale, (piece, 128))
        hid[at, :] = hidden
        low[at, :] = hidden.astype(bf16)
        acc[at, :] = jnp.zeros((piece, width), f32)

    by_rows(norm_one)
    low_t[...] = low[...].T
    get_u.wait()
    get_d.wait()

    def feed(i, _):
        at = pl.ds(pl.multiple_of(i * cut, cut), cut)
        pre = nn(low[...], wup[:, at]) + vec_ref[i, :, 2 * third :]
        phi = 0.5 * (1.0 + lax.erf(pre * ROOT_HALF))
        density = jnp.exp(-0.5 * pre * pre) * PHI_SCALE
        active = (pre * phi).astype(bf16)
        act[i] = active
        slope[i] = (phi + pre * density).astype(bf16)
        acc[...] += nn(active, wdown[at, :])
        return 0

    lax.fori_loop(0, chunks, feed, 0, unroll=4)
    get_c.wait()
    ds_ref[...] = jnp.zeros_like(ds_ref)

    def norm_two(at, r):
        z_two = hid[at, :] + acc[at, :] + sv_ref[1:2, :]
        normed, scale = standard(z_two)
        row = lax.broadcasted_iota(jnp.int32, (piece, 1), 0) + part * rows + r * piece
        valid = (row < length).astype(f32)
        out[at, :] = ((normed * sv_ref[4:5, :] + sv_ref[5:6, :]) * valid).astype(bf16)
        grad = cot[at, :].astype(f32) * valid
        back = standard_back(grad, normed, scale, sv_ref[4:5, :])
        ds_ref[4:5, :] += col_sum(grad * normed)
        ds_ref[5:6, :] += col_sum(grad)
        ds_ref[1:2, :] += col_sum(back)
        g_low[at, :] = back.astype(bf16)
        acc[at, :] = back

    by_rows(norm_two)
    put_out = pltpu.make_async_copy(out, out_ref, stores.at[0])
    put_out.start()

    def put_u(i):
        return pltpu.make_async_copy(su.at[i % 2], tu_ref.at[i], su_sem.at[i % 2])

    def put_d(i):
        return pltpu.make_async_copy(sd.at[i % 2], td_ref.at[i], sd_sem.at[i % 2])

    def cut_up(grad, keep):
        for r in range(grad.shape[0] // 96):
            for g in range(grad.shape[1] // 384):
                pieces = [
                    grad[96 * r : 96 * r + 96, 384 * g + 128 * n : 384 * g + 128 * n + 128]
                    for n in range(3)
                ]
                for t, wire in enumerate(split_four(pieces)):
                    keep(r, 4 * g + t, wire.astype(bf16))

    def feed_back(i, _):
        at = pl.ds(pl.multiple_of(i * cut, cut), cut)

        @pl.when(i >= 2)
        def _():
            put_u(i - 2).wait()
            put_d(i - 2).wait()

        grad_low = (nt(g_low[...], wdown[at, :]) * slope[i].astype(f32)).astype(bf16)
        dl_ref[i, :, 2 * third :] = col_sum(grad_low.astype(f32))
        acc[...] += nt(grad_low, wup[:, at])

        def keep_down(r, j, wire):
            sd[i % 2, r * tiles + j] = wire

        def keep_up(r, j, wire):
            su[i % 2, r * tiles + j] = wire

        cut_up(tn(act[i], g_low[...]), keep_down)
        cut_up(nn(low_t[...], grad_low), keep_up)
        put_u(i).start()
        put_d(i).start()
        return 0

    lax.fori_loop(0, chunks, feed_back, 0)

    def norm_back(at, r):
        grad = acc[at, :]
        normed = n_one[at, :]
        back = standard_back(grad, normed, r_one[at, 0:1], sv_ref[2:3, :])
        ds_ref[2:3, :] += col_sum(grad * normed)
        ds_ref[3:4, :] += col_sum(grad)
        ds_ref[0:1, :] += col_sum(back)
        acc[at, :] = back
        g_low[at, :] = back.astype(bf16)

    by_rows(norm_back)
    g_o[...] = nt(g_low[...], wout[...]).astype(bf16)

    def keep_out(r, j, wire):
        sd[0, r * tiles + j] = wire

    put_d(chunks - 2).wait()
    cut_up(nn(o_t[...], g_low[...]), keep_out)
    put_o = pltpu.make_async_copy(sd.at[0], to_ref, stores.at[1])
    put_o.start()
    dk[...] = jnp.zeros_like(dk)
    dv[...] = jnp.zeros_like(dv)

    def backward(pair, _):
        cols = pl.ds(pl.multiple_of(pair * 128, 128), 128)
        pick, pick_t = picks((rows, 128), 0), picks((128, rows), 1)
        queries, grads = q[:, cols], g_o[:, cols]
        grads_t = grads.T
        inner = grads_t.astype(f32) * o_t[cols, :].astype(f32)
        outs = []
        for w, (start, _) in enumerate(windows):
            at = pl.ds(start, rows)
            mine = (lambda a: jnp.where(pick, a, zero)) if w == 0 else (lambda a: jnp.where(pick, zero, a))
            mine_t = (lambda a: jnp.where(pick_t, a, jnp.zeros((), a.dtype))) if w == 0 else (lambda a: jnp.where(pick_t, jnp.zeros((), a.dtype), a))
            dot_sum = jnp.sum(mine_t(inner), 0, keepdims=True)
            grad_probs = nn(v[at, cols], mine_t(grads_t))
            these = probs[2 * pair + w]
            grad_scores = (these.astype(f32) * (grad_probs - dot_sum)).astype(bf16)
            dv[at, cols] = nn(these, mine(grads)).astype(bf16)
            dk[at, cols] = nn(grad_scores, mine(queries)).astype(bf16)
            outs.append(tn(k[at, cols], grad_scores))
        dq[:, cols] = (jnp.where(pick_t, outs[0], outs[1]) * 0.125).astype(bf16).T
        return 0

    lax.fori_loop(0, pairs, backward, 0, unroll=3)

    other[...] = (
        nt(dk[there, :], wqkv[:, width : 2 * width]) + nt(dv[there, :], wqkv[:, 2 * width :])
    ).astype(bf16)
    put_x = pltpu.make_async_copy(other, other_ref, stores.at[2])
    put_x.start()
    hid[...] = (
        acc[...]
        + nt(dq[...], wqkv[:, :width])
        + nt(dk[here, :], wqkv[:, width : 2 * width])
        + nt(dv[here, :], wqkv[:, 2 * width :])
    )
    put_own = pltpu.make_async_copy(hid, own_ref, stores.at[3])
    put_own.start()
    sum_q = col_sum(dq[...].astype(f32))
    sum_v = col_sum(dv[...].astype(f32))
    for p in range(groups):
        dl_ref[p, :, :third] = sum_q[:, third * p : third * p + third]
        dl_ref[p, :, third : 2 * third] = sum_v[:, third * p : third * p + third]

    x_t[...] = x[...].T
    puts = []
    for index, grad in enumerate((dk, dv, dq)):
        part_no = (1, 2, 0)[index]
        outer = nn(x_t[:, here] if part_no == 0 else x_t[...], grad[...])
        if index >= 2:
            puts[index - 2].wait()

        def keep(r, j, wire):
            sq[index % 2, j // 2, r, j % 2] = wire

        cut_up(outer, keep)
        put = pltpu.make_async_copy(sq.at[index % 2], tq_ref.at[:, :, part_no], sq_sem.at[index % 2])
        put.start()
        puts.append(put)
    for i in (chunks - 2, chunks - 1):
        put_u(i).wait()
    put_d(chunks - 1).wait()
    for put in (put_out, put_o, put_x, put_own, puts[-2], puts[-1]):
        put.wait()


def layer(tokens, cotangent, lengths, vectors, shared, w_qkv, w_out, w_up, w_down, rows):
    width = w_out.shape[0]
    hidden = w_up.shape[1]
    seq_len = tokens.shape[0] // lengths.shape[0]
    groups = vectors.shape[0]
    cut = hidden // groups
    chunks = groups
    tiles = width // 96
    anywhere = pl.BlockSpec(memory_space=pl.ANY)
    vm = pl.BlockSpec(memory_space=pltpu.VMEM)
    smem = pl.BlockSpec(memory_space=pltpu.SMEM)
    out = jax.ShapeDtypeStruct
    V = pltpu.VMEM
    dma = pltpu.SemaphoreType.DMA
    tall, wide, long = (rows, width), (width, rows), (seq_len, width)
    return pl.pallas_call(
        layer_kernel,
        in_specs=[anywhere, anywhere, smem, vm, vm] + [anywhere] * 4,
        out_specs=[anywhere] * 7 + [vm, vm],
        out_shape=[
            out(tall, bf16),
            out((groups, tiles, 3, 2, 72, 128), bf16),
            out((tiles * tiles, 72, 128), bf16),
            out((groups, cut // 96 * tiles, 72, 128), bf16),
            out((groups, cut // 96 * tiles, 72, 128), bf16),
            out(tall, f32),
            out(tall, bf16),
            out(vectors.shape, f32),
            out(shared.shape, f32),
        ],
        scratch_shapes=[
            V(long, bf16), V(tall, bf16), V(w_qkv.shape, bf16), V(w_out.shape, bf16), V(w_up.shape, bf16),
            V(w_down.shape, bf16), V((1, 2 * width), f32), V(tall, bf16), V(long, bf16), V(long, bf16),
            V((width // 64, rows, rows), bf16), V(wide, bf16), V(tall, f32), V(tall, bf16), V(wide, bf16),
            V(tall, f32), V((rows, 128), f32), V(tall, f32), V((chunks, rows, cut), bf16),
            V((chunks, rows, cut), bf16), V(tall, bf16), V(tall, bf16), V(tall, bf16), V(long, bf16),
            V(long, bf16), V((width, seq_len), bf16), V(tall, bf16), V(tall, bf16),
            V((2, cut // 96 * tiles, 72, 128), bf16), V((2, cut // 96 * tiles, 72, 128), bf16),
            V((2, groups, tiles, 2, 72, 128), bf16), dma((9,)), dma((4,)), dma((2,)), dma((2,)), dma((2,)),
        ],
        compiler_params=pltpu.CompilerParams(vmem_limit_bytes=60 << 20),
        name="layer",
    )(tokens, cotangent, lengths, vectors, shared, w_qkv, w_out, w_up, w_down)


class ScatterPart(Part):
    def __init__(self, net, kinds, index, order_ref, held, held_other, bufs, sems):
        super().__init__(net, kinds, index, sems)
        self.order_ref, self.held, self.held_other = order_ref, held, held_other
        self.S, self.A, self.R, self.XD, self.YD, self.X, self.Y, self.Z, self.ZX = bufs

    def at(self, ref, zo, kind, lo=0, n=None):
        return ref.at[zo, kind, pl.ds(self.base + lo, self.size if n is None else n)]

    def line(self, ref, zo, n):
        return ref.at[zo, pl.ds(self.base, n)]

    def toward(self, direction):
        return self.net.up if direction == 0 else self.net.dn

    def c_copy(self, zo, kind):
        return send(
            self.at(self.S, zo, kind), self.at(self.R, zo, kind),
            self.sem(0, zo, kind), self.sem(1, zo, kind), self.net.cn,
        )

    def xd_copy(self, zo, side):
        n = self.split(side)[1]
        return send(
            self.at(self.A, zo, 3, 0, n), self.line(self.XD, zo, n), self.sem(2, zo), self.sem(3, zo), self.net.xn
        )

    def yd_copy(self, zo, side):
        count, lo = self.split(side)
        n = count - lo
        return send(
            self.at(self.A, zo, 3, lo, n), self.line(self.YD, zo, n), self.sem(4, zo), self.sem(5, zo), self.net.yn
        )

    def x_copy(self, zo, side):
        n = self.split(side)[0]
        return send(
            self.at(self.A, zo, 1, 0, n), self.line(self.X, zo, n), self.sem(6, zo), self.sem(7, zo), self.net.xn
        )

    def y_copy(self, zo, side):
        n = self.split(side)[0]
        return send(
            self.at(self.A, zo, 2, 0, n), self.line(self.Y, zo, n), self.sem(8, zo), self.sem(9, zo), self.net.yn
        )

    def z_copy(self, zo, direction):
        return send(
            self.at(self.A, zo, 0), self.at(self.Z, zo, direction),
            self.sem(10, zo), self.sem(11, zo, direction), self.toward(direction),
        )

    def late_copies(self, zo, direction):
        first = sum(n for _, n in CHUNKS[: self.index])
        for k in range(3):
            yield send(
                self.at(self.A, zo, k + 1, self.early, self.late),
                self.ZX.at[zo, direction, k, pl.ds(first, self.late)],
                self.sem(12, zo, k), self.sem(13, zo, direction, k), self.toward(direction),
            )

    def place(self, zo, kind):
        return kind // 2, (zo * 2 + self.kinds[kind][1]) * 24

    def begin(self, zo, side, these=(3, 1, 2, 0)):
        for kind in these:
            row, first = self.place(zo, kind)

            def one(i):
                self.S[zo, kind, i] = self.held_other[row][self.order_ref[first + i]]

            rounds(self.base, self.size, one)
            self.c_copy(zo, kind).start()

    def begin_far(self, zo, side):
        self.begin(zo, side, (3, 2))

    def begin_near(self, zo, side):
        self.begin(zo, side, (1, 0))

    def add(self, zo, kind, other, lo, n):
        def one(i):
            self.A[zo, kind, i] = self.A[zo, kind, i] + other(i)

        rounds(self.base + lo, n, one)

    def late_add(self, zo, direction):
        first = sum(n for _, n in CHUNKS[: self.index]) - self.base - self.early
        for k, copy in enumerate(self.late_copies(zo, direction)):
            copy.wait_recv()
            self.add(
                zo, k + 1, lambda i: self.ZX[zo, direction, k, i + first], self.early, self.late
            )

    def diagonal(self, zo, side):
        self.xd_copy(zo, side).start()
        self.yd_copy(zo, side).start()

    def one(self, zo, side):
        for kind in (3, 1, 2, 0):
            self.c_copy(zo, kind).wait_recv()
            row, first = self.place(zo, kind)

            def both(i):
                self.A[zo, kind, i] = self.held[row][self.order_ref[first + i]] + self.R[zo, kind, i]

            rounds(self.base, self.size, both)
            if kind == 3 and not is_own(side):
                self.diagonal(zo, side)
        if is_own(side) or side == -1:
            pl.when(self.net.has_dn)(lambda: self.late_add(zo, 0))
        if is_own(side) or side == 1:
            pl.when(self.net.has_up)(lambda: self.late_add(zo, 1))
        if is_own(side):
            self.diagonal(zo, side)
        else:
            for copy in self.late_copies(zo, 0 if side == -1 else 1):
                copy.start()

    def two(self, zo, side):
        count, lo = self.split(side)
        self.yd_copy(zo, side).wait_recv()
        self.add(zo, 1, lambda i: self.YD[zo, i - lo], lo, count - lo)
        self.x_copy(zo, side).start()
        self.xd_copy(zo, side).wait_recv()
        self.add(zo, 2, lambda i: self.XD[zo, i], 0, lo)
        self.y_copy(zo, side).start()

    def three(self, zo, side):
        self.x_copy(zo, side).wait_recv()
        self.y_copy(zo, side).wait_recv()
        self.add(
            zo, 0, lambda i: (self.X[zo, i].astype(f32) + self.Y[zo, i].astype(f32)).astype(bf16), 0, self.split(side)[0]
        )
        if is_own(side):
            return

        def more(direction):
            self.z_copy(zo, direction).wait_recv()
            self.add(zo, 0, lambda i: self.Z[zo, direction, i], 0, self.size)

        if side == -1:
            pl.when(self.net.has_dn)(lambda: more(0))
            self.z_copy(zo, 0).start()
        else:
            pl.when(self.net.has_up)(lambda: more(1))
            self.z_copy(zo, 1).start()

    def total(self, zo):
        pl.when(self.net.has_dn)(lambda: self.z_copy(zo, 0).wait_recv())
        pl.when(self.net.has_up)(lambda: self.z_copy(zo, 1).wait_recv())

    def sent(self, zo, side):
        for kind in range(4):
            self.c_copy(zo, kind).wait_send()
        self.xd_copy(zo, side).wait_send()
        self.yd_copy(zo, side).wait_send()
        self.x_copy(zo, side).wait_send()
        self.y_copy(zo, side).wait_send()
        if is_own(side):
            return
        self.z_copy(zo, 0).wait_send()
        for copy in self.late_copies(zo, 0):
            copy.wait_send()


def rounds(first, count, fn):
    wide = next(n for n in (6, 5, 4, 3, 2, 1) if count % n == 0)

    def body(i, _):
        for j in range(wide):
            fn(first + wide * i + j)
        return 0

    lax.fori_loop(0, count // wide, body, 0)


def scatter_kernel(
    nz, order_ref, tq_ref, to_ref, tu_ref, td_ref, other_ref, local_ref, shared_ref,
    tile_o, dx_o, local_o, shared_o,
    TAN, TAF, TBN, TBF, S, A, R, XD, YD, X, Y, Z, ZX, la, lb, sa, sb,
    tsem, dxs, vs, vr, *sems,
):
    net = Net(nz)
    z, x, y, c, m, d = net.z, net.x, net.y, net.c, net.m, net.d
    my = (1 - y) * 2 + c
    far = (lax.rem(z + 2, nz) * 2 + x, m)
    near = ((z + 1 - 2 * (z % 2)) * 2 + x, m)

    def loads(held, group):
        first = 0
        for i, src in enumerate((tq_ref, to_ref, tu_ref, td_ref)):
            count = src.shape[1]
            yield pltpu.make_async_copy(
                src.at[group], held.at[pl.ds(first, count)], tsem.at[group, i]
            )
            first += count

    groups = (
        (TBF, (1 - y) * 2 + 1 - c), (TBN, y * 2 + 1 - c), (TAF, my), (TAN, m),
    )
    for held, group in groups:
        for copy in loads(held, group):
            copy.start()

    def loaded(i):
        for copy in loads(*groups[i]):
            copy.wait()

    net.greet()
    kinds = ((m, x), (m, 1 - x), (my, x), (my, 1 - x))
    bufs = (S, A, R, XD, YD, X, Y, Z, ZX)
    parts = [ScatterPart(net, kinds, i, order_ref, (TAN, TAF), (TBN, TBF), bufs, sems) for i in range(len(CHUNKS))]

    def step_of(distance, name):
        def run(zo, side):
            for part in parts:
                getattr(part, name)(zo, side)

        each(net, distance, run)

    dx_copy = send(other_ref, dx_o, dxs.at[0], dxs.at[1], net.cn)
    peers = (net.cn, net.xn, net.yn, near, far)

    def v_copies(k):
        return (
            send(la.at[k], lb.at[k], vs.at[k, 0], vr.at[k, 0], peers[k]),
            send(sa.at[k], sb.at[k], vs.at[k, 1], vr.at[k, 1], peers[k]),
        )

    def v_start(k):
        for copy in v_copies(k):
            copy.start()

    def v_finish(k):
        for copy in v_copies(k):
            copy.wait_recv()
        la[k + 1] = la[k] + lb[k]
        sa[k + 1] = sa[k] + sb[k]

    la[0] = local_ref[...]
    sa[0] = shared_ref[...]
    net.await_all()
    loaded(0)
    step_of(nz - 1, "begin_far")
    loaded(1)
    step_of(nz - 1, "begin_near")
    loaded(2)
    loaded(3)
    v_start(0)
    for turn_no in range(nz + 2):
        if turn_no + 1 < nz:
            step_of(nz - 2 - turn_no, "begin")
        if turn_no < nz:
            step_of(nz - 1 - turn_no, "one")
        if turn_no == 0:
            dx_copy.start()
        if 0 <= turn_no - 1 < nz:
            step_of(nz - turn_no, "two")
        if 0 <= turn_no - 2:
            step_of(nz + 1 - turn_no, "three")
        if turn_no < 5:
            v_finish(turn_no)
            if turn_no < 4:
                v_start(turn_no + 1)
    local_o[...] = la[5]
    shared_o[...] = sa[5]
    dx_copy.wait_recv()

    for part in parts:
        part.total(z)

    def finish(i):
        total = A[z, 0, i].astype(f32)
        total = total + jnp.where(net.has_dn, Z[z, 0, i].astype(f32), 0.0)
        tile_o[i] = total + jnp.where(net.has_up, Z[z, 1, i].astype(f32), 0.0)

    rounds(0, 24, finish)
    for step in range(nz):
        step_of(step, "sent")
    dx_copy.wait_send()
    for k in range(5):
        for copy in v_copies(k):
            copy.wait_send()


def scatter_grads(nz, order, parts, other, local, shared):
    dma = pltpu.SemaphoreType.DMA
    vm = pl.BlockSpec(memory_space=pltpu.VMEM)
    block = lambda *lead: pltpu.VMEM((*lead, 72, 128), bf16)
    anywhere = pl.BlockSpec(memory_space=pl.ANY)
    return pl.pallas_call(
        functools.partial(scatter_kernel, nz),
        out_shape=[
            jax.ShapeDtypeStruct((24, 72, 128), f32),
            jax.ShapeDtypeStruct(other.shape, bf16),
            jax.ShapeDtypeStruct(local.shape, f32),
            jax.ShapeDtypeStruct(shared.shape, f32),
        ],
        in_specs=[pl.BlockSpec(memory_space=pltpu.SMEM)] + [anywhere] * 5 + [vm] * 2,
        out_specs=[vm, anywhere, vm, vm],
        scratch_shapes=[
            block(48 * nz), block(48 * nz), block(48 * nz), block(48 * nz), block(nz, 4, 24), block(nz, 4, 24), block(nz, 4, 24),
            block(nz, 24), block(nz, 24), block(nz, 24), block(nz, 24), block(nz, 2, 24),
            block(nz, 2, 3, sum(late for _, late in CHUNKS)),
            pltpu.VMEM((6, *local.shape), f32), pltpu.VMEM((5, *local.shape), f32),
            pltpu.VMEM((6, *shared.shape), f32), pltpu.VMEM((5, *shared.shape), f32),
            dma((4, 4)), dma((2,)), dma((5, 2)), dma((5, 2)),
        ]
        + [
            dma((len(CHUNKS), nz, *tail))
            for tail in ((4,), (4,), *([()] * 9), (2,), (3,), (2, 3))
        ],
        compiler_params=pltpu.CompilerParams(
            collective_id=1, has_side_effects=True, vmem_limit_bytes=60 << 20
        ),
        name="scatter_grads",
    )(order, *parts, other, local, shared)


STEP = 5
BETA_ONE = 0.5
BETA_TWO = 0.5
ADAM_EPS = 1e-08
RATE_TILES = 0.04
RATE_VECTORS = 0.2
DECAY = 0.01


def adam(grad, first, second):
    first_new = BETA_ONE * first + (1.0 - BETA_ONE) * grad
    second_new = BETA_TWO * second + (1.0 - BETA_TWO) * grad * grad
    step_dir = (
        first_new
        / (1.0 - BETA_ONE**STEP)
        / (jnp.sqrt(second_new / (1.0 - BETA_TWO**STEP)) + ADAM_EPS)
    )
    return (first_new, second_new, step_dir)


def update_kernel(
    order_ref, own_ref, came_ref, grad_ref, first_ref, second_ref, left_ref, right_ref, master_ref,
    lg_ref, lv_ref, lf_ref, ls_ref, sg_ref, sv_ref, sf_ref, ss_ref,
    o_own, o_grad, o_first, o_second, o_weight, o_lg, o_lf, o_ls, o_lv, o_sg, o_sf, o_ss, o_sv,
):
    @pl.when(pl.program_id(0) == 0)
    def _():
        local = lg_ref[lax.axis_index("mp")]
        first, second, step_dir = adam(local, lf_ref[...], ls_ref[...])
        o_lg[...] = local
        o_lf[...] = first
        o_ls[...] = second
        o_lv[...] = lv_ref[...] - RATE_VECTORS * step_dir
        shared = sg_ref[...]
        first, second, step_dir = adam(shared, sf_ref[...], ss_ref[...])
        o_sg[...] = shared
        o_sf[...] = first
        o_ss[...] = second
        o_sv[...] = sv_ref[...] - RATE_VECTORS * step_dir

    o_own[...] = own_ref[...] + came_ref[...].astype(f32)
    every = range(grad_ref.shape[0])
    edge = left_ref.shape[-1]
    place_at = (lax.axis_index("dp") * pl.num_programs(0) + pl.program_id(0)) * grad_ref.shape[0]
    grads = []
    for i in every:
        j = part_of(lax.axis_index("mp"), order_ref[place_at + i])
        wire = grad_ref[i]
        tile = jnp.concatenate([wire, rest_of(wire, free_of(j))], 0)
        grads.append(turned(tile, j, -1)[:, :edge])
    left = [left_ref[i].astype(bf16) for i in every]
    right = [right_ref[i].astype(bf16) for i in every]
    for i in every:
        o_grad[i] = grads[i]
    half = [nn(grads[i].astype(bf16), right[i]).astype(bf16) for i in every]
    rotated = [tn(left[i], half[i]) for i in every]
    moved = [adam(rotated[i], first_ref[i], second_ref[i]) for i in every]
    for i in every:
        o_first[i] = moved[i][0]
        o_second[i] = moved[i][1]
    half = [nn(left[i], moved[i][2].astype(bf16)).astype(bf16) for i in every]
    for i in every:
        turn_back = nt(half[i], right[i])
        master = master_ref[i]
        o_weight[i] = master - RATE_TILES * (turn_back + DECAY * master)


def update(order, own, came, grad, first, second, left, right, master, local, shared):
    count, edge = first.shape[:2]
    part = 12 if count % 12 == 0 else count
    tile = lambda rows, lanes: pl.BlockSpec((part, rows, lanes), lambda i: (i, 0, 0))
    whole = lambda v: pl.BlockSpec(v.shape, lambda i: (0,) * v.ndim)
    band = pl.BlockSpec((own.shape[0] * part // count, own.shape[1]), lambda i: (i, 0))
    out = lambda v: jax.ShapeDtypeStruct(v.shape, f32)
    return pl.pallas_call(
        update_kernel,
        grid=(count // part,),
        in_specs=[pl.BlockSpec(memory_space=pltpu.SMEM), band, band, tile(*grad.shape[1:])]
        + [tile(edge, edge)] * 5 + [whole(v) for v in (*local, *shared)],
        out_specs=[band] + [tile(edge, edge)] * 4 + [whole(local[1])] * 4 + [whole(shared[1])] * 4,
        out_shape=[out(own)] + [out(first)] * 4 + [out(local[1])] * 4 + [out(shared[1])] * 4,
        compiler_params=pltpu.CompilerParams(vmem_limit_bytes=58 << 20),
        name="update",
    )(order, own, came, grad, first, second, left, right, master, *local, *shared)


def from_tiles(tile_set, row_count, col_count):
    edge = tile_set.shape[-1]
    return (
        tile_set.reshape(row_count // edge, col_count // edge, edge, edge)
        .transpose(0, 2, 1, 3)
        .reshape(row_count, col_count)
    )


def plain_weights(tile_order, master, local):
    tiles = lax.all_gather(master.astype(bf16), "dp", axis=0, tiled=True)
    tiles = lax.all_gather(tiles, "mp", axis=0)
    count = tile_order.shape[0]
    inverse = jnp.zeros((count,), jnp.int32).at[tile_order].set(jnp.arange(count, dtype=jnp.int32))
    natural = tiles[:, inverse]
    dense = []
    for rows, cols, where in GRIDS:
        pieces = []
        for r in range(rows):
            pick = [where(r, j) for j in range(cols)]
            groups = jnp.asarray([p for p, _ in pick], jnp.int32)
            numbers = jnp.asarray([n for _, n in pick], jnp.int32)
            pieces.append(natural[groups, numbers].transpose(1, 0, 2).reshape(96, cols * 96))
        dense.append(jnp.concatenate(pieces, 0))
    return (*dense, lax.all_gather(local, "mp", axis=0))


def plain_scatter(order, parts, other, local, shared):
    tiles = jnp.concatenate(parts, 1)[:, order]
    mine = lax.psum_scatter(tiles, "mp", scatter_dimension=0, tiled=False).astype(f32)
    owned = lax.psum_scatter(mine, "dp", scatter_dimension=0, tiled=True)
    count = lax.axis_size("mp")
    swapped = lax.ppermute(other, "mp", [(i, i ^ 1) for i in range(count)])
    local_sum, shared_sum = lax.psum((local, shared), ("dp", "mp"))
    return owned, swapped, local_sum, shared_sum


def shards(
    tokens,
    cotangent,
    lengths,
    tile_order,
    master,
    first_moment,
    second_moment,
    basis_left,
    basis_right,
    local_vec,
    local_first,
    local_second,
    shared_vec,
    shared_first,
    shared_second,
):
    group_count = lax.axis_size("mp")
    group_index = lax.axis_index("mp")
    owners = lax.axis_size("dp")
    row_total, width = tokens.shape
    rows = row_total // group_count
    per_owner = master.shape[1]
    nz = owners // 2
    routed = per_owner == 24 and nz == 4 and group_count == 4

    if routed:
        w_qkv, w_out, w_up, w_down, vectors = gather_weights(
            nz, tile_order, master[0], local_vec
        )
    else:
        w_qkv, w_out, w_up, w_down, vectors = plain_weights(tile_order, master[0], local_vec)
    output, tq, to, tu, td, own, other, local_terms, shared_terms = layer(
        tokens, cotangent, lengths, vectors, shared_vec, w_qkv, w_out, w_up, w_down, rows
    )
    parts = [t.reshape(group_count, -1, 72, 128) for t in (tq, to, tu, td)]
    if routed:
        owned, came, local_sum, shared_grad = scatter_grads(
            nz, tile_order, parts, other, local_terms, shared_terms
        )
    else:
        owned, came, local_sum, shared_grad = plain_scatter(
            tile_order, parts, other, local_terms, shared_terms
        )
    input_grad, *tiles = update(
        tile_order, own, came, owned, first_moment[0], second_moment[0], basis_left[0], basis_right[0], master[0],
        (local_sum, local_vec, local_first, local_second),
        (shared_grad, shared_vec, shared_first, shared_second),
    )
    return (output, input_grad, *(t[None] for t in tiles[:4]), *tiles[4:])


def solution(mesh):
    placed = (
        P("dp", None),
        P("dp", None),
        P("dp"),
        P(),
        P("mp", "dp", None, None),
        P("mp", "dp", None, None),
        P("mp", "dp", None, None),
        P("mp", "dp", None, None),
        P("mp", "dp", None, None),
        P("mp", None),
        P("mp", None),
        P("mp", None),
        P(),
        P(),
        P(),
    )
    return jax.shard_map(
        shards,
        mesh=mesh,
        in_specs=placed,
        out_specs=(
            P(("dp", "mp"), None),
            P(("dp", "mp"), None),
            P("mp", "dp", None, None),
            P("mp", "dp", None, None),
            P("mp", "dp", None, None),
            P("mp", "dp", None, None),
            P("mp", None),
            P("mp", None),
            P("mp", None),
            P("mp", None),
            P(),
            P(),
            P(),
            P(),
        ),
        check_vma=False,
    )
```

```python
import functools
import jax
import jax.numpy as jnp
from jax import lax
from jax.experimental import pallas as pl
from jax.experimental.pallas import tpu as pltpu
from jax.sharding import PartitionSpec as P

MESH = pl.DeviceIdType.MESH
f32 = jnp.float32
bf16 = jnp.bfloat16


def lanes_of(shape):
    return lax.broadcasted_iota(jnp.int32, shape, len(shape) - 1)


def turn(v, amount):
    return pltpu.roll(v, amount, v.ndim - 1)


def free_of(j):
    return (3 * j + 3) % 4


def part_of(group, number):
    return jnp.where(number < 48, 2 * group + number % 2, number) % 4


def groups_of(shape):
    return lanes_of(shape) // 32


def to_wire(tile, free):
    rest = tile[72:96]
    side = jnp.concatenate([turn(rest, 96), turn(rest, 64), turn(rest, 32)], 0)
    return jnp.where(groups_of(side.shape) == free, side, tile[:72])


def rest_of(wire, free):
    group = groups_of((24, 128))
    first, second, third = turn(wire[:24], 32), turn(wire[24:48], 64), turn(wire[48:72], 96)
    return jnp.where(
        group == (free + 1) % 4, first, jnp.where(group == (free + 2) % 4, second, third)
    )


def turned(tile, j, sign):
    half = (j == 1) | (j == 2) if sign > 0 else j >= 2
    out = jnp.where(half, turn(tile, 64), tile)
    return jnp.where(j % 2 == 1, turn(out, 32), out)


def join_four(wires):
    lane, group = lanes_of((72, 128)), groups_of((24, 128))
    a, b, c, d = wires
    tops = [jnp.where(lane < 96, a, b), jnp.where(lane < 64, b, c), jnp.where(lane < 32, c, d)]
    rests = []
    for i in range(3):
        at = slice(24 * i, 24 * i + 24)
        mixed = jnp.where(
            group == 3, a[at], jnp.where(group == 2, b[at], jnp.where(group == 1, c[at], d[at]))
        )
        rests.append(turn(mixed, 32 * (i + 1)))
    pieces = []
    for k in range(3):
        index = (group + k) % 3
        rest = jnp.where(index == 0, rests[0], jnp.where(index == 1, rests[1], rests[2]))
        pieces.append(jnp.concatenate([tops[k], rest], 0))
    return pieces


def split_four(pieces):
    lane, group = lanes_of((72, 128)), groups_of((24, 128))
    a, b, c = (p[:72] for p in pieces)
    rests = [p[72:] for p in pieces]
    sides = []
    for i in range(3):
        mixed = jnp.where(
            group % 3 == 0,
            rests[i],
            jnp.where(group == 1, rests[(i - 1) % 3], rests[(i - 2) % 3]),
        )
        sides.append(turn(mixed, 96 - 32 * i))
    side = jnp.concatenate(sides, 0)
    tops = [a, jnp.where(lane < 64, b, a), jnp.where(lane < 32, c, b), c]
    return [jnp.where(lane // 32 == 3 - t, side, tops[t]) for t in range(4)]


def place():
    d, m = lax.axis_index("dp"), lax.axis_index("mp")
    return d // 2, d % 2, m // 2, m % 2


class Net:
    def __init__(self, nz):
        self.nz = nz
        self.z, self.x, self.y, self.c = place()
        self.d = self.z * 2 + self.x
        self.m = self.y * 2 + self.c
        self.xn = (self.z * 2 + 1 - self.x, self.m)
        self.yn = (self.d, (1 - self.y) * 2 + self.c)
        self.cn = (self.d, self.y * 2 + 1 - self.c)
        self.up = (self.d + 2, self.m)
        self.dn = (self.d - 2, self.m)
        self.has_up = self.z < nz - 1
        self.has_dn = self.z > 0

    def peers(self):
        others = [(lax.rem(self.z + k, self.nz) * 2 + self.x, self.m) for k in range(1, self.nz)]
        return [self.xn, self.yn, self.cn] + others

    def greet(self):
        for peer in self.peers():
            pl.semaphore_signal(
                pltpu.get_barrier_semaphore(), inc=1, device_id=peer, device_id_type=MESH
            )

    def await_all(self):
        pl.semaphore_wait(pltpu.get_barrier_semaphore(), len(self.peers()))


def send(src, dst, ss, rs, peer):
    return pltpu.make_async_remote_copy(
        src_ref=src, dst_ref=dst, send_sem=ss, recv_sem=rs, device_id=peer, device_id_type=MESH
    )


def tile_qkv(r, j):
    return (j % 8) // 2, r * 6 + (j // 8) * 2 + j % 2


def tile_out(r, j):
    return r // 2, 48 + (r % 2) * 8 + j


def tile_up(r, j):
    return j // 8, 64 + r * 8 + j % 8


def tile_down(r, j):
    return r // 8, 128 + (r % 8) * 8 + j


GRIDS = ((8, 24, tile_qkv), (8, 8, tile_out), (8, 32, tile_up), (32, 8, tile_down))


CHUNKS = ((24, 4),)


def is_own(side):
    return isinstance(side, int) and side == 0


def each(net, step, fn):
    if step == 0:
        fn(net.z, 0)
        return

    @pl.when(net.z >= step)
    def _():
        fn(net.z - step, 1)

    @pl.when(net.z + step < net.nz)
    def _():
        fn(net.z + step, -1)


class Part:
    def __init__(self, net, kinds, index, sems):
        self.net, self.kinds, self.index, self.sems = net, kinds, index, sems
        self.size, self.late = CHUNKS[index]
        self.base = sum(n for n, _ in CHUNKS[:index])
        self.early = self.size - self.late

    def sem(self, i, *at):
        return self.sems[i].at[(self.index, *at)]

    def split(self, side):
        count = self.size if is_own(side) else self.early
        return count, (count + self.index % 2) // 2


class GatherPart(Part):
    def __init__(self, net, kinds, index, G, sems):
        super().__init__(net, kinds, index, sems)
        self.G = G

    def slot(self, kind, zo, lo=0, n=None, shift=0):
        mo, xo = self.kinds[kind]
        n = self.size if n is None else n
        return self.G.at[mo + shift, pl.ds((zo * 2 + xo) * 24 + self.base + lo, n)]

    def go(self, s, i, i_at, j, j_at, peer):
        return send(s, s, self.sem(i, *i_at), self.sem(j, *j_at), peer)

    def toward(self, direction):
        return self.net.up if direction == 0 else self.net.dn

    def z_copy(self, zo, direction):
        return self.go(self.slot(0, zo), 0, (zo, direction), 1, (zo,), self.toward(direction))

    def late_copies(self, zo, direction):
        for k in range(3):
            s = self.slot(k + 1, zo, self.early, self.late)
            yield self.go(s, 12, (zo, k, direction), 13, (zo, k), self.toward(direction))

    def c_copy(self, zo, kind, side, shift=0):
        n = self.size if kind == 0 or is_own(side) else self.early
        return self.go(self.slot(kind, zo, 0, n, shift), 10, (zo, kind), 11, (zo, kind), self.net.cn)

    def c_late(self, zo, k, shift=0):
        s = self.slot(k + 1, zo, self.early, self.late, shift)
        return self.go(s, 14, (zo, k), 15, (zo, k), self.net.cn)

    def x_copy(self, zo, kind, side):
        return self.go(self.slot(kind, zo, 0, self.split(side)[0]), 2, (zo,), 3, (zo,), self.net.xn)

    def y_copy(self, zo, kind, side):
        return self.go(self.slot(kind, zo, 0, self.split(side)[0]), 4, (zo,), 5, (zo,), self.net.yn)

    def xd_copy(self, zo, kind, side):
        return self.go(self.slot(kind, zo, 0, self.split(side)[1]), 6, (zo,), 7, (zo,), self.net.xn)

    def yd_copy(self, zo, kind, side):
        count, lo = self.split(side)
        return self.go(self.slot(kind, zo, lo, count - lo), 8, (zo,), 9, (zo,), self.net.yn)

    def onward(self, side, act):
        if is_own(side) or side == 1:
            pl.when(self.net.has_up)(lambda: act(0))
        if is_own(side) or side == -1:
            pl.when(self.net.has_dn)(lambda: act(1))

    def arrive(self, zo, side):
        if not is_own(side):
            self.z_copy(zo, 0).wait_recv()
        self.onward(side, lambda direction: self.z_copy(zo, direction).start())
        self.x_copy(zo, 0, side).start()
        self.y_copy(zo, 0, side).start()
        self.c_copy(zo, 0, side).start()

    def diag(self, zo, side):
        self.x_copy(zo, 1, side).wait_recv()
        self.yd_copy(zo, 1, side).start()
        self.c_copy(zo, 1, side).start()
        self.y_copy(zo, 2, side).wait_recv()
        self.xd_copy(zo, 2, side).start()
        self.c_copy(zo, 2, side).start()

    def fin(self, zo, side):
        self.xd_copy(zo, 3, side).wait_recv()
        self.yd_copy(zo, 3, side).wait_recv()
        self.c_copy(zo, 3, side).start()

    def last(self, zo, side):
        if not is_own(side):
            for copy in self.late_copies(zo, 0):
                copy.wait_recv()

        def act(direction):
            for copy in self.late_copies(zo, direction):
                copy.start()

        self.onward(side, act)
        if not is_own(side):
            for k in range(3):
                self.c_late(zo, k).start()

    def other_core(self, zo, side):
        flip = 1 - 2 * self.net.c
        for kind in range(4):
            self.c_copy(zo, kind, side, flip).wait_recv()
            if kind and not is_own(side):
                self.c_late(zo, kind - 1, flip).wait_recv()

    def sent(self, zo, side):
        self.x_copy(zo, 0, side).wait_send()
        self.y_copy(zo, 0, side).wait_send()
        self.yd_copy(zo, 1, side).wait_send()
        self.xd_copy(zo, 2, side).wait_send()
        for kind in range(4):
            self.c_copy(zo, kind, side).wait_send()
        if not is_own(side):
            for k in range(3):
                self.c_late(zo, k).wait_send()

        def done(direction):
            self.z_copy(zo, direction).wait_send()
            for copy in self.late_copies(zo, direction):
                copy.wait_send()

        self.onward(side, done)


def gather_kernel(
    nz, order_ref, row_ref, master_ref, local_ref, o_qkv, o_out, o_up, o_down, o_local,
    G, src_ref, inverse, LV, d_qkv, d_out, d_up, d_down,
    outs, lvs, lvr, inv_sem, *sems,
):
    net = Net(nz)
    z, x, y, c, m = net.z, net.x, net.y, net.c, net.m
    my = (1 - y) * 2 + c
    full = 24
    net.greet()

    def stage(i, _):
        tile = jnp.concatenate([master_ref[i], jnp.zeros((96, 32), f32)], axis=-1)
        j = part_of(m, order_ref[net.d * full + i])
        tile = turned(tile, j, 1)
        G[m, net.d * full + i] = to_wire(tile, free_of(j)).astype(bf16)
        return 0

    lax.fori_loop(0, full, stage, 0)
    LV[m] = local_ref[...]
    net.await_all()
    lv_y = send(LV.at[m], LV.at[m], lvs.at[0], lvr.at[0], net.yn)
    lv_c = send(LV.at[m], LV.at[m], lvs.at[1], lvr.at[1], net.cn)
    lv_d = send(LV.at[my], LV.at[my], lvs.at[2], lvr.at[2], net.cn)

    kinds = ((m, x), (m, 1 - x), (my, x), (my, 1 - x))
    flip = 1 - 2 * c
    parts = [GatherPart(net, kinds, i, G, sems) for i in range(len(CHUNKS))]

    def step_of(distance, name, reverse=False):
        def run(zo, side):
            for part in parts:
                getattr(part, name)(zo, side)

        each(net, distance, run)

    def forwarded(zo, side):
        for part in parts:
            part.other_core(zo, side)

    step_of(0, "arrive")
    lv_y.start()
    lv_c.start()
    step_of(1, "arrive")
    step_of(0, "diag")
    send(LV.at[my], LV.at[my], lvs.at[0], lvr.at[0], net.yn).wait_recv()
    lv_d.start()
    step_of(2, "arrive")
    step_of(1, "diag")
    step_of(0, "fin")
    step_of(0, "last")
    step_of(3, "arrive")
    step_of(1, "fin")
    step_of(1, "last")
    step_of(2, "diag")
    step_of(2, "last")
    step_of(2, "fin")
    step_of(3, "diag")
    step_of(3, "last")
    step_of(3, "fin")
    for step in range(nz):
        step_of(step, "other_core")
    count = row_ref.shape[1]
    down = lax.broadcasted_iota(jnp.int32, (count, count), 0)
    along = lax.broadcasted_iota(jnp.int32, (count, count), 1)
    column = jnp.sum(jnp.where(down == along, row_ref[...], 0), 1, keepdims=True)
    inverse[...] = jnp.max(jnp.where(column == along, down, 0), 0, keepdims=True)
    to_scalars = pltpu.make_async_copy(inverse, src_ref, inv_sem.at[0])
    to_scalars.start()
    mc = m + flip
    send(LV.at[mc], LV.at[mc], lvs.at[1], lvr.at[1], net.cn).wait_recv()
    mc = my + flip
    send(LV.at[mc], LV.at[mc], lvs.at[2], lvr.at[2], net.cn).wait_recv()
    o_local[...] = LV[...]
    to_scalars.wait()

    copies = []
    for i, ((rows, cols, where), dense, out) in enumerate(
        zip(GRIDS, (d_qkv, d_out, d_up, d_down), (o_qkv, o_out, o_up, o_down))
    ):
        def fill(r, _):
            for g in range(cols // 4):
                tiles = []
                for t in range(4):
                    p, n = where(r, 4 * g + t)
                    tiles.append(G[p, src_ref[0, n]])
                for k, piece in enumerate(join_four(tiles)):
                    dense[pl.ds(pl.multiple_of(r * 96, 96), 96), pl.ds(384 * g + 128 * k, 128)] = (
                        piece.astype(bf16)
                    )
            band = pl.ds(pl.multiple_of(r * 96, 96), 96)
            pltpu.make_async_copy(dense.at[band], out.at[band], outs.at[i]).start()
            return 0

        lax.fori_loop(0, rows, fill, 0)
        copies.append(pltpu.make_async_copy(dense, out, outs.at[i]))

    for step in range(nz):
        step_of(step, "sent")
    lv_y.wait_send()
    lv_c.wait_send()
    lv_d.wait_send()
    for copy in copies:
        copy.wait()


def gather_weights(nz, order, master, local):
    dma = pltpu.SemaphoreType.DMA
    shapes = [(r * 96, c * 96) for r, c, _ in GRIDS]
    return pl.pallas_call(
        functools.partial(gather_kernel, nz),
        out_shape=[jax.ShapeDtypeStruct(s, bf16) for s in shapes]
        + [jax.ShapeDtypeStruct((4, *local.shape), f32)],
        in_specs=[pl.BlockSpec(memory_space=pltpu.SMEM)] + [pl.BlockSpec(memory_space=pltpu.VMEM)] * 3,
        out_specs=[pl.BlockSpec(memory_space=pl.ANY)] * 4 + [pl.BlockSpec(memory_space=pltpu.VMEM)],
        scratch_shapes=[pltpu.VMEM((4, 2 * nz * 24, 72, 128), bf16), pltpu.SMEM((1, 2 * nz * 24), jnp.int32),
            pltpu.VMEM((1, 2 * nz * 24), jnp.int32), pltpu.VMEM((4, *local.shape), f32)]
        + [pltpu.VMEM(s, bf16) for s in shapes]
        + [dma((4,)), dma((3,)), dma((3,)), dma((1,))]
        + [dma((len(CHUNKS), nz, *tail)) for tail in ((2,), (), *([()] * 8), (4,), (4,), (3, 2), (3,), (3,), (3,))],
        compiler_params=pltpu.CompilerParams(
            collective_id=0, has_side_effects=True, vmem_limit_bytes=56 << 20
        ),
        name="gather_weights",
    )(order, order.reshape(1, -1), master, local)


NEG_BIG = -1e30
NORM_EPS = 1e-05
ROOT_HALF = 0.7071067811865476
PHI_SCALE = 0.3989422804014327


def nt(a, b):
    return lax.dot_general(a, b, (((1,), (1,)), ((), ())), preferred_element_type=f32)


def tn(a, b):
    return lax.dot_general(a, b, (((0,), (0,)), ((), ())), preferred_element_type=f32)


def nn(a, b):
    return jnp.dot(a, b, preferred_element_type=f32)


def standard(values):
    centre = values - jnp.mean(values, -1, keepdims=True)
    scale = lax.rsqrt(jnp.mean(centre * centre, -1, keepdims=True) + NORM_EPS)
    return centre * scale, scale


def standard_back(grad, normed, scale, gain):
    inner = grad * gain
    return scale * (
        inner - jnp.mean(inner, -1, keepdims=True) - normed * jnp.mean(inner * normed, -1, keepdims=True)
    )


def col_sum(values):
    return jnp.sum(values, 0, keepdims=True)


def layer_kernel(
    tokens_ref, cot_ref, lengths_ref, vec_ref, sv_ref, wq_ref, wo_ref, wu_ref, wd_ref,
    out_ref, tq_ref, to_ref, tu_ref, td_ref, own_ref, other_ref, dl_ref, ds_ref,
    x, cot, wqkv, wout, wup, wdown, bias, q, k, v, probs, o_t, hid, low, low_t, n_one, r_one, acc,
    act, slope, g_low, g_o, dq, dk, dv, x_t, out, other, su, sd, sq, loads, stores, su_sem, sd_sem, sq_sem,
):
    rows, width = q.shape
    seq_len = k.shape[0]
    chunks, _, cut = act.shape
    tiles = width // 96
    pairs = width // 128
    piece = 512
    zero = jnp.zeros((), bf16)
    member = lax.axis_index("mp")
    share = seq_len // rows
    seq, part = member // share, member % share
    length = lengths_ref[seq]
    bound = 64 * ((length + 127) // 128)
    start_b = pl.multiple_of(bound, 64)
    here = pl.ds(pl.multiple_of(part * rows, rows), rows)
    there = pl.ds(pl.multiple_of((1 - part) * rows, rows), rows)

    def load(src, dst, i):
        copy = pltpu.make_async_copy(src, dst, loads.at[i])
        copy.start()
        return copy

    get_x = load(tokens_ref.at[pl.ds(pl.multiple_of(seq * seq_len, seq_len), seq_len)], x, 0)
    get_qkv = [
        load(wq_ref.at[:, pl.ds(i * width, width)], wqkv.at[:, pl.ds(i * width, width)], 6 + i)
        for i in range(3)
    ]
    get_o = load(wo_ref, wout, 2)
    get_u = load(wu_ref, wup, 3)
    get_d = load(wd_ref, wdown, 4)
    get_c = load(cot_ref.at[pl.ds(pl.multiple_of(member * rows, rows), rows)], cot, 5)

    groups = vec_ref.shape[0]
    third = width // groups
    bias[:, :width] = jnp.concatenate([vec_ref[p][:, :third] for p in range(groups)], 1)
    bias[:, width:] = jnp.concatenate([vec_ref[p][:, third : 2 * third] for p in range(groups)], 1)

    get_x.wait()
    get_qkv[0].wait()
    q[...] = (nn(x[here, :], wqkv[:, :width]) + bias[:, :width]).astype(bf16) * jnp.asarray(0.125, bf16)

    get_qkv[1].wait()
    get_qkv[2].wait()

    def project(r, _):
        at = pl.ds(pl.multiple_of(r * rows, rows), rows)
        k[at, :] = nn(x[at, :], wqkv[:, width : 2 * width]).astype(bf16)
        v[at, :] = (nn(x[at, :], wqkv[:, 2 * width :]) + bias[:, width:]).astype(bf16)
        return 0

    lax.fori_loop(0, share, project, 0, unroll=True)

    def picks(shape, rows_at):
        row = lax.broadcasted_iota(jnp.int32, shape, rows_at) + part * rows
        lane = lax.broadcasted_iota(jnp.int32, shape, 1 - rows_at)
        return (row < bound) == (lane < 64)

    windows = ((0, bound), (start_b, length - bound))

    def forward(pair, _):
        cols = pl.ds(pl.multiple_of(pair * 128, 128), 128)
        queries = q[:, cols]
        pick = picks((rows, 128), 0)
        mine = (jnp.where(pick, queries, zero), jnp.where(pick, zero, queries))
        scores = [nt(k[pl.ds(start, rows), cols], mine[w]) for w, (start, _) in enumerate(windows)]
        outs = []
        for w, (start, limit) in enumerate(windows):
            inside = lax.broadcasted_iota(jnp.int32, scores[w].shape, 0) < limit
            masked = jnp.where(inside, scores[w], NEG_BIG)
            weight = jnp.exp(masked - jnp.max(masked, 0, keepdims=True))
            low_probs = (weight * (1.0 / jnp.sum(weight, 0, keepdims=True))).astype(bf16)
            probs[2 * pair + w] = low_probs
            outs.append(tn(v[pl.ds(start, rows), cols], low_probs))
        o_t[cols, :] = jnp.where(picks((128, rows), 1), outs[0], outs[1]).astype(bf16)
        return 0

    lax.fori_loop(0, pairs, forward, 0, unroll=3)

    def by_rows(fn):
        def body(r, _):
            fn(pl.ds(pl.multiple_of(r * piece, piece), piece), r)
            return 0

        lax.fori_loop(0, rows // piece, body, 0)

    get_o.wait()
    acc[...] = tn(o_t[...], wout[...])

    def norm_one(at, r):
        mine = pl.ds(pl.multiple_of(part * rows + r * piece, piece), piece)
        z_one = x[mine, :].astype(f32) + acc[at, :] + sv_ref[0:1, :]
        normed, scale = standard(z_one)
        hidden = normed * sv_ref[2:3, :] + sv_ref[3:4, :]
        n_one[at, :] = normed
        r_one[at, :] = jnp.broadcast_to(scale, (piece, 128))
        hid[at, :] = hidden
        low[at, :] = hidden.astype(bf16)
        acc[at, :] = jnp.zeros((piece, width), f32)

    by_rows(norm_one)
    low_t[...] = low[...].T
    get_u.wait()
    get_d.wait()

    def feed(i, _):
        at = pl.ds(pl.multiple_of(i * cut, cut), cut)
        pre = nn(low[...], wup[:, at]) + vec_ref[i, :, 2 * third :]
        phi = 0.5 * (1.0 + lax.erf(pre * ROOT_HALF))
        density = jnp.exp(-0.5 * pre * pre) * PHI_SCALE
        active = (pre * phi).astype(bf16)
        act[i] = active
        slope[i] = (phi + pre * density).astype(bf16)
        acc[...] += nn(active, wdown[at, :])
        return 0

    lax.fori_loop(0, chunks, feed, 0, unroll=4)
    get_c.wait()
    ds_ref[...] = jnp.zeros_like(ds_ref)

    def norm_two(at, r):
        z_two = hid[at, :] + acc[at, :] + sv_ref[1:2, :]
        normed, scale = standard(z_two)
        row = lax.broadcasted_iota(jnp.int32, (piece, 1), 0) + part * rows + r * piece
        valid = (row < length).astype(f32)
        out[at, :] = ((normed * sv_ref[4:5, :] + sv_ref[5:6, :]) * valid).astype(bf16)
        grad = cot[at, :].astype(f32) * valid
        back = standard_back(grad, normed, scale, sv_ref[4:5, :])
        ds_ref[4:5, :] += col_sum(grad * normed)
        ds_ref[5:6, :] += col_sum(grad)
        ds_ref[1:2, :] += col_sum(back)
        g_low[at, :] = back.astype(bf16)
        acc[at, :] = back

    by_rows(norm_two)
    put_out = pltpu.make_async_copy(out, out_ref, stores.at[0])
    put_out.start()

    def put_u(i):
        return pltpu.make_async_copy(su.at[i % 2], tu_ref.at[i], su_sem.at[i % 2])

    def put_d(i):
        return pltpu.make_async_copy(sd.at[i % 2], td_ref.at[i], sd_sem.at[i % 2])

    def cut_up(grad, keep):
        for r in range(grad.shape[0] // 96):
            for g in range(grad.shape[1] // 384):
                pieces = [
                    grad[96 * r : 96 * r + 96, 384 * g + 128 * n : 384 * g + 128 * n + 128]
                    for n in range(3)
                ]
                for t, wire in enumerate(split_four(pieces)):
                    keep(r, 4 * g + t, wire.astype(bf16))

    def feed_back(i, _):
        at = pl.ds(pl.multiple_of(i * cut, cut), cut)

        @pl.when(i >= 2)
        def _():
            put_u(i - 2).wait()
            put_d(i - 2).wait()

        grad_low = (nt(g_low[...], wdown[at, :]) * slope[i].astype(f32)).astype(bf16)
        dl_ref[i, :, 2 * third :] = col_sum(grad_low.astype(f32))
        def keep_down(r, j, wire):
            sd[i % 2, r * tiles + j] = wire

        def keep_up(r, j, wire):
            su[i % 2, r * tiles + j] = wire

        cut_up(tn(act[i], g_low[...]), keep_down)
        cut_up(nn(low_t[...], grad_low), keep_up)
        acc[...] += nt(grad_low, wup[:, at])
        put_u(i).start()
        put_d(i).start()
        return 0

    lax.fori_loop(0, chunks, feed_back, 0)

    def norm_back(at, r):
        grad = acc[at, :]
        normed = n_one[at, :]
        back = standard_back(grad, normed, r_one[at, 0:1], sv_ref[2:3, :])
        ds_ref[2:3, :] += col_sum(grad * normed)
        ds_ref[3:4, :] += col_sum(grad)
        ds_ref[0:1, :] += col_sum(back)
        acc[at, :] = back
        g_low[at, :] = back.astype(bf16)

    by_rows(norm_back)
    g_o[...] = nt(g_low[...], wout[...]).astype(bf16)

    def keep_out(r, j, wire):
        sd[0, r * tiles + j] = wire

    put_d(chunks - 2).wait()
    cut_up(nn(o_t[...], g_low[...]), keep_out)
    put_o = pltpu.make_async_copy(sd.at[0], to_ref, stores.at[1])
    put_o.start()
    dk[rows:, :] = jnp.zeros((seq_len - rows, width), bf16)
    dv[rows:, :] = jnp.zeros((seq_len - rows, width), bf16)

    def backward(pair, _):
        cols = pl.ds(pl.multiple_of(pair * 128, 128), 128)
        pick, pick_t = picks((rows, 128), 0), picks((128, rows), 1)
        queries, grads = q[:, cols], g_o[:, cols]
        grads_t = grads.T
        inner = grads_t.astype(f32) * o_t[cols, :].astype(f32)
        outs = []
        for w, (start, _) in enumerate(windows):
            at = pl.ds(start, rows)
            mine = (lambda a: jnp.where(pick, a, zero)) if w == 0 else (lambda a: jnp.where(pick, zero, a))
            mine_t = (lambda a: jnp.where(pick_t, a, jnp.zeros((), a.dtype))) if w == 0 else (lambda a: jnp.where(pick_t, jnp.zeros((), a.dtype), a))
            dot_sum = jnp.sum(mine_t(inner), 0, keepdims=True)
            grad_probs = nn(v[at, cols], mine_t(grads_t))
            these = probs[2 * pair + w]
            grad_scores = (these.astype(f32) * (grad_probs - dot_sum)).astype(bf16)
            dv[at, cols] = nn(these, mine(grads)).astype(bf16)
            dk[at, cols] = nn(grad_scores, mine(queries)).astype(bf16)
            outs.append(tn(k[at, cols], grad_scores))
        dq[:, cols] = (jnp.where(pick_t, outs[0], outs[1]) * 0.125).astype(bf16).T
        return 0

    lax.fori_loop(0, pairs, backward, 0, unroll=3)

    other[...] = (
        nt(dk[there, :], wqkv[:, width : 2 * width]) + nt(dv[there, :], wqkv[:, 2 * width :])
    ).astype(bf16)
    put_x = pltpu.make_async_copy(other, other_ref, stores.at[2])
    put_x.start()
    hid[...] = (
        acc[...]
        + nt(dq[...], wqkv[:, :width])
        + nt(dk[here, :], wqkv[:, width : 2 * width])
        + nt(dv[here, :], wqkv[:, 2 * width :])
    )
    put_own = pltpu.make_async_copy(hid, own_ref, stores.at[3])
    put_own.start()
    sum_q = col_sum(dq[...].astype(f32))
    sum_v = col_sum(dv[...].astype(f32))
    for p in range(groups):
        dl_ref[p, :, :third] = sum_q[:, third * p : third * p + third]
        dl_ref[p, :, third : 2 * third] = sum_v[:, third * p : third * p + third]

    x_t[...] = x[...].T
    puts = []
    for index, grad in enumerate((dk, dv, dq)):
        part_no = (1, 2, 0)[index]
        outer = nn(x_t[:, here] if part_no == 0 else x_t[...], grad[...])
        if index >= 2:
            puts[index - 2].wait()

        def keep(r, j, wire):
            sq[index % 2, j // 2, r, j % 2] = wire

        cut_up(outer, keep)
        put = pltpu.make_async_copy(sq.at[index % 2], tq_ref.at[:, :, part_no], sq_sem.at[index % 2])
        put.start()
        puts.append(put)
    for i in (chunks - 2, chunks - 1):
        put_u(i).wait()
    put_d(chunks - 1).wait()
    for put in (put_out, put_o, put_x, put_own, puts[-2], puts[-1]):
        put.wait()


def layer(tokens, cotangent, lengths, vectors, shared, w_qkv, w_out, w_up, w_down, rows):
    width = w_out.shape[0]
    hidden = w_up.shape[1]
    seq_len = tokens.shape[0] // lengths.shape[0]
    groups = vectors.shape[0]
    cut = hidden // groups
    chunks = groups
    tiles = width // 96
    anywhere = pl.BlockSpec(memory_space=pl.ANY)
    vm = pl.BlockSpec(memory_space=pltpu.VMEM)
    smem = pl.BlockSpec(memory_space=pltpu.SMEM)
    out = jax.ShapeDtypeStruct
    V = pltpu.VMEM
    dma = pltpu.SemaphoreType.DMA
    tall, wide, long = (rows, width), (width, rows), (seq_len, width)
    return pl.pallas_call(
        layer_kernel,
        in_specs=[anywhere, anywhere, smem, vm, vm] + [anywhere] * 4,
        out_specs=[anywhere] * 7 + [vm, vm],
        out_shape=[
            out(tall, bf16),
            out((groups, tiles, 3, 2, 72, 128), bf16),
            out((tiles * tiles, 72, 128), bf16),
            out((groups, cut // 96 * tiles, 72, 128), bf16),
            out((groups, cut // 96 * tiles, 72, 128), bf16),
            out(tall, f32),
            out(tall, bf16),
            out(vectors.shape, f32),
            out(shared.shape, f32),
        ],
        scratch_shapes=[
            V(long, bf16), V(tall, bf16), V(w_qkv.shape, bf16), V(w_out.shape, bf16), V(w_up.shape, bf16),
            V(w_down.shape, bf16), V((1, 2 * width), f32), V(tall, bf16), V(long, bf16), V(long, bf16),
            V((width // 64, rows, rows), bf16), V(wide, bf16), V(tall, f32), V(tall, bf16), V(wide, bf16),
            V(tall, f32), V((rows, 128), f32), V(tall, f32), V((chunks, rows, cut), bf16),
            V((chunks, rows, cut), bf16), V(tall, bf16), V(tall, bf16), V(tall, bf16), V(long, bf16),
            V(long, bf16), V((width, seq_len), bf16), V(tall, bf16), V(tall, bf16),
            V((2, cut // 96 * tiles, 72, 128), bf16), V((2, cut // 96 * tiles, 72, 128), bf16),
            V((2, groups, tiles, 2, 72, 128), bf16), dma((9,)), dma((4,)), dma((2,)), dma((2,)), dma((2,)),
        ],
        compiler_params=pltpu.CompilerParams(vmem_limit_bytes=60 << 20),
        name="layer",
    )(tokens, cotangent, lengths, vectors, shared, w_qkv, w_out, w_up, w_down)


class ScatterPart(Part):
    def __init__(self, net, kinds, index, order_ref, held, held_other, bufs, sems):
        super().__init__(net, kinds, index, sems)
        self.order_ref, self.held, self.held_other = order_ref, held, held_other
        self.S, self.A, self.R, self.XD, self.YD, self.X, self.Y, self.Z, self.ZX = bufs

    def at(self, ref, zo, kind, lo=0, n=None):
        return ref.at[zo, kind, pl.ds(self.base + lo, self.size if n is None else n)]

    def line(self, ref, zo, n):
        return ref.at[zo, pl.ds(self.base, n)]

    def toward(self, direction):
        return self.net.up if direction == 0 else self.net.dn

    def c_copy(self, zo, kind):
        return send(
            self.at(self.S, zo, kind), self.at(self.R, zo, kind),
            self.sem(0, zo, kind), self.sem(1, zo, kind), self.net.cn,
        )

    def xd_copy(self, zo, side):
        n = self.split(side)[1]
        return send(
            self.at(self.A, zo, 3, 0, n), self.line(self.XD, zo, n), self.sem(2, zo), self.sem(3, zo), self.net.xn
        )

    def yd_copy(self, zo, side):
        count, lo = self.split(side)
        n = count - lo
        return send(
            self.at(self.A, zo, 3, lo, n), self.line(self.YD, zo, n), self.sem(4, zo), self.sem(5, zo), self.net.yn
        )

    def x_copy(self, zo, side):
        n = self.split(side)[0]
        return send(
            self.at(self.A, zo, 1, 0, n), self.line(self.X, zo, n), self.sem(6, zo), self.sem(7, zo), self.net.xn
        )

    def y_copy(self, zo, side):
        n = self.split(side)[0]
        return send(
            self.at(self.A, zo, 2, 0, n), self.line(self.Y, zo, n), self.sem(8, zo), self.sem(9, zo), self.net.yn
        )

    def z_copy(self, zo, direction):
        return send(
            self.at(self.A, zo, 0), self.at(self.Z, zo, direction),
            self.sem(10, zo), self.sem(11, zo, direction), self.toward(direction),
        )

    def late_copies(self, zo, direction):
        first = sum(n for _, n in CHUNKS[: self.index])
        for k in range(3):
            yield send(
                self.at(self.A, zo, k + 1, self.early, self.late),
                self.ZX.at[zo, direction, k, pl.ds(first, self.late)],
                self.sem(12, zo, k), self.sem(13, zo, direction, k), self.toward(direction),
            )

    def place(self, zo, kind):
        return kind // 2, (zo * 2 + self.kinds[kind][1]) * 24

    def begin(self, zo, side, these=(3, 1, 2, 0)):
        for kind in these:
            row, first = self.place(zo, kind)

            def one(i):
                self.S[zo, kind, i] = self.held_other[row][self.order_ref[first + i]]

            rounds(self.base, self.size, one)
            self.c_copy(zo, kind).start()

    def begin_far(self, zo, side):
        self.begin(zo, side, (3, 2))

    def begin_near(self, zo, side):
        self.begin(zo, side, (1, 0))

    def add(self, zo, kind, other, lo, n):
        def one(i):
            self.A[zo, kind, i] = self.A[zo, kind, i] + other(i)

        rounds(self.base + lo, n, one)

    def late_add(self, zo, direction):
        first = sum(n for _, n in CHUNKS[: self.index]) - self.base - self.early
        for k, copy in enumerate(self.late_copies(zo, direction)):
            copy.wait_recv()
            self.add(
                zo, k + 1, lambda i: self.ZX[zo, direction, k, i + first], self.early, self.late
            )

    def diagonal(self, zo, side):
        self.xd_copy(zo, side).start()
        self.yd_copy(zo, side).start()

    def one(self, zo, side):
        for kind in (3, 1, 2, 0):
            self.c_copy(zo, kind).wait_recv()
            row, first = self.place(zo, kind)

            def both(i):
                self.A[zo, kind, i] = self.held[row][self.order_ref[first + i]] + self.R[zo, kind, i]

            rounds(self.base, self.size, both)
            if kind == 3 and not is_own(side):
                self.diagonal(zo, side)
        if is_own(side) or side == -1:
            pl.when(self.net.has_dn)(lambda: self.late_add(zo, 0))
        if is_own(side) or side == 1:
            pl.when(self.net.has_up)(lambda: self.late_add(zo, 1))
        if is_own(side):
            self.diagonal(zo, side)
        else:
            for copy in self.late_copies(zo, 0 if side == -1 else 1):
                copy.start()

    def two(self, zo, side):
        count, lo = self.split(side)
        self.yd_copy(zo, side).wait_recv()
        self.add(zo, 1, lambda i: self.YD[zo, i - lo], lo, count - lo)
        self.x_copy(zo, side).start()
        self.xd_copy(zo, side).wait_recv()
        self.add(zo, 2, lambda i: self.XD[zo, i], 0, lo)
        self.y_copy(zo, side).start()

    def three(self, zo, side):
        self.x_copy(zo, side).wait_recv()
        self.y_copy(zo, side).wait_recv()
        self.add(
            zo, 0, lambda i: (self.X[zo, i].astype(f32) + self.Y[zo, i].astype(f32)).astype(bf16), 0, self.split(side)[0]
        )
        if is_own(side):
            return

        def more(direction):
            self.z_copy(zo, direction).wait_recv()
            self.add(zo, 0, lambda i: self.Z[zo, direction, i], 0, self.size)

        if side == -1:
            pl.when(self.net.has_dn)(lambda: more(0))
            self.z_copy(zo, 0).start()
        else:
            pl.when(self.net.has_up)(lambda: more(1))
            self.z_copy(zo, 1).start()

    def total(self, zo):
        pl.when(self.net.has_dn)(lambda: self.z_copy(zo, 0).wait_recv())
        pl.when(self.net.has_up)(lambda: self.z_copy(zo, 1).wait_recv())

    def sent(self, zo, side):
        for kind in range(4):
            self.c_copy(zo, kind).wait_send()
        self.xd_copy(zo, side).wait_send()
        self.yd_copy(zo, side).wait_send()
        self.x_copy(zo, side).wait_send()
        self.y_copy(zo, side).wait_send()
        if is_own(side):
            return
        self.z_copy(zo, 0).wait_send()
        for copy in self.late_copies(zo, 0):
            copy.wait_send()


def rounds(first, count, fn):
    wide = next(n for n in (6, 5, 4, 3, 2, 1) if count % n == 0)

    def body(i, _):
        for j in range(wide):
            fn(first + wide * i + j)
        return 0

    lax.fori_loop(0, count // wide, body, 0)


def scatter_kernel(
    nz, order_ref, tq_ref, to_ref, tu_ref, td_ref, other_ref, local_ref, shared_ref,
    tile_o, dx_o, local_o, shared_o,
    TAN, TAF, TBN, TBF, S, A, R, XD, YD, X, Y, Z, ZX, la, lb, sa, sb,
    tsem, dxs, vs, vr, *sems,
):
    net = Net(nz)
    z, x, y, c, m, d = net.z, net.x, net.y, net.c, net.m, net.d
    my = (1 - y) * 2 + c
    far = (lax.rem(z + 2, nz) * 2 + x, m)
    near = ((z + 1 - 2 * (z % 2)) * 2 + x, m)

    def loads(held, group):
        first = 0
        for i, src in enumerate((tq_ref, to_ref, tu_ref, td_ref)):
            count = src.shape[1]
            yield pltpu.make_async_copy(
                src.at[group], held.at[pl.ds(first, count)], tsem.at[group, i]
            )
            first += count

    groups = (
        (TBF, (1 - y) * 2 + 1 - c), (TBN, y * 2 + 1 - c), (TAF, my), (TAN, m),
    )
    for held, group in groups:
        for copy in loads(held, group):
            copy.start()

    def loaded(i):
        for copy in loads(*groups[i]):
            copy.wait()

    net.greet()
    kinds = ((m, x), (m, 1 - x), (my, x), (my, 1 - x))
    bufs = (S, A, R, XD, YD, X, Y, Z, ZX)
    parts = [ScatterPart(net, kinds, i, order_ref, (TAN, TAF), (TBN, TBF), bufs, sems) for i in range(len(CHUNKS))]

    def step_of(distance, name):
        def run(zo, side):
            for part in parts:
                getattr(part, name)(zo, side)

        each(net, distance, run)

    dx_copy = send(other_ref, dx_o, dxs.at[0], dxs.at[1], net.cn)
    peers = (net.cn, net.xn, net.yn, near, far)

    def v_copies(k):
        return (
            send(la.at[k], lb.at[k], vs.at[k, 0], vr.at[k, 0], peers[k]),
            send(sa.at[k], sb.at[k], vs.at[k, 1], vr.at[k, 1], peers[k]),
        )

    def v_start(k):
        for copy in v_copies(k):
            copy.start()

    def v_finish(k):
        for copy in v_copies(k):
            copy.wait_recv()
        la[k + 1] = la[k] + lb[k]
        sa[k + 1] = sa[k] + sb[k]

    la[0] = local_ref[...]
    sa[0] = shared_ref[...]
    net.await_all()
    loaded(0)
    step_of(nz - 1, "begin_far")
    loaded(1)
    step_of(nz - 1, "begin_near")
    loaded(2)
    loaded(3)
    v_start(0)
    for turn_no in range(nz + 2):
        if turn_no + 1 < nz:
            step_of(nz - 2 - turn_no, "begin")
        if turn_no < nz:
            step_of(nz - 1 - turn_no, "one")
        if turn_no == 0:
            dx_copy.start()
        if 0 <= turn_no - 1 < nz:
            step_of(nz - turn_no, "two")
        if 0 <= turn_no - 2:
            step_of(nz + 1 - turn_no, "three")
        if turn_no < 5:
            v_finish(turn_no)
            if turn_no < 4:
                v_start(turn_no + 1)
    local_o[...] = la[5]
    shared_o[...] = sa[5]
    dx_copy.wait_recv()

    for part in parts:
        part.total(z)

    def finish(i):
        total = A[z, 0, i].astype(f32)
        total = total + jnp.where(net.has_dn, Z[z, 0, i].astype(f32), 0.0)
        tile_o[i] = total + jnp.where(net.has_up, Z[z, 1, i].astype(f32), 0.0)

    rounds(0, 24, finish)
    for step in range(nz):
        step_of(step, "sent")
    dx_copy.wait_send()
    for k in range(5):
        for copy in v_copies(k):
            copy.wait_send()


def scatter_grads(nz, order, parts, other, local, shared):
    dma = pltpu.SemaphoreType.DMA
    vm = pl.BlockSpec(memory_space=pltpu.VMEM)
    block = lambda *lead: pltpu.VMEM((*lead, 72, 128), bf16)
    anywhere = pl.BlockSpec(memory_space=pl.ANY)
    return pl.pallas_call(
        functools.partial(scatter_kernel, nz),
        out_shape=[
            jax.ShapeDtypeStruct((24, 72, 128), f32),
            jax.ShapeDtypeStruct(other.shape, bf16),
            jax.ShapeDtypeStruct(local.shape, f32),
            jax.ShapeDtypeStruct(shared.shape, f32),
        ],
        in_specs=[pl.BlockSpec(memory_space=pltpu.SMEM)] + [anywhere] * 5 + [vm] * 2,
        out_specs=[vm, anywhere, vm, vm],
        scratch_shapes=[
            block(48 * nz), block(48 * nz), block(48 * nz), block(48 * nz), block(nz, 4, 24), block(nz, 4, 24), block(nz, 4, 24),
            block(nz, 24), block(nz, 24), block(nz, 24), block(nz, 24), block(nz, 2, 24),
            block(nz, 2, 3, sum(late for _, late in CHUNKS)),
            pltpu.VMEM((6, *local.shape), f32), pltpu.VMEM((5, *local.shape), f32),
            pltpu.VMEM((6, *shared.shape), f32), pltpu.VMEM((5, *shared.shape), f32),
            dma((4, 4)), dma((2,)), dma((5, 2)), dma((5, 2)),
        ]
        + [
            dma((len(CHUNKS), nz, *tail))
            for tail in ((4,), (4,), *([()] * 9), (2,), (3,), (2, 3))
        ],
        compiler_params=pltpu.CompilerParams(
            collective_id=1, has_side_effects=True, vmem_limit_bytes=60 << 20
        ),
        name="scatter_grads",
    )(order, *parts, other, local, shared)


STEP = 5
BETA_ONE = 0.5
BETA_TWO = 0.5
ADAM_EPS = 1e-08
RATE_TILES = 0.04
RATE_VECTORS = 0.2
DECAY = 0.01


def adam(grad, first, second):
    first_new = BETA_ONE * first + (1.0 - BETA_ONE) * grad
    second_new = BETA_TWO * second + (1.0 - BETA_TWO) * grad * grad
    step_dir = (
        first_new
        / (1.0 - BETA_ONE**STEP)
        / (jnp.sqrt(second_new / (1.0 - BETA_TWO**STEP)) + ADAM_EPS)
    )
    return (first_new, second_new, step_dir)


def update_kernel(
    order_ref, own_ref, came_ref, grad_ref, first_ref, second_ref, left_ref, right_ref, master_ref,
    lg_ref, lv_ref, lf_ref, ls_ref, sg_ref, sv_ref, sf_ref, ss_ref,
    o_own, o_grad, o_first, o_second, o_weight, o_lg, o_lf, o_ls, o_lv, o_sg, o_sf, o_ss, o_sv,
):
    @pl.when(pl.program_id(0) == 0)
    def _():
        local = lg_ref[lax.axis_index("mp")]
        first, second, step_dir = adam(local, lf_ref[...], ls_ref[...])
        o_lg[...] = local
        o_lf[...] = first
        o_ls[...] = second
        o_lv[...] = lv_ref[...] - RATE_VECTORS * step_dir
        shared = sg_ref[...]
        first, second, step_dir = adam(shared, sf_ref[...], ss_ref[...])
        o_sg[...] = shared
        o_sf[...] = first
        o_ss[...] = second
        o_sv[...] = sv_ref[...] - RATE_VECTORS * step_dir

    o_own[...] = own_ref[...] + came_ref[...].astype(f32)
    every = range(grad_ref.shape[0])
    edge = left_ref.shape[-1]
    place_at = (lax.axis_index("dp") * pl.num_programs(0) + pl.program_id(0)) * grad_ref.shape[0]
    grads = []
    for i in every:
        j = part_of(lax.axis_index("mp"), order_ref[place_at + i])
        wire = grad_ref[i]
        tile = jnp.concatenate([wire, rest_of(wire, free_of(j))], 0)
        grads.append(turned(tile, j, -1)[:, :edge])
    left = [left_ref[i].astype(bf16) for i in every]
    right = [right_ref[i].astype(bf16) for i in every]
    for i in every:
        o_grad[i] = grads[i]
    half = [nn(grads[i].astype(bf16), right[i]).astype(bf16) for i in every]
    rotated = [tn(left[i], half[i]) for i in every]
    moved = [adam(rotated[i], first_ref[i], second_ref[i]) for i in every]
    for i in every:
        o_first[i] = moved[i][0]
        o_second[i] = moved[i][1]
    half = [nn(left[i], moved[i][2].astype(bf16)).astype(bf16) for i in every]
    for i in every:
        turn_back = nt(half[i], right[i])
        master = master_ref[i]
        o_weight[i] = master - RATE_TILES * (turn_back + DECAY * master)


def update(order, own, came, grad, first, second, left, right, master, local, shared):
    count, edge = first.shape[:2]
    part = 12 if count % 12 == 0 else count
    tile = lambda rows, lanes: pl.BlockSpec((part, rows, lanes), lambda i: (i, 0, 0))
    whole = lambda v: pl.BlockSpec(v.shape, lambda i: (0,) * v.ndim)
    band = pl.BlockSpec((own.shape[0] * part // count, own.shape[1]), lambda i: (i, 0))
    out = lambda v: jax.ShapeDtypeStruct(v.shape, f32)
    return pl.pallas_call(
        update_kernel,
        grid=(count // part,),
        in_specs=[pl.BlockSpec(memory_space=pltpu.SMEM), band, band, tile(*grad.shape[1:])]
        + [tile(edge, edge)] * 5 + [whole(v) for v in (*local, *shared)],
        out_specs=[band] + [tile(edge, edge)] * 4 + [whole(local[1])] * 4 + [whole(shared[1])] * 4,
        out_shape=[out(own)] + [out(first)] * 4 + [out(local[1])] * 4 + [out(shared[1])] * 4,
        compiler_params=pltpu.CompilerParams(vmem_limit_bytes=58 << 20),
        name="update",
    )(order, own, came, grad, first, second, left, right, master, *local, *shared)


def from_tiles(tile_set, row_count, col_count):
    edge = tile_set.shape[-1]
    return (
        tile_set.reshape(row_count // edge, col_count // edge, edge, edge)
        .transpose(0, 2, 1, 3)
        .reshape(row_count, col_count)
    )


def plain_weights(tile_order, master, local):
    tiles = lax.all_gather(master.astype(bf16), "dp", axis=0, tiled=True)
    tiles = lax.all_gather(tiles, "mp", axis=0)
    count = tile_order.shape[0]
    inverse = jnp.zeros((count,), jnp.int32).at[tile_order].set(jnp.arange(count, dtype=jnp.int32))
    natural = tiles[:, inverse]
    dense = []
    for rows, cols, where in GRIDS:
        pieces = []
        for r in range(rows):
            pick = [where(r, j) for j in range(cols)]
            groups = jnp.asarray([p for p, _ in pick], jnp.int32)
            numbers = jnp.asarray([n for _, n in pick], jnp.int32)
            pieces.append(natural[groups, numbers].transpose(1, 0, 2).reshape(96, cols * 96))
        dense.append(jnp.concatenate(pieces, 0))
    return (*dense, lax.all_gather(local, "mp", axis=0))


def plain_scatter(order, parts, other, local, shared):
    tiles = jnp.concatenate(parts, 1)[:, order]
    mine = lax.psum_scatter(tiles, "mp", scatter_dimension=0, tiled=False).astype(f32)
    owned = lax.psum_scatter(mine, "dp", scatter_dimension=0, tiled=True)
    count = lax.axis_size("mp")
    swapped = lax.ppermute(other, "mp", [(i, i ^ 1) for i in range(count)])
    local_sum, shared_sum = lax.psum((local, shared), ("dp", "mp"))
    return owned, swapped, local_sum, shared_sum


def shards(
    tokens,
    cotangent,
    lengths,
    tile_order,
    master,
    first_moment,
    second_moment,
    basis_left,
    basis_right,
    local_vec,
    local_first,
    local_second,
    shared_vec,
    shared_first,
    shared_second,
):
    group_count = lax.axis_size("mp")
    group_index = lax.axis_index("mp")
    owners = lax.axis_size("dp")
    row_total, width = tokens.shape
    rows = row_total // group_count
    per_owner = master.shape[1]
    nz = owners // 2
    routed = per_owner == 24 and nz == 4 and group_count == 4

    if routed:
        w_qkv, w_out, w_up, w_down, vectors = gather_weights(
            nz, tile_order, master[0], local_vec
        )
    else:
        w_qkv, w_out, w_up, w_down, vectors = plain_weights(tile_order, master[0], local_vec)
    output, tq, to, tu, td, own, other, local_terms, shared_terms = layer(
        tokens, cotangent, lengths, vectors, shared_vec, w_qkv, w_out, w_up, w_down, rows
    )
    parts = [t.reshape(group_count, -1, 72, 128) for t in (tq, to, tu, td)]
    if routed:
        owned, came, local_sum, shared_grad = scatter_grads(
            nz, tile_order, parts, other, local_terms, shared_terms
        )
    else:
        owned, came, local_sum, shared_grad = plain_scatter(
            tile_order, parts, other, local_terms, shared_terms
        )
    input_grad, *tiles = update(
        tile_order, own, came, owned, first_moment[0], second_moment[0], basis_left[0], basis_right[0], master[0],
        (local_sum, local_vec, local_first, local_second),
        (shared_grad, shared_vec, shared_first, shared_second),
    )
    return (output, input_grad, *(t[None] for t in tiles[:4]), *tiles[4:])


def solution(mesh):
    placed = (
        P("dp", None),
        P("dp", None),
        P("dp"),
        P(),
        P("mp", "dp", None, None),
        P("mp", "dp", None, None),
        P("mp", "dp", None, None),
        P("mp", "dp", None, None),
        P("mp", "dp", None, None),
        P("mp", None),
        P("mp", None),
        P("mp", None),
        P(),
        P(),
        P(),
    )
    return jax.shard_map(
        shards,
        mesh=mesh,
        in_specs=placed,
        out_specs=(
            P(("dp", "mp"), None),
            P(("dp", "mp"), None),
            P("mp", "dp", None, None),
            P("mp", "dp", None, None),
            P("mp", "dp", None, None),
            P("mp", "dp", None, None),
            P("mp", None),
            P("mp", None),
            P("mp", None),
            P("mp", None),
            P(),
            P(),
            P(),
            P(),
        ),
        check_vma=False,
    )
```
